256 devices in a mesh: section: 2 (over x_lo), lat: 4 (over x_hi, core), lon: 32 (over y, z).
Axes of the slice: x: 4 (x_hi: 2, x_lo: 2; x = x_hi * 2 + x_lo), y: 4, z: 8, core: 2. Of those that a mesh axis runs over, the one named last changes fastest.
Arguments:
- fields: bfloat16 [2, 4, 24, 384, 384], P(None, None, 'lat', 'lon'), may hold values from -6 to 6
- surface_class: int32 [4, 24, 384], replicated, may hold values from 0 to 2
- norm_gains: bfloat16 [2, 2, 384], P('section'), may hold values from 0.25 to 1.75
- joint_proj: bfloat16 [2, 384, 1152], P('section'), may hold values from -0.3125 to 0.3125
- out_proj: bfloat16 [2, 384, 384], P('section'), may hold values from -0.3125 to 0.3125
- expand_proj: bfloat16 [2, 384, 1536], P('section'), may hold values from -0.3125 to 0.3125
- reduce_proj: bfloat16 [2, 1536, 384], P('section'), may hold values from -0.15625 to 0.15625
- earth_bias: bfloat16 [2, 8, 12, 3312], P('section'), may hold values from -4 to 300
Outputs:
- section_fields: bfloat16 [2, 2, 4, 24, 384, 384], P('section', None, None, 'lat', 'lon')
The draws below stay inside these ranges and needn't reach their ends.
Inputs may be any that keep to these rules, and one draw needn't show every extreme that they name: `surface_class`: tokens attend only to tokens of equal class inside a window.
All inputs are finite; a program needn't handle non-finite values.
Results may differ from the reference program's by a relative error of at most 0.013.
Values may be sent and summed in bfloat16 or wider, within the bound.
A program may use at most 64 MiB of HBM per device.

```python
import jax
import jax.numpy as jnp
import numpy as np
from jax import lax

WIDTH = 384
HEADS = 12
FF = 1536
WIN_P = 2
WIN_H = 6
WIN_W = 12
BIAS_LEN = 3312
LEVELS = 4
MICRO = 2
LAT = 24
LON = 384
TYPES = 8


def draw_earth_bias(key, part):
    key = jax.random.fold_in(key, 7)
    key_list = jax.random.split(key, 1)
    shape_full = (2, TYPES, HEADS, BIAS_LEN)
    baseline = jnp.clip(jax.random.normal(key_list[0], shape_full, jnp.float32), -4.0, 4.0)
    return baseline.astype(jnp.bfloat16)


def place_ends(array, own_key, smallest, top_value):
    longest = array.shape.index(max(array.shape))
    spots = []
    for shift in (0, 1):
        where = [jax.random.randint(jax.random.fold_in(own_key, axis), (), 0, length) for axis, length in enumerate(array.shape)]
        where[longest] = (where[longest] + shift) % array.shape[longest]
        spots.append(tuple(where))
    return array.at[spots[0]].set(smallest).at[spots[1]].set(top_value)


def block_levels(own_key, extent, shards, least, high):
    def one(position, shards_of):
        steps = jax.random.uniform(jax.random.fold_in(jax.random.fold_in(own_key, 6), position), (shards_of,), jnp.float32, least / len(shards), high / len(shards))
        return jnp.repeat(jnp.exp(steps), extent[position] // shards_of).reshape((-1,) + (1,) * (len(extent) - position - 1))

    level = one(*shards[0])
    for cut in shards[1:]:
        level = level * one(*cut)
    return level


def scatter_about(own_key, dims, scale, reach, cuts=(), held_as=jnp.bfloat16):
    loudness = block_levels(own_key, dims, cuts, -0.22, 0.18) if cuts else 1.0
    drawn = jax.random.normal(own_key, dims, jnp.float32) * scale * loudness
    return jnp.minimum(jnp.maximum(drawn, -reach), reach).astype(held_as)


def setup_inputs(seed: int = 0) -> dict:
    streams_of = jax.random.split(jax.random.key(seed), 9)
    fields = scatter_about(streams_of[0], (MICRO, LEVELS, LAT, LON, WIDTH), 1.0, 6.0, ((2, 4), (3, 32)))
    surface_class = place_ends(jax.random.randint(streams_of[1], (LEVELS, LAT, LON), 0, 3), jax.random.fold_in(streams_of[1], 1), 0, 2).astype(jnp.int32)
    norm_gains = jnp.clip(1.0 + 0.15 * jax.random.normal(streams_of[2], (2, 2, WIDTH), jnp.float32), 0.25, 1.75).astype(jnp.bfloat16)
    joint_proj = scatter_about(streams_of[3], (2, WIDTH, 3 * WIDTH), WIDTH ** -0.5, 0.3125, ((0, 2),))
    out_proj = scatter_about(streams_of[4], (2, WIDTH, WIDTH), WIDTH ** -0.5, 0.3125, ((0, 2),))
    expand_proj = scatter_about(streams_of[5], (2, WIDTH, FF), WIDTH ** -0.5, 0.3125, ((0, 2),))
    reduce_proj = scatter_about(streams_of[6], (2, FF, WIDTH), FF ** -0.5, 0.15625, ((0, 2),))
    earth_bias = draw_earth_bias(jax.random.fold_in(streams_of[8], 71), 0)
    return dict(fields=fields, surface_class=surface_class, norm_gains=norm_gains, joint_proj=joint_proj, out_proj=out_proj, expand_proj=expand_proj, reduce_proj=reduce_proj, earth_bias=earth_bias)


def relative_index():
    level_grid, row_grid, col_grid = np.meshgrid(np.arange(WIN_P), np.arange(WIN_H), np.arange(WIN_W), indexing='ij')
    level_flat = level_grid.reshape(-1)
    row_flat = row_grid.reshape(-1)
    col_flat = col_grid.reshape(-1)
    level_part = level_flat[:, None] + level_flat[None, :] * WIN_P
    row_part = row_flat[:, None] + row_flat[None, :] * WIN_H
    col_part = col_flat[:, None] - col_flat[None, :] + WIN_W - 1
    joined = level_part * (WIN_H * WIN_H * (2 * WIN_W - 1)) + row_part * (2 * WIN_W - 1) + col_part
    return joined.astype(np.int32)

def layer_norm(values, gain):
    average = lax.optimization_barrier(jnp.mean(values, axis=-1, keepdims=True))
    centred = values - average
    spread = lax.optimization_barrier(jnp.mean(centred * centred, axis=-1, keepdims=True))
    return centred * lax.rsqrt(spread + 1e-05) * gain.astype(jnp.float32)

def to_windows(token_grid):
    level_count, row_count, col_count = token_grid.shape[:3]
    trailing = token_grid.shape[3:]
    shaped = token_grid.reshape((level_count // WIN_P, WIN_P, row_count // WIN_H, WIN_H, col_count // WIN_W, WIN_W) + trailing)
    order = (0, 2, 4, 1, 3, 5) + tuple(range(6, 6 + len(trailing)))
    return shaped.transpose(order).reshape((-1, WIN_P * WIN_H * WIN_W) + trailing)

def from_windows(windowed, level_count, row_count, col_count):
    trailing = windowed.shape[2:]
    shaped = windowed.reshape((level_count // WIN_P, row_count // WIN_H, col_count // WIN_W, WIN_P, WIN_H, WIN_W) + trailing)
    order = (0, 3, 1, 4, 2, 5) + tuple(range(6, 6 + len(trailing)))
    return shaped.transpose(order).reshape((level_count, row_count, col_count) + trailing)

def window_core(window_tokens, region_win, bias_win, params):
    gain_pair, joint_weight, output_weight, expand_weight, reduce_weight = params
    window_count, window_size, model_width = window_tokens.shape
    head_count = bias_win.shape[1]
    head_size = model_width // head_count
    flat_rows = window_tokens.reshape((-1, model_width)).astype(jnp.float32)
    normed = layer_norm(flat_rows, gain_pair[0]).astype(jnp.bfloat16)
    projected = jnp.dot(normed, joint_weight, preferred_element_type=jnp.float32).astype(jnp.bfloat16)
    projected = projected.reshape((window_count, window_size, 3, head_count, head_size))
    queries = projected[:, :, 0].astype(jnp.float32)
    key_rows = projected[:, :, 1].astype(jnp.float32)
    value_rows = projected[:, :, 2].astype(jnp.float32)
    scores = jnp.einsum('wqhd,wkhd->whqk', queries, key_rows) * head_size ** (-0.5) + bias_win
    same_region = region_win[:, :, None] == region_win[:, None, :]
    scores = jnp.where(same_region[:, None], scores, -1e+30)
    row_max = lax.optimization_barrier(jnp.max(scores, axis=-1, keepdims=True))
    exponent = jnp.exp(scores - row_max)
    attn_weights = (exponent / lax.optimization_barrier(jnp.sum(exponent, axis=-1, keepdims=True))).astype(jnp.bfloat16)
    mixed_heads = jnp.einsum('whqk,wkhd->wqhd', attn_weights.astype(jnp.float32), value_rows)
    mixed_heads = mixed_heads.astype(jnp.bfloat16).reshape((-1, model_width))
    hidden = flat_rows + jnp.dot(mixed_heads, output_weight, preferred_element_type=jnp.float32)
    normed_again = layer_norm(hidden, gain_pair[1]).astype(jnp.bfloat16)
    activated = jax.nn.gelu(jnp.dot(normed_again, expand_weight, preferred_element_type=jnp.float32), approximate=False).astype(jnp.bfloat16)
    result = (hidden + jnp.dot(activated, reduce_weight, preferred_element_type=jnp.float32)).astype(jnp.bfloat16)
    return result.reshape((window_count, window_size, model_width))

def grid_block(token_grid, region_grid, kind_grid, params, bias_grid):
    level_count, row_count, col_count, model_width = token_grid.shape
    group_width = col_count // WIN_W
    window_size = WIN_P * WIN_H * WIN_W
    window_tokens = to_windows(token_grid).reshape((-1, group_width, window_size, model_width))
    region_win = to_windows(region_grid).reshape((-1, group_width, window_size))
    kind_rows = kind_grid.reshape((-1, group_width))

    def one_group(pieces):
        tokens_part, regions_part, kinds_part = pieces
        return window_core(tokens_part, regions_part, jnp.take(bias_grid, kinds_part, axis=0), params)
    processed = lax.map(one_group, (window_tokens, region_win, kind_rows))
    return from_windows(processed.reshape((-1, window_size, model_width)), level_count, row_count, col_count)

def reference(fields, surface_class, norm_gains, joint_proj, out_proj, expand_proj, reduce_proj, earth_bias):
    relative = jnp.asarray(relative_index())
    shifts = (-(WIN_P // 2), -(WIN_H // 2), -(WIN_W // 2))
    backs = (WIN_P // 2, WIN_H // 2, WIN_W // 2)
    level_flag = (jnp.arange(LEVELS) >= LEVELS - WIN_P // 2).astype(jnp.int32)
    row_flag = (jnp.arange(LAT) >= LAT - WIN_H // 2).astype(jnp.int32)
    first_regions = jnp.roll(surface_class, shifts, axis=(0, 1, 2)) * 4 + level_flag[:, None, None] * 2 + row_flag[None, :, None]
    second_regions = surface_class * 4
    level_wins = jnp.arange(LEVELS // WIN_P, dtype=jnp.int32)
    row_wins = jnp.arange(LAT // WIN_H, dtype=jnp.int32)
    kind_grid = level_wins[:, None, None] * (LAT // WIN_H) + row_wins[None, :, None] + jnp.zeros((1, 1, LON // WIN_W), jnp.int32)
    section_params = [tuple((member[section_slot] for member in (norm_gains, joint_proj, out_proj, expand_proj, reduce_proj))) for section_slot in range(2)]
    bias_grids = [earth_bias[section_slot].astype(jnp.float32)[:, :, relative] for section_slot in range(2)]
    firsts = []
    seconds = []
    for micro_index in range(MICRO):
        rolled = jnp.roll(fields[micro_index], shifts, axis=(0, 1, 2))
        processed = grid_block(rolled, first_regions, kind_grid, section_params[0], bias_grids[0])
        first_out = jnp.roll(processed, backs, axis=(0, 1, 2))
        second_out = grid_block(first_out, second_regions, kind_grid, section_params[1], bias_grids[1])
        firsts.append(first_out)
        seconds.append(second_out)
    return jnp.stack([jnp.stack(firsts), jnp.stack(seconds)])
```

```python
import functools

import jax
import jax.numpy as jnp
import numpy as np
from jax import lax
from jax.experimental import pallas as pl
from jax.experimental.pallas import tpu as pltpu
from jax.sharding import PartitionSpec as P

WIN_P = 2
WIN_H = 6
WIN_W = 12
TOK = WIN_P * WIN_H * WIN_W
LEVELS = 4
MICRO = 2
WIDTH = 384
HEADS = 12
FF = 1536
QROWS = 80
GRID_ROWS = LEVELS * WIN_H * 16
GROUP = 640
GUSED = 576
KDIM = 288
LOG2E = 1.4426950408889634
MESH = pl.DeviceIdType.MESH


def permutations():
    into = np.zeros((2, 2 * TOK, 4 * QROWS), np.float32)
    gather = np.zeros((4 * QROWS, GRID_ROWS), np.float32)
    plain = np.zeros((GRID_ROWS, 2 * TOK), np.float32)
    for level in range(LEVELS):
        for row in range(WIN_H):
            for col in range(WIN_W):
                token = (level // 2) * TOK + col * 12 + (level % 2) * 6 + row
                inner = (row % 3) * 6 + col % 6
                shifted_slot = (row >= 3) + 2 * (col >= 6)
                into[0, token, shifted_slot * QROWS + level * 18 + inner] = 1
                slot = (row < 3) + 2 * (col < 6)
                source = slot * QROWS + ((level + 3) % 4) * 18 + inner
                into[1, token, source] = 1
                place = (level * 6 + row) * 16 + col
                gather[source, place] = 1
                plain[place, token] = 1
    scatter = into[0].T.copy()
    back = gather.T.copy()
    return tuple(jnp.asarray(m, jnp.bfloat16) for m in (into, gather, scatter, back, plain))


def dot(a, b):
    return jnp.dot(a, b, preferred_element_type=jnp.float32)


def dot_nt(a, b):
    return lax.dot_general(a, b, (((1,), (1,)), ((), ())), preferred_element_type=jnp.float32)


def layer_norm(values, gain):
    average = jnp.mean(values, axis=-1, keepdims=True)
    centred = values - average
    spread = jnp.mean(centred * centred, axis=-1, keepdims=True)
    return centred * lax.rsqrt(spread + 1e-05) * gain


def gelu(x):
    return x * (0.5 + 0.5 * lax.erf(x * 0.7071067811865476))


def token_parts(token):
    col = (token * 5462) >> 16
    rest = token - col * 12
    level = (rest >= 6).astype(jnp.int32)
    return col, level, rest - level * 6


def lane_tokens():
    lane = lax.broadcasted_iota(jnp.int32, (1, 256), 1)
    return jnp.where(lane < 128, lane, 128 + (lane & 15))


def prepare_bias(first, lat, lon, lat_count, lon_count, class_ref, table_ref, rows_ref, bias_ref):
    rows_ref[...] = jnp.zeros_like(rows_ref)
    for i in range(2):
        for j in range(12):
            pb, rb = j // 6, j % 6
            for pa in range(2):
                begin = pb * 1656 + pa * 828 + rb * 138
                rows_ref[i, j, 0:12, pa * 144 : pa * 144 + 138] = table_ref[i, :, begin : begin + 138]
    to_row = lax.broadcasted_iota(jnp.int32, (192, 192), 0)
    to_col = lax.broadcasted_iota(jnp.int32, (192, 192), 1)
    swap = (((to_row & 15) << 4) + (to_row >> 4) == to_col).astype(jnp.float32).astype(jnp.bfloat16)
    by_head = [
        dot(swap, rows_ref[i].reshape(192, KDIM)).astype(jnp.bfloat16) for i in range(2)
    ]
    by_head = jnp.concatenate(by_head, axis=0)
    col_a, level_a, row_a = token_parts(lane_tokens())
    base = level_a * 144 + row_a * 23 + col_a + 11
    depth = lax.broadcasted_iota(jnp.int32, (KDIM, 256), 0)
    segment = lax.broadcasted_iota(jnp.int32, (12, 128), 1) >> 4
    for cb in range(12):
        pick = (depth == base - cb).astype(jnp.float32).astype(jnp.bfloat16)
        spread = dot(by_head, pick) * LOG2E
        for i in range(2):
            for g in range(3):
                tail = None
                for t in range(4):
                    start = i * 192 + (g * 4 + t) * 16
                    piece = spread[start : start + 12]
                    bias_ref[i, cb * 12 : cb * 12 + 12, g * GROUP + t * 128 : g * GROUP + t * 128 + 128] = piece[:, 0:128]
                    last = piece[:, 128:256]
                    tail = last if tail is None else jnp.where(segment == t, last, tail)
                bias_ref[i, cb * 12 : cb * 12 + 12, g * GROUP + 512 : g * GROUP + 640] = tail
    rows_all = 6 * lat_count
    cols_all = 12 * lon_count
    one = jnp.where(first, 1, 0)
    row_start = lat * 6 + 3 * one
    col_start = lon * 12 + 6 * one
    classes = class_ref[...].reshape(LEVELS * rows_all, cols_all).astype(jnp.float32).astype(jnp.bfloat16)
    col_b, level_b, row_b = token_parts(lax.broadcasted_iota(jnp.int32, (TOK, 1), 0))

    def wrap(v, extent):
        return jnp.where(v >= extent, v - extent, v)

    def onehot(a, b):
        return (a == b).astype(jnp.float32).astype(jnp.bfloat16)

    across = dot(
        classes,
        onehot(lax.broadcasted_iota(jnp.int32, (cols_all, 256), 0), wrap(col_start + col_a, cols_all)),
    )
    down = dot_nt(
        onehot(lax.broadcasted_iota(jnp.int32, (TOK, cols_all), 1), wrap(col_start + col_b, cols_all)),
        classes,
    )
    place_a = lax.broadcasted_iota(jnp.int32, across.shape, 0)
    place_b = lax.broadcasted_iota(jnp.int32, down.shape, 1)
    for i in range(2):

        def region(place, level, row, values, axis):
            at = ((2 * i + level + one) & 3) * rows_all + wrap(row_start + row, rows_all)
            value = jnp.sum(jnp.where(place == at, values, 0.0), axis=axis, keepdims=True)
            flags = 2 * (2 * i + level >= 3).astype(jnp.int32)
            flags = flags + (lat * 6 + row >= rows_all - 3).astype(jnp.int32)
            return 4.0 * value + (one * flags).astype(jnp.float32)

        region_a = region(place_a, level_a, row_a, across, 0)
        region_b = region(place_b, level_b, row_b, down, 1)
        same = region_b == region_a
        for g in range(3):
            for t in range(5):
                lanes = slice(g * GROUP + t * 128, g * GROUP + t * 128 + 128)
                part = same[:, 0:128] if t < 4 else same[:, 128:256]
                bias_ref[i, :, lanes] = jnp.where(part, bias_ref[i, :, lanes], -1e30)


def attention(query, key, value, bias_ref, i):
    head = lax.broadcasted_iota(jnp.int32, (1, 128), 1) >> 5
    keep = [(head == t).astype(jnp.float32).astype(jnp.bfloat16) for t in range(4)]
    ones = jnp.ones((16, TOK), jnp.bfloat16)
    mixed = []
    for g in range(3):
        lanes = slice(g * 128, g * 128 + 128)
        q, k, v = query[:, lanes], key[:, lanes], value[:, lanes]
        wide = jnp.concatenate([q[0:128] * m for m in keep] + [q[128:144] * m for m in keep], axis=0)
        scores = dot_nt(k, wide) + bias_ref[i, :, g * GROUP : g * GROUP + GUSED]
        top = jnp.max(scores, axis=0, keepdims=True)
        weights = jnp.exp2(scores - top).astype(jnp.bfloat16)
        v_turned = jnp.concatenate([jnp.transpose(v.astype(jnp.float32)).astype(jnp.bfloat16), ones], axis=0)
        out = dot(v_turned, weights)
        out = out[0:128] * (1.0 / out[128:129])
        main = jnp.concatenate(
            [out[t * 32 : t * 32 + 32, t * 128 : t * 128 + 128] for t in range(4)], axis=0
        )
        main = jnp.transpose(main).astype(jnp.bfloat16)
        tail = jnp.transpose(out[:, 512:576]).astype(jnp.bfloat16)
        tail = sum(tail[t * 16 : t * 16 + 16] * keep[t] for t in range(4))
        mixed.append(jnp.concatenate([main, tail], axis=0))
    return jnp.concatenate(mixed, axis=1)


def block(x, gains_ref, joint_ref, out_ref, expand_ref, reduce_ref, bias_ref):
    gains = gains_ref[...].astype(jnp.float32)
    normed = layer_norm(x, gains[0:1]).astype(jnp.bfloat16)
    projected = dot(normed, joint_ref[...])
    query = (projected[:, 0:WIDTH] * (LOG2E * 32**-0.5)).astype(jnp.bfloat16)
    key = projected[:, WIDTH : 2 * WIDTH].astype(jnp.bfloat16)
    value = projected[:, 2 * WIDTH :].astype(jnp.bfloat16)
    mixed = []
    for i in range(2):
        rows = slice(i * TOK, i * TOK + TOK)
        mixed.append(attention(query[rows], key[rows], value[rows], bias_ref, i))
    hidden = x + dot(jnp.concatenate(mixed, axis=0), out_ref[...])
    again = layer_norm(hidden, gains[1:2]).astype(jnp.bfloat16)
    total = hidden
    step = 512
    for start in range(0, FF, step):
        act = gelu(dot(again, expand_ref[:, start : start + step])).astype(jnp.bfloat16)
        total = total + dot(act, reduce_ref[start : start + step, :])
    return total.astype(jnp.bfloat16)


def kernel(
    lat_count,
    lon_count,
    fields_hbm,
    class_hbm,
    gains_hbm,
    joint_hbm,
    oproj_hbm,
    expand_hbm,
    reduce_hbm,
    table_hbm,
    into_hbm,
    gather_hbm,
    scatter_hbm,
    back_hbm,
    plain_hbm,
    result_ref,
    fields_ref,
    class_ref,
    gains_ref,
    joint_ref,
    oproj_ref,
    expand_ref,
    reduce_ref,
    table_ref,
    into_ref,
    gather_ref,
    scatter_ref,
    back_ref,
    plain_ref,
    grid_ref,
    rows_ref,
    bias_ref,
    halo_ref,
    take_ref,
    done_ref,
    home_ref,
    load_sem,
    halo_send,
    take_recv,
    home_send,
    home_recv,
    next_send,
):
    sec = lax.axis_index("section")
    lat = lax.axis_index("lat")
    lon = lax.axis_index("lon")
    first = sec == 0
    lat_up = lax.rem(lat + 1, lat_count)
    lat_down = lax.rem(lat + lat_count - 1, lat_count)
    lon_up = lax.rem(lon + 1, lon_count)
    lon_down = lax.rem(lon + lon_count - 1, lon_count)
    behind = [(lat, lon), (lat_down, lon), (lat, lon_down), (lat_down, lon_down)]
    ahead = [(lat, lon), (lat_up, lon), (lat, lon_up), (lat_up, lon_up)]

    barrier = pltpu.get_barrier_semaphore()

    @pl.when(first)
    def _():
        for where in behind[1:] + ahead[1:]:
            pl.semaphore_signal(barrier, inc=1, device_id=(0,) + where, device_id_type=MESH)

    @pl.when(jnp.logical_not(first))
    def _():
        for where in behind:
            pl.semaphore_signal(barrier, inc=1, device_id=(0,) + where, device_id_type=MESH)

    loads = []

    def load(src, dst):
        copy = pltpu.make_async_copy(src, dst, load_sem.at[len(loads)])
        copy.start()
        loads.append(copy)
        return copy

    load_fields = load(fields_hbm, fields_ref)
    load_gather = load(gather_hbm, gather_ref)
    prep = [load(table_hbm.at[0, i * lat_count + lat], table_ref.at[i]) for i in range(2)]
    prep.append(load(class_hbm, class_ref))
    rest = [
        load(into_hbm.at[sec], into_ref),
        load(gains_hbm.at[0], gains_ref),
        load(joint_hbm.at[0], joint_ref),
        load(oproj_hbm.at[0], oproj_ref),
        load(expand_hbm.at[0], expand_ref),
        load(reduce_hbm.at[0], reduce_ref),
        load(scatter_hbm, scatter_ref),
        load(back_hbm, back_ref),
        load(plain_hbm, plain_ref),
    ]

    def halo_copy(m, q):
        return pltpu.make_async_remote_copy(
            src_ref=halo_ref.at[m, q],
            dst_ref=take_ref.at[m, q],
            send_sem=halo_send.at[m, q],
            recv_sem=take_recv.at[m, q],
            device_id=(0,) + behind[q],
            device_id_type=MESH,
        )

    def home_copy(m, q):
        return pltpu.make_async_remote_copy(
            src_ref=done_ref.at[m, q],
            dst_ref=home_ref.at[m, q],
            send_sem=home_send.at[m, q],
            recv_sem=home_recv.at[m, q],
            device_id=(0,) + ahead[q],
            device_id_type=MESH,
        )

    def next_copy(m, q):
        return pltpu.make_async_remote_copy(
            src_ref=done_ref.at[m, q],
            dst_ref=take_ref.at[m, q],
            send_sem=next_send.at[m, q],
            recv_sem=take_recv.at[m, q],
            device_id=(1,) + ahead[q],
            device_id_type=MESH,
        )

    load_fields.wait()
    load_gather.wait()

    @pl.when(first)
    def _():
        grid_ref[...] = jnp.zeros_like(grid_ref)
        for m in range(MICRO):
            for p in range(LEVELS):
                for h in range(WIN_H):
                    grid_ref[m, p * 6 + h, 0:12, :] = fields_ref[m, p, h]
        for m in range(MICRO):
            sorted_rows = dot(gather_ref[...], grid_ref[m].reshape(GRID_ROWS, WIDTH)).astype(jnp.bfloat16)
            take_ref[m, 0] = sorted_rows[0:QROWS]
            for q in range(1, 4):
                halo_ref[m, q] = sorted_rows[q * QROWS : (q + 1) * QROWS]
            if m == 0:
                pl.semaphore_wait(barrier, 10)
            for q in (3, 2, 1):
                halo_copy(m, q).start()

    for copy in prep:
        copy.wait()
    prepare_bias(first, lat, lon, lat_count, lon_count, class_ref, table_ref, rows_ref, bias_ref)
    for copy in rest:
        copy.wait()

    def step(m, carry):
        @pl.when(first)
        def _():
            for q in range(1, 4):
                halo_copy(m, q).wait_recv()

        @pl.when(jnp.logical_not(first))
        def _():
            for q in range(4):
                next_copy(m, q).wait_recv()

        x = dot(into_ref[...], take_ref[m].reshape(4 * QROWS, WIDTH))
        y = block(x, gains_ref, joint_ref, oproj_ref, expand_ref, reduce_ref, bias_ref)

        @pl.when(first)
        def _():
            pieces = dot(scatter_ref[...], y).astype(jnp.bfloat16)
            done_ref[m] = pieces.reshape(4, QROWS, WIDTH)
            home_ref[m, 0] = pieces[0:QROWS]
            for q in (3, 2, 1, 0):
                next_copy(m, q).start()
            for q in (3, 2, 1):
                home_copy(m, q).start()

        @pl.when(jnp.logical_not(first))
        def _():
            write(m, dot(plain_ref[...], y).astype(jnp.bfloat16))

        return carry

    def write(m, rows):
        for p in range(LEVELS):
            for h in range(WIN_H):
                at = (p * 6 + h) * 16
                result_ref[m, p, h] = rows[at : at + 12]

    lax.fori_loop(0, MICRO, step, 0)

    @pl.when(first)
    def _():
        for m in range(MICRO):
            for q in range(1, 4):
                home_copy(m, q).wait_recv()
            write(m, dot(back_ref[...], home_ref[m].reshape(4 * QROWS, WIDTH)).astype(jnp.bfloat16))
        for m in range(MICRO):
            for q in range(1, 4):
                halo_copy(m, q).wait_send()
                home_copy(m, q).wait_send()
            for q in range(4):
                next_copy(m, q).wait_send()


def body(
    fields, surface_class, norm_gains, joint_proj, out_proj, expand_proj, reduce_proj, earth_bias
):
    lat_count = lax.axis_size("lat")
    lon_count = lax.axis_size("lon")
    matrices = permutations()
    operands = (
        fields, surface_class, norm_gains, joint_proj, out_proj, expand_proj, reduce_proj, earth_bias,
    ) + matrices
    bf16 = jnp.bfloat16
    scratch = [
        pltpu.VMEM(fields.shape, bf16),
        pltpu.VMEM(surface_class.shape, jnp.int32),
        pltpu.VMEM((2, WIDTH), bf16),
        pltpu.VMEM((WIDTH, 3 * WIDTH), bf16),
        pltpu.VMEM((WIDTH, WIDTH), bf16),
        pltpu.VMEM((WIDTH, FF), bf16),
        pltpu.VMEM((FF, WIDTH), bf16),
        pltpu.VMEM((2, HEADS, earth_bias.shape[-1]), bf16),
        pltpu.VMEM(matrices[0].shape[1:], bf16),
        pltpu.VMEM(matrices[1].shape, bf16),
        pltpu.VMEM(matrices[2].shape, bf16),
        pltpu.VMEM(matrices[3].shape, bf16),
        pltpu.VMEM(matrices[4].shape, bf16),
        pltpu.VMEM((MICRO, LEVELS * WIN_H, 16, WIDTH), bf16),
        pltpu.VMEM((2, 12, 16, KDIM), bf16),
        pltpu.VMEM((2, TOK, 3 * GROUP), jnp.float32),
        pltpu.VMEM((MICRO, 4, QROWS, WIDTH), bf16),
        pltpu.VMEM((MICRO, 4, QROWS, WIDTH), bf16),
        pltpu.VMEM((MICRO, 4, QROWS, WIDTH), bf16),
        pltpu.VMEM((MICRO, 4, QROWS, WIDTH), bf16),
        pltpu.SemaphoreType.DMA((14,)),
        pltpu.SemaphoreType.DMA((MICRO, 4)),
        pltpu.SemaphoreType.DMA((MICRO, 4)),
        pltpu.SemaphoreType.DMA((MICRO, 4)),
        pltpu.SemaphoreType.DMA((MICRO, 4)),
        pltpu.SemaphoreType.DMA((MICRO, 4)),
    ]
    result = pl.pallas_call(
        functools.partial(kernel, lat_count, lon_count),
        out_shape=jax.ShapeDtypeStruct(fields.shape, bf16),
        in_specs=[pl.BlockSpec(memory_space=pl.ANY)] * len(operands),
        out_specs=pl.BlockSpec(memory_space=pltpu.VMEM),
        scratch_shapes=scratch,
        compiler_params=pltpu.CompilerParams(
            collective_id=0, has_side_effects=True, vmem_limit_bytes=48 * 1024 * 1024
        ),
        name="two_blocks",
    )(*operands)
    return result[None]


def solution(mesh):
    return jax.shard_map(
        body,
        mesh=mesh,
        in_specs=(
            P(None, None, "lat", "lon", None),
            P(),
            P("section", None, None),
            P("section", None, None),
            P("section", None, None),
            P("section", None, None),
            P("section", None, None),
            P("section", None, None, None),
        ),
        out_specs=P("section", None, None, "lat", "lon", None),
        check_vma=False,
    )
```

```python
import functools

import jax
import jax.numpy as jnp
from jax import lax
from jax.experimental import pallas as pl
from jax.experimental.pallas import tpu as pltpu
from jax.sharding import PartitionSpec as P

WIN_P = 2
WIN_H = 6
WIN_W = 12
TOK = WIN_P * WIN_H * WIN_W
LEVELS = 4
MICRO = 2
WIDTH = 384
HEADS = 12
FF = 1536
QROWS = 80
GRID_ROWS = LEVELS * WIN_H * WIN_W
GROUP = 640
GUSED = 576
KDIM = 288
LOG2E = 1.4426950408889634
MESH = pl.DeviceIdType.MESH


def divide(value, by):
    return (value * (-(-65536 // by))) >> 16


def token_parts(token):
    col = divide(token, 12)
    rest = token - col * 12
    level = (rest >= 6).astype(jnp.int32)
    return col, level, rest - level * 6


def slot_row(row_half, col_half, level, row, col):
    return (row_half + 2 * col_half) * QROWS + level * 18 + row * 6 + col


def halves(position, extent):
    half = (position >= extent).astype(jnp.int32)
    return half, position - half * extent


def one_hot(rows, target):
    at = lax.broadcasted_iota(jnp.int32, (rows, target.shape[1]), 0)
    return (at == target).astype(jnp.float32).astype(jnp.bfloat16)


def grid_place(row, col, level):
    return (row * 12 + col) * 4 + level


def gather_matrix():
    place = lax.broadcasted_iota(jnp.int32, (1, GRID_ROWS), 1)
    pair = place >> 2
    row = divide(pair, 12)
    row_half, row_in = halves(row, 3)
    col_half, col_in = halves(pair - row * 12, 6)
    level = ((place & 3) + 3) & 3
    return one_hot(4 * QROWS, slot_row(1 - row_half, 1 - col_half, level, row_in, col_in))


def scatter_matrix():
    token = lax.broadcasted_iota(jnp.int32, (1, 2 * TOK), 1)
    window, rest = halves(token, TOK)
    col, level, row = token_parts(rest)
    row_half, row_in = halves(row, 3)
    col_half, col_in = halves(col, 6)
    return one_hot(4 * QROWS, slot_row(row_half, col_half, 2 * window + level, row_in, col_in))


def slot_parts():
    place = lax.broadcasted_iota(jnp.int32, (1, 4 * QROWS), 1)
    slot = divide(place, QROWS)
    rest = place - slot * QROWS
    level = divide(rest, 18)
    inner = rest - level * 18
    row = divide(inner, 6)
    return rest < 72, slot & 1, slot >> 1, level, row, inner - row * 6


def into_matrix(one):
    used, row_half, col_half, level, row, col = slot_parts()
    row = row + 3 * (row_half * one + (1 - row_half) * (1 - one))
    col = col + 6 * (col_half * one + (1 - col_half) * (1 - one))
    level = (level + 1 - one) & 3
    token = (level >> 1) * TOK + col * 12 + (level & 1) * 6 + row
    return one_hot(2 * TOK, jnp.where(used, token, -1))


def back_matrix():
    used, row_half, col_half, level, row, col = slot_parts()
    place = grid_place(row + 3 * (1 - row_half), col + 6 * (1 - col_half), (level + 1) & 3)
    return one_hot(GRID_ROWS, jnp.where(used, place, -1))


def plain_matrix():
    token = lax.broadcasted_iota(jnp.int32, (1, 2 * TOK), 1)
    window, rest = halves(token, TOK)
    col, level, row = token_parts(rest)
    return one_hot(GRID_ROWS, grid_place(row, col, 2 * window + level))


def dot(a, b):
    return jnp.dot(a, b, preferred_element_type=jnp.float32)


def dot_nt(a, b):
    return lax.dot_general(a, b, (((1,), (1,)), ((), ())), preferred_element_type=jnp.float32)


def layer_norm(values, gain):
    average = jnp.mean(values, axis=-1, keepdims=True)
    centred = values - average
    spread = jnp.mean(centred * centred, axis=-1, keepdims=True)
    return centred * lax.rsqrt(spread + 1e-05) * gain


def gelu(x):
    return x * (0.5 + 0.5 * lax.erf(x * 0.7071067811865476))


def lane_tokens():
    lane = lax.broadcasted_iota(jnp.int32, (1, 256), 1)
    return jnp.where(lane < 128, lane, 128 + (lane & 15))


def prepare_bias(first, lat, lon, lat_count, lon_count, class_ref, table_ref, rows_ref, bias_ref):
    kinds = 2 * lat_count
    to_row = lax.broadcasted_iota(jnp.int32, (32, HEADS * kinds), 0)
    to_col = lax.broadcasted_iota(jnp.int32, (32, HEADS * kinds), 1)
    wanted = (to_row & 15) * kinds + (to_row >> 4) * lat_count + lat
    own = (to_col == wanted).astype(jnp.float32).astype(jnp.bfloat16)
    table = dot(own, table_ref[...].reshape(HEADS * kinds, -1)).astype(jnp.bfloat16)
    rows_ref[...] = jnp.zeros_like(rows_ref)
    for i in range(2):
        for j in range(12):
            pb, rb = j // 6, j % 6
            for pa in range(2):
                begin = pb * 1656 + pa * 828 + rb * 138
                rows_ref[i, j, :, pa * 144 : pa * 144 + 138] = table[
                    i * 16 : i * 16 + 16, begin : begin + 138
                ]
    to_row = lax.broadcasted_iota(jnp.int32, (192, 192), 0)
    to_col = lax.broadcasted_iota(jnp.int32, (192, 192), 1)
    swap = (((to_row & 15) << 4) + (to_row >> 4) == to_col).astype(jnp.float32).astype(jnp.bfloat16)
    by_head = [
        dot(swap, rows_ref[i].reshape(192, KDIM)).astype(jnp.bfloat16) for i in range(2)
    ]
    by_head = jnp.concatenate(by_head, axis=0)
    col_a, level_a, row_a = token_parts(lane_tokens())
    base = level_a * 144 + row_a * 23 + col_a + 11
    depth = lax.broadcasted_iota(jnp.int32, (KDIM, 256), 0)
    segment = lax.broadcasted_iota(jnp.int32, (12, 128), 1) >> 4
    for cb in range(12):
        pick = (depth == base - cb).astype(jnp.float32).astype(jnp.bfloat16)
        spread = dot(by_head, pick) * LOG2E
        for i in range(2):
            for g in range(3):
                tail = None
                for t in range(4):
                    start = i * 192 + (g * 4 + t) * 16
                    piece = spread[start : start + 12]
                    bias_ref[i, cb * 12 : cb * 12 + 12, g * GROUP + t * 128 : g * GROUP + t * 128 + 128] = piece[:, 0:128]
                    last = piece[:, 128:256]
                    tail = last if tail is None else jnp.where(segment == t, last, tail)
                bias_ref[i, cb * 12 : cb * 12 + 12, g * GROUP + 512 : g * GROUP + 640] = tail
    rows_all = 6 * lat_count
    cols_all = 12 * lon_count
    one = jnp.where(first, 1, 0)
    row_start = lat * 6 + 3 * one
    col_start = lon * 12 + 6 * one
    classes = class_ref[...].reshape(LEVELS * rows_all, cols_all).astype(jnp.float32).astype(jnp.bfloat16)
    col_b, level_b, row_b = token_parts(lax.broadcasted_iota(jnp.int32, (TOK, 1), 0))

    def wrap(v, extent):
        return jnp.where(v >= extent, v - extent, v)

    def onehot(a, b):
        return (a == b).astype(jnp.float32).astype(jnp.bfloat16)

    across = dot(
        classes,
        onehot(lax.broadcasted_iota(jnp.int32, (cols_all, 256), 0), wrap(col_start + col_a, cols_all)),
    )
    down = dot_nt(
        onehot(lax.broadcasted_iota(jnp.int32, (TOK, cols_all), 1), wrap(col_start + col_b, cols_all)),
        classes,
    )
    place_a = lax.broadcasted_iota(jnp.int32, across.shape, 0)
    place_b = lax.broadcasted_iota(jnp.int32, down.shape, 1)
    for i in range(2):

        def region(place, level, row, values, axis):
            at = ((2 * i + level + one) & 3) * rows_all + wrap(row_start + row, rows_all)
            value = jnp.sum(jnp.where(place == at, values, 0.0), axis=axis, keepdims=True)
            flags = 2 * (2 * i + level >= 3).astype(jnp.int32)
            flags = flags + (lat * 6 + row >= rows_all - 3).astype(jnp.int32)
            return 4.0 * value + (one * flags).astype(jnp.float32)

        region_a = region(place_a, level_a, row_a, across, 0)
        region_b = region(place_b, level_b, row_b, down, 1)
        same = region_b == region_a
        for g in range(3):
            for t in range(5):
                lanes = slice(g * GROUP + t * 128, g * GROUP + t * 128 + 128)
                part = same[:, 0:128] if t < 4 else same[:, 128:256]
                bias_ref[i, :, lanes] = jnp.where(part, bias_ref[i, :, lanes], -1e30)


def attention(query, key, value, bias_ref, i):
    head = lax.broadcasted_iota(jnp.int32, (1, 128), 1) >> 5
    keep = [(head == t).astype(jnp.float32).astype(jnp.bfloat16) for t in range(4)]
    ones = jnp.ones((16, TOK), jnp.bfloat16)
    mixed = []
    for g in range(3):
        lanes = slice(g * 128, g * 128 + 128)
        q, k, v = query[:, lanes], key[:, lanes], value[:, lanes]
        wide = jnp.concatenate([q[0:128] * m for m in keep] + [q[128:144] * m for m in keep], axis=0)
        scores = dot_nt(k, wide) + bias_ref[i, :, g * GROUP : g * GROUP + GUSED]
        top = jnp.max(scores, axis=0, keepdims=True)
        weights = jnp.exp2(scores - top).astype(jnp.bfloat16)
        v_turned = jnp.concatenate([jnp.transpose(v.astype(jnp.float32)).astype(jnp.bfloat16), ones], axis=0)
        out = dot(v_turned, weights)
        out = out[0:128] * (1.0 / out[128:129])
        main = jnp.concatenate(
            [out[t * 32 : t * 32 + 32, t * 128 : t * 128 + 128] for t in range(4)], axis=0
        )
        main = jnp.transpose(main).astype(jnp.bfloat16)
        tail = jnp.transpose(out[:, 512:576]).astype(jnp.bfloat16)
        tail = sum(tail[t * 16 : t * 16 + 16] * keep[t] for t in range(4))
        mixed.append(jnp.concatenate([main, tail], axis=0))
    return jnp.concatenate(mixed, axis=1)


def block(x, gains_ref, joint_ref, out_ref, expand_ref, reduce_ref, bias_ref):
    gains = gains_ref[...].astype(jnp.float32)
    normed = layer_norm(x, gains[0:1]).astype(jnp.bfloat16)
    projected = dot(normed, joint_ref[...])
    query = (projected[:, 0:WIDTH] * (LOG2E * 32**-0.5)).astype(jnp.bfloat16)
    key = projected[:, WIDTH : 2 * WIDTH].astype(jnp.bfloat16)
    value = projected[:, 2 * WIDTH :].astype(jnp.bfloat16)
    mixed = []
    for i in range(2):
        rows = slice(i * TOK, i * TOK + TOK)
        mixed.append(attention(query[rows], key[rows], value[rows], bias_ref, i))
    hidden = x + dot(jnp.concatenate(mixed, axis=0), out_ref[...])
    again = layer_norm(hidden, gains[1:2]).astype(jnp.bfloat16)
    total = hidden
    step = 512
    for start in range(0, FF, step):
        act = gelu(dot(again, expand_ref[:, start : start + step])).astype(jnp.bfloat16)
        total = total + dot(act, reduce_ref[start : start + step, :])
    return total.astype(jnp.bfloat16)


def kernel(
    lat_count,
    lon_count,
    fields_hbm,
    class_hbm,
    gains_hbm,
    joint_hbm,
    oproj_hbm,
    expand_hbm,
    reduce_hbm,
    table_hbm,
    result_ref,
    fields_ref,
    class_ref,
    gains_ref,
    joint_ref,
    oproj_ref,
    expand_ref,
    reduce_ref,
    table_ref,
    into_ref,
    scatter_ref,
    last_ref,
    rows_ref,
    bias_ref,
    halo_ref,
    take_ref,
    done_ref,
    home_ref,
    load_sem,
    halo_send,
    take_recv,
    home_send,
    home_recv,
    next_send,
):
    sec = lax.axis_index("section")
    lat = lax.axis_index("lat")
    lon = lax.axis_index("lon")
    first = sec == 0
    lat_up = lax.rem(lat + 1, lat_count)
    lat_down = lax.rem(lat + lat_count - 1, lat_count)
    lon_up = lax.rem(lon + 1, lon_count)
    lon_down = lax.rem(lon + lon_count - 1, lon_count)
    behind = [(lat, lon), (lat_down, lon), (lat, lon_down), (lat_down, lon_down)]
    ahead = [(lat, lon), (lat_up, lon), (lat, lon_up), (lat_up, lon_up)]

    barrier = pltpu.get_barrier_semaphore()

    @pl.when(first)
    def _():
        for where in behind[1:] + ahead[1:]:
            pl.semaphore_signal(barrier, inc=1, device_id=(0,) + where, device_id_type=MESH)

    @pl.when(jnp.logical_not(first))
    def _():
        for where in behind:
            pl.semaphore_signal(barrier, inc=1, device_id=(0,) + where, device_id_type=MESH)

    loads = []

    def load(src, dst):
        copy = pltpu.make_async_copy(src, dst, load_sem.at[len(loads)])
        copy.start()
        loads.append(copy)
        return copy

    load_fields = load(fields_hbm, fields_ref)
    prep = [load(table_hbm.at[0], table_ref), load(class_hbm, class_ref)]
    rest = [
        load(gains_hbm.at[0], gains_ref),
        load(joint_hbm.at[0], joint_ref),
        load(oproj_hbm.at[0], oproj_ref),
        load(expand_hbm.at[0], expand_ref),
        load(reduce_hbm.at[0], reduce_ref),
    ]

    def halo_copy(m, q):
        return pltpu.make_async_remote_copy(
            src_ref=halo_ref.at[m, q],
            dst_ref=take_ref.at[m, q],
            send_sem=halo_send.at[m, q],
            recv_sem=take_recv.at[m, q],
            device_id=(0,) + behind[q],
            device_id_type=MESH,
        )

    def home_copy(m, q):
        return pltpu.make_async_remote_copy(
            src_ref=done_ref.at[m, q],
            dst_ref=home_ref.at[m, q],
            send_sem=home_send.at[m, q],
            recv_sem=home_recv.at[m, q],
            device_id=(0,) + ahead[q],
            device_id_type=MESH,
        )

    def next_copy(m, q):
        return pltpu.make_async_remote_copy(
            src_ref=done_ref.at[m, q],
            dst_ref=take_ref.at[m, q],
            send_sem=next_send.at[m, q],
            recv_sem=take_recv.at[m, q],
            device_id=(1,) + ahead[q],
            device_id_type=MESH,
        )

    load_fields.wait()

    @pl.when(first)
    def _():
        gather = gather_matrix()
        for m in range(MICRO):
            sorted_rows = dot(gather, fields_ref[m].reshape(GRID_ROWS, WIDTH)).astype(jnp.bfloat16)
            take_ref[m, 0] = sorted_rows[0:QROWS]
            for q in range(1, 4):
                halo_ref[m, q] = sorted_rows[q * QROWS : (q + 1) * QROWS]
            if m == 0:
                pl.semaphore_wait(barrier, 10)
            for q in (3, 2, 1):
                halo_copy(m, q).start()

    into_ref[...] = into_matrix(jnp.where(first, 1, 0))

    @pl.when(first)
    def _():
        scatter_ref[...] = scatter_matrix()
        last_ref[...] = back_matrix()

    @pl.when(jnp.logical_not(first))
    def _():
        last_ref[:, 0 : 2 * TOK] = plain_matrix()

    for copy in prep:
        copy.wait()
    prepare_bias(first, lat, lon, lat_count, lon_count, class_ref, table_ref, rows_ref, bias_ref)
    for copy in rest:
        copy.wait()

    def step(m, carry):
        @pl.when(first)
        def _():
            for q in range(1, 4):
                halo_copy(m, q).wait_recv()

        @pl.when(jnp.logical_not(first))
        def _():
            for q in range(4):
                next_copy(m, q).wait_recv()

        x = dot(into_ref[...], take_ref[m].reshape(4 * QROWS, WIDTH))
        y = block(x, gains_ref, joint_ref, oproj_ref, expand_ref, reduce_ref, bias_ref)

        @pl.when(first)
        def _():
            pieces = dot(scatter_ref[...], y).astype(jnp.bfloat16)
            done_ref[m] = pieces.reshape(4, QROWS, WIDTH)
            home_ref[m, 0] = pieces[0:QROWS]
            for q in (3, 2, 1, 0):
                next_copy(m, q).start()
            for q in (3, 2, 1):
                home_copy(m, q).start()

        @pl.when(jnp.logical_not(first))
        def _():
            write(m, dot(last_ref[:, 0 : 2 * TOK], y).astype(jnp.bfloat16))

        return carry

    def write(m, rows):
        result_ref[m] = rows.reshape(WIN_H, WIN_W, LEVELS, WIDTH)

    lax.fori_loop(0, MICRO, step, 0)

    @pl.when(first)
    def _():
        for m in range(MICRO):
            for q in range(1, 4):
                home_copy(m, q).wait_recv()
            write(m, dot(last_ref[...], home_ref[m].reshape(4 * QROWS, WIDTH)).astype(jnp.bfloat16))
        for m in range(MICRO):
            for q in range(1, 4):
                halo_copy(m, q).wait_send()
                home_copy(m, q).wait_send()
            for q in range(4):
                next_copy(m, q).wait_send()


def body(
    fields, surface_class, norm_gains, joint_proj, out_proj, expand_proj, reduce_proj, earth_bias
):
    lat_count = lax.axis_size("lat")
    lon_count = lax.axis_size("lon")
    fields = jnp.transpose(fields, (0, 2, 3, 1, 4))
    operands = (
        fields, surface_class, norm_gains, joint_proj, out_proj, expand_proj, reduce_proj,
        jnp.transpose(earth_bias, (0, 2, 1, 3)),
    )
    bf16 = jnp.bfloat16
    scratch = [
        pltpu.VMEM(fields.shape, bf16),
        pltpu.VMEM(surface_class.shape, jnp.int32),
        pltpu.VMEM((2, WIDTH), bf16),
        pltpu.VMEM((WIDTH, 3 * WIDTH), bf16),
        pltpu.VMEM((WIDTH, WIDTH), bf16),
        pltpu.VMEM((WIDTH, FF), bf16),
        pltpu.VMEM((FF, WIDTH), bf16),
        pltpu.VMEM((HEADS,) + earth_bias.shape[1:2] + earth_bias.shape[3:], bf16),
        pltpu.VMEM((2 * TOK, 4 * QROWS), bf16),
        pltpu.VMEM((4 * QROWS, 2 * TOK), bf16),
        pltpu.VMEM((GRID_ROWS, 4 * QROWS), bf16),
        pltpu.VMEM((2, 12, 16, KDIM), bf16),
        pltpu.VMEM((2, TOK, 3 * GROUP), jnp.float32),
        pltpu.VMEM((MICRO, 4, QROWS, WIDTH), bf16),
        pltpu.VMEM((MICRO, 4, QROWS, WIDTH), bf16),
        pltpu.VMEM((MICRO, 4, QROWS, WIDTH), bf16),
        pltpu.VMEM((MICRO, 4, QROWS, WIDTH), bf16),
        pltpu.SemaphoreType.DMA((14,)),
        pltpu.SemaphoreType.DMA((MICRO, 4)),
        pltpu.SemaphoreType.DMA((MICRO, 4)),
        pltpu.SemaphoreType.DMA((MICRO, 4)),
        pltpu.SemaphoreType.DMA((MICRO, 4)),
        pltpu.SemaphoreType.DMA((MICRO, 4)),
    ]
    result = pl.pallas_call(
        functools.partial(kernel, lat_count, lon_count),
        out_shape=jax.ShapeDtypeStruct(fields.shape, bf16),
        in_specs=[pl.BlockSpec(memory_space=pl.ANY)] * len(operands),
        out_specs=pl.BlockSpec(memory_space=pltpu.VMEM),
        scratch_shapes=scratch,
        compiler_params=pltpu.CompilerParams(
            collective_id=0, has_side_effects=True, vmem_limit_bytes=63 * 1024 * 1024
        ),
        name="two_blocks",
    )(*operands)
    return jnp.transpose(result, (0, 3, 1, 2, 4))[None]


def solution(mesh):
    return jax.shard_map(
        body,
        mesh=mesh,
        in_specs=(
            P(None, None, "lat", "lon", None),
            P(),
            P("section", None, None),
            P("section", None, None),
            P("section", None, None),
            P("section", None, None),
            P("section", None, None),
            P("section", None, None, None),
        ),
        out_specs=P("section", None, None, "lat", "lon", None),
        check_vma=False,
    )
```

```python
import functools

import jax
import jax.numpy as jnp
from jax import lax
from jax.experimental import pallas as pl
from jax.experimental.pallas import tpu as pltpu
from jax.sharding import PartitionSpec as P

WIN_P = 2
WIN_H = 6
WIN_W = 12
TOK = WIN_P * WIN_H * WIN_W
LEVELS = 4
MICRO = 2
WIDTH = 384
HEADS = 12
FF = 1536
QROWS = 80
GRID_ROWS = LEVELS * WIN_H * WIN_W
GROUP = 640
GUSED = 576
KDIM = 288
LOG2E = 1.4426950408889634
MESH = pl.DeviceIdType.MESH


def divide(value, by):
    return (value * (-(-65536 // by))) >> 16


def token_parts(token):
    col = divide(token, 12)
    rest = token - col * 12
    level = (rest >= 6).astype(jnp.int32)
    return col, level, rest - level * 6


def slot_row(row_half, col_half, level, row, col):
    return (row_half + 2 * col_half) * QROWS + level * 18 + row * 6 + col


def halves(position, extent):
    half = (position >= extent).astype(jnp.int32)
    return half, position - half * extent


def one_hot(rows, target):
    at = lax.broadcasted_iota(jnp.int32, (rows, target.shape[1]), 0)
    return (at == target).astype(jnp.float32).astype(jnp.bfloat16)


def grid_place(row, col, level):
    return (row * 12 + col) * 4 + level


def gather_matrix():
    place = lax.broadcasted_iota(jnp.int32, (1, GRID_ROWS), 1)
    pair = place >> 2
    row = divide(pair, 12)
    row_half, row_in = halves(row, 3)
    col_half, col_in = halves(pair - row * 12, 6)
    level = ((place & 3) + 3) & 3
    return one_hot(4 * QROWS, slot_row(1 - row_half, 1 - col_half, level, row_in, col_in))


def scatter_matrix():
    token = lax.broadcasted_iota(jnp.int32, (1, 2 * TOK), 1)
    window, rest = halves(token, TOK)
    col, level, row = token_parts(rest)
    row_half, row_in = halves(row, 3)
    col_half, col_in = halves(col, 6)
    return one_hot(4 * QROWS, slot_row(row_half, col_half, 2 * window + level, row_in, col_in))


def slot_parts():
    place = lax.broadcasted_iota(jnp.int32, (1, 4 * QROWS), 1)
    slot = divide(place, QROWS)
    rest = place - slot * QROWS
    level = divide(rest, 18)
    inner = rest - level * 18
    row = divide(inner, 6)
    return rest < 72, slot & 1, slot >> 1, level, row, inner - row * 6


def into_matrix(one):
    used, row_half, col_half, level, row, col = slot_parts()
    row = row + 3 * (row_half * one + (1 - row_half) * (1 - one))
    col = col + 6 * (col_half * one + (1 - col_half) * (1 - one))
    level = (level + 1 - one) & 3
    token = (level >> 1) * TOK + col * 12 + (level & 1) * 6 + row
    return one_hot(2 * TOK, jnp.where(used, token, -1))


def back_matrix():
    used, row_half, col_half, level, row, col = slot_parts()
    place = grid_place(row + 3 * (1 - row_half), col + 6 * (1 - col_half), (level + 1) & 3)
    return one_hot(GRID_ROWS, jnp.where(used, place, -1))


def plain_matrix():
    token = lax.broadcasted_iota(jnp.int32, (1, 2 * TOK), 1)
    window, rest = halves(token, TOK)
    col, level, row = token_parts(rest)
    return one_hot(GRID_ROWS, grid_place(row, col, 2 * window + level))


def dot(a, b):
    return jnp.dot(a, b, preferred_element_type=jnp.float32)


def dot_nt(a, b):
    return lax.dot_general(a, b, (((1,), (1,)), ((), ())), preferred_element_type=jnp.float32)


def layer_norm(values, gain):
    average = jnp.mean(values, axis=-1, keepdims=True)
    centred = values - average
    spread = jnp.mean(centred * centred, axis=-1, keepdims=True)
    return centred * lax.rsqrt(spread + 1e-05) * gain


def gelu(x):
    return x * (0.5 + 0.5 * lax.erf(x * 0.7071067811865476))


def lane_tokens():
    lane = lax.broadcasted_iota(jnp.int32, (1, 256), 1)
    return jnp.where(lane < 128, lane, 128 + (lane & 15))


def prepare_bias(first, lat, lon, lat_count, lon_count, class_ref, table_ref, rows_ref, turned_ref, bias_ref):
    kinds = 2 * lat_count
    to_row = lax.broadcasted_iota(jnp.int32, (32, HEADS * kinds), 0)
    to_col = lax.broadcasted_iota(jnp.int32, (32, HEADS * kinds), 1)
    wanted = (to_row & 15) * kinds + (to_row >> 4) * lat_count + lat
    own = (to_col == wanted).astype(jnp.float32).astype(jnp.bfloat16)
    table = dot(own, table_ref[...].reshape(HEADS * kinds, -1)).astype(jnp.bfloat16)
    rows_ref[...] = jnp.zeros_like(rows_ref)
    for i in range(2):
        for j in range(12):
            pb, rb = j // 6, j % 6
            for pa in range(2):
                begin = pb * 1656 + pa * 828 + rb * 138
                rows_ref[i, j, :, pa * 144 : pa * 144 + 138] = table[
                    i * 16 : i * 16 + 16, begin : begin + 138
                ]
    to_row = lax.broadcasted_iota(jnp.int32, (192, 192), 0)
    to_col = lax.broadcasted_iota(jnp.int32, (192, 192), 1)
    swap = (((to_row & 15) << 4) + (to_row >> 4) == to_col).astype(jnp.float32).astype(jnp.bfloat16)
    by_head = [
        dot(swap, rows_ref[i].reshape(192, KDIM)).astype(jnp.bfloat16) for i in range(2)
    ]
    by_head = jnp.concatenate(by_head, axis=0)
    col_a, level_a, row_a = token_parts(lane_tokens())
    base = level_a * 144 + row_a * 23 + col_a + 11
    depth = lax.broadcasted_iota(jnp.int32, (KDIM, 256), 0)
    for cb in range(12):
        pick = (depth == base - cb).astype(jnp.float32).astype(jnp.bfloat16)
        spread = dot(by_head, pick)
        for i in range(2):
            for h in range(HEADS):
                start = i * 192 + h * 16
                turned_ref[i * HEADS + h, cb * 12 : cb * 12 + 12, :] = spread[start : start + 12]
    rows_all = 6 * lat_count
    cols_all = 12 * lon_count
    one = jnp.where(first, 1, 0)
    row_start = lat * 6 + 3 * one
    col_start = lon * 12 + 6 * one
    classes = class_ref[...].reshape(LEVELS * rows_all, cols_all).astype(jnp.float32).astype(jnp.bfloat16)
    col_b, level_b, row_b = token_parts(lax.broadcasted_iota(jnp.int32, (TOK, 1), 0))

    def wrap(v, extent):
        return jnp.where(v >= extent, v - extent, v)

    def onehot(a, b):
        return (a == b).astype(jnp.float32).astype(jnp.bfloat16)

    across = dot(
        classes,
        onehot(lax.broadcasted_iota(jnp.int32, (cols_all, 256), 0), wrap(col_start + col_a, cols_all)),
    )
    down = dot_nt(
        onehot(lax.broadcasted_iota(jnp.int32, (TOK, cols_all), 1), wrap(col_start + col_b, cols_all)),
        classes,
    )
    identity = (
        lax.broadcasted_iota(jnp.int32, (TOK, 256), 0) == lax.broadcasted_iota(jnp.int32, (TOK, 256), 1)
    )
    identity = identity.astype(jnp.float32).astype(jnp.bfloat16)
    place_a = lax.broadcasted_iota(jnp.int32, across.shape, 0)
    place_b = lax.broadcasted_iota(jnp.int32, down.shape, 1)
    for i in range(2):

        def region(place, level, row, values, axis):
            at = ((2 * i + level + one) & 3) * rows_all + wrap(row_start + row, rows_all)
            value = jnp.sum(jnp.where(place == at, values, 0.0), axis=axis, keepdims=True)
            flags = 2 * (2 * i + level >= 3).astype(jnp.int32)
            flags = flags + (lat * 6 + row >= rows_all - 3).astype(jnp.int32)
            return 4.0 * value + (one * flags).astype(jnp.float32)

        region_a = region(place_a, level_a, row_a, across, 0)
        region_b = region(place_b, level_b, row_b, down, 1)
        same = region_b == region_a
        for g in range(3):
            heads = [turned_ref[i * HEADS + g * 4 + t] for t in range(4)]
            stack = jnp.concatenate([h[0:128] for h in heads] + [h[128:144] for h in heads], axis=0)
            spread = dot_nt(identity, stack.astype(jnp.bfloat16)) * LOG2E
            for t in range(5):
                lanes = slice(t * 128, min(t * 128 + 128, GUSED))
                part = same[:, 0:128] if t < 4 else same[:, 128:192]
                to = slice(g * GROUP + lanes.start, g * GROUP + lanes.stop)
                bias_ref[i, :, to] = jnp.where(part, spread[:, lanes], -1e30)
            bias_ref[i, :, g * GROUP + GUSED : (g + 1) * GROUP] = jnp.full((TOK, GROUP - GUSED), -1e30, jnp.float32)


def attention(query, key, value, bias_ref, i):
    head = lax.broadcasted_iota(jnp.int32, (1, 128), 1) >> 5
    keep = [(head == t).astype(jnp.float32).astype(jnp.bfloat16) for t in range(4)]
    segment = lax.broadcasted_iota(jnp.int32, (1, 128), 1) >> 4
    blank = jnp.zeros((64, 128), jnp.bfloat16)
    blank_wide = jnp.zeros((64, 256), jnp.bfloat16)
    mixed = []
    for g in range(3):
        lanes = slice(g * 128, g * 128 + 128)
        q, k, v = query[:, lanes], key[:, lanes], value[:, lanes]
        wide = jnp.concatenate([k[0:128] * m for m in keep] + [k[128:144] * m for m in keep] + [blank], axis=0)
        scores = dot_nt(q, wide) + bias_ref[i, :, g * GROUP : (g + 1) * GROUP]
        tail = scores[:, 512:640]
        top, weights = [], []
        for t in range(4):
            main = scores[:, t * 128 : t * 128 + 128]
            joined = jnp.maximum(main, jnp.where(segment == t, tail, -1e30))
            top.append(jnp.max(joined, axis=1, keepdims=True))
            weights.append(jnp.exp2(main - top[t]).astype(jnp.bfloat16))
        tops = jnp.where(segment < 2, jnp.where(segment == 0, top[0], top[1]), jnp.where(segment == 2, top[2], top[3]))
        weights.append(jnp.exp2(tail - tops).astype(jnp.bfloat16))
        weights = jnp.concatenate(weights, axis=1)
        pairs = [jnp.concatenate([v[0:128] * m, jnp.broadcast_to(m, (128, 128))], axis=1) for m in keep]
        pairs += [jnp.concatenate([v[128:144] * m, jnp.broadcast_to(m, (16, 128))], axis=1) for m in keep]
        out = dot(weights, jnp.concatenate(pairs + [blank_wide], axis=0))
        mixed.append((out[:, 0:128] / out[:, 128:256]).astype(jnp.bfloat16))
    return jnp.concatenate(mixed, axis=1)


def block(x, gains_ref, joint_ref, out_ref, expand_ref, reduce_ref, bias_ref):
    gains = gains_ref[...].astype(jnp.float32)
    normed = layer_norm(x, gains[0:1]).astype(jnp.bfloat16)
    projected = dot(normed, joint_ref[...])
    query = (projected[:, 0:WIDTH] * (LOG2E * 32**-0.5)).astype(jnp.bfloat16)
    key = projected[:, WIDTH : 2 * WIDTH].astype(jnp.bfloat16)
    value = projected[:, 2 * WIDTH :].astype(jnp.bfloat16)
    mixed = []
    for i in range(2):
        rows = slice(i * TOK, i * TOK + TOK)
        mixed.append(attention(query[rows], key[rows], value[rows], bias_ref, i))
    hidden = x + dot(jnp.concatenate(mixed, axis=0), out_ref[...])
    again = layer_norm(hidden, gains[1:2]).astype(jnp.bfloat16)
    total = hidden
    step = 512
    for start in range(0, FF, step):
        act = gelu(dot(again, expand_ref[:, start : start + step])).astype(jnp.bfloat16)
        total = total + dot(act, reduce_ref[start : start + step, :])
    return total.astype(jnp.bfloat16)


def kernel(
    lat_count,
    lon_count,
    fields_hbm,
    class_hbm,
    gains_hbm,
    joint_hbm,
    oproj_hbm,
    expand_hbm,
    reduce_hbm,
    table_hbm,
    result_ref,
    fields_ref,
    class_ref,
    gains_ref,
    joint_ref,
    oproj_ref,
    expand_ref,
    reduce_ref,
    table_ref,
    into_ref,
    scatter_ref,
    last_ref,
    rows_ref,
    turned_ref,
    bias_ref,
    halo_ref,
    take_ref,
    done_ref,
    home_ref,
    load_sem,
    halo_send,
    take_recv,
    home_send,
    home_recv,
    next_send,
):
    sec = lax.axis_index("section")
    lat = lax.axis_index("lat")
    lon = lax.axis_index("lon")
    first = sec == 0
    lat_up = lax.rem(lat + 1, lat_count)
    lat_down = lax.rem(lat + lat_count - 1, lat_count)
    lon_up = lax.rem(lon + 1, lon_count)
    lon_down = lax.rem(lon + lon_count - 1, lon_count)
    behind = [(lat, lon), (lat_down, lon), (lat, lon_down), (lat_down, lon_down)]
    ahead = [(lat, lon), (lat_up, lon), (lat, lon_up), (lat_up, lon_up)]

    barrier = pltpu.get_barrier_semaphore()

    @pl.when(first)
    def _():
        for where in behind[1:] + ahead[1:]:
            pl.semaphore_signal(barrier, inc=1, device_id=(0,) + where, device_id_type=MESH)

    @pl.when(jnp.logical_not(first))
    def _():
        for where in behind:
            pl.semaphore_signal(barrier, inc=1, device_id=(0,) + where, device_id_type=MESH)

    loads = []

    def load(src, dst):
        copy = pltpu.make_async_copy(src, dst, load_sem.at[len(loads)])
        copy.start()
        loads.append(copy)
        return copy

    load_fields = load(fields_hbm, fields_ref)
    prep = [load(table_hbm.at[0], table_ref), load(class_hbm, class_ref)]
    rest = [
        load(gains_hbm.at[0], gains_ref),
        load(joint_hbm.at[0], joint_ref),
        load(oproj_hbm.at[0], oproj_ref),
        load(expand_hbm.at[0], expand_ref),
        load(reduce_hbm.at[0], reduce_ref),
    ]

    def halo_copy(m, q):
        return pltpu.make_async_remote_copy(
            src_ref=halo_ref.at[m, q],
            dst_ref=take_ref.at[m, q],
            send_sem=halo_send.at[m, q],
            recv_sem=take_recv.at[m, q],
            device_id=(0,) + behind[q],
            device_id_type=MESH,
        )

    def home_copy(m, q):
        return pltpu.make_async_remote_copy(
            src_ref=done_ref.at[m, q],
            dst_ref=home_ref.at[m, q],
            send_sem=home_send.at[m, q],
            recv_sem=home_recv.at[m, q],
            device_id=(0,) + ahead[q],
            device_id_type=MESH,
        )

    def next_copy(m, q):
        return pltpu.make_async_remote_copy(
            src_ref=done_ref.at[m, q],
            dst_ref=take_ref.at[m, q],
            send_sem=next_send.at[m, q],
            recv_sem=take_recv.at[m, q],
            device_id=(1,) + ahead[q],
            device_id_type=MESH,
        )

    load_fields.wait()

    @pl.when(first)
    def _():
        gather = gather_matrix()
        for m in range(MICRO):
            sorted_rows = dot(gather, fields_ref[m].reshape(GRID_ROWS, WIDTH)).astype(jnp.bfloat16)
            take_ref[m, 0] = sorted_rows[0:QROWS]
            for q in range(1, 4):
                halo_ref[m, q] = sorted_rows[q * QROWS : (q + 1) * QROWS]
            if m == 0:
                pl.semaphore_wait(barrier, 10)
            for q in (3, 2, 1):
                halo_copy(m, q).start()

    into_ref[...] = into_matrix(jnp.where(first, 1, 0))

    @pl.when(first)
    def _():
        scatter_ref[...] = scatter_matrix()
        last_ref[...] = back_matrix()

    @pl.when(jnp.logical_not(first))
    def _():
        last_ref[:, 0 : 2 * TOK] = plain_matrix()

    for copy in prep:
        copy.wait()
    prepare_bias(first, lat, lon, lat_count, lon_count, class_ref, table_ref, rows_ref, turned_ref, bias_ref)
    for copy in rest:
        copy.wait()

    def step(m, carry):
        @pl.when(first)
        def _():
            for q in range(1, 4):
                halo_copy(m, q).wait_recv()

        @pl.when(jnp.logical_not(first))
        def _():
            for q in range(4):
                next_copy(m, q).wait_recv()

        x = dot(into_ref[...], take_ref[m].reshape(4 * QROWS, WIDTH))
        y = block(x, gains_ref, joint_ref, oproj_ref, expand_ref, reduce_ref, bias_ref)

        @pl.when(first)
        def _():
            pieces = dot(scatter_ref[...], y).astype(jnp.bfloat16)
            done_ref[m] = pieces.reshape(4, QROWS, WIDTH)
            home_ref[m, 0] = pieces[0:QROWS]
            for q in (3, 2, 1, 0):
                next_copy(m, q).start()
            for q in (3, 2, 1):
                home_copy(m, q).start()

        @pl.when(jnp.logical_not(first))
        def _():
            write(m, dot(last_ref[:, 0 : 2 * TOK], y).astype(jnp.bfloat16))

        return carry

    def write(m, rows):
        result_ref[m] = rows.reshape(WIN_H, WIN_W, LEVELS, WIDTH)

    lax.fori_loop(0, MICRO, step, 0)

    @pl.when(first)
    def _():
        for m in range(MICRO):
            for q in range(1, 4):
                home_copy(m, q).wait_recv()
            write(m, dot(last_ref[...], home_ref[m].reshape(4 * QROWS, WIDTH)).astype(jnp.bfloat16))
        for m in range(MICRO):
            for q in range(1, 4):
                halo_copy(m, q).wait_send()
                home_copy(m, q).wait_send()
            for q in range(4):
                next_copy(m, q).wait_send()


def body(
    fields, surface_class, norm_gains, joint_proj, out_proj, expand_proj, reduce_proj, earth_bias
):
    lat_count = lax.axis_size("lat")
    lon_count = lax.axis_size("lon")
    fields = jnp.transpose(fields, (0, 2, 3, 1, 4))
    operands = (
        fields, surface_class, norm_gains, joint_proj, out_proj, expand_proj, reduce_proj,
        jnp.transpose(earth_bias, (0, 2, 1, 3)),
    )
    bf16 = jnp.bfloat16
    scratch = [
        pltpu.VMEM(fields.shape, bf16),
        pltpu.VMEM(surface_class.shape, jnp.int32),
        pltpu.VMEM((2, WIDTH), bf16),
        pltpu.VMEM((WIDTH, 3 * WIDTH), bf16),
        pltpu.VMEM((WIDTH, WIDTH), bf16),
        pltpu.VMEM((WIDTH, FF), bf16),
        pltpu.VMEM((FF, WIDTH), bf16),
        pltpu.VMEM((HEADS,) + earth_bias.shape[1:2] + earth_bias.shape[3:], bf16),
        pltpu.VMEM((2 * TOK, 4 * QROWS), bf16),
        pltpu.VMEM((4 * QROWS, 2 * TOK), bf16),
        pltpu.VMEM((GRID_ROWS, 4 * QROWS), bf16),
        pltpu.VMEM((2, 12, 16, KDIM), bf16),
        pltpu.VMEM((2 * HEADS, TOK, 256), jnp.float32),
        pltpu.VMEM((2, TOK, 3 * GROUP), jnp.float32),
        pltpu.VMEM((MICRO, 4, QROWS, WIDTH), bf16),
        pltpu.VMEM((MICRO, 4, QROWS, WIDTH), bf16),
        pltpu.VMEM((MICRO, 4, QROWS, WIDTH), bf16),
        pltpu.VMEM((MICRO, 4, QROWS, WIDTH), bf16),
        pltpu.SemaphoreType.DMA((14,)),
        pltpu.SemaphoreType.DMA((MICRO, 4)),
        pltpu.SemaphoreType.DMA((MICRO, 4)),
        pltpu.SemaphoreType.DMA((MICRO, 4)),
        pltpu.SemaphoreType.DMA((MICRO, 4)),
        pltpu.SemaphoreType.DMA((MICRO, 4)),
    ]
    result = pl.pallas_call(
        functools.partial(kernel, lat_count, lon_count),
        out_shape=pltpu.VMEM(fields.shape, bf16),
        in_specs=[pl.BlockSpec(memory_space=pltpu.HBM)] * len(operands),
        out_specs=pl.BlockSpec(memory_space=pltpu.VMEM),
        scratch_shapes=scratch,
        compiler_params=pltpu.CompilerParams(
            collective_id=0, has_side_effects=True, vmem_limit_bytes=56 * 1024 * 1024
        ),
        name="two_blocks",
    )(*operands)
    return jnp.transpose(result, (0, 3, 1, 2, 4))[None]


def solution(mesh):
    return jax.shard_map(
        body,
        mesh=mesh,
        in_specs=(
            P(None, None, "lat", "lon", None),
            P(),
            P("section", None, None),
            P("section", None, None),
            P("section", None, None),
            P("section", None, None),
            P("section", None, None),
            P("section", None, None, None),
        ),
        out_specs=P("section", None, None, "lat", "lon", None),
        check_vma=False,
    )
```

```python
import functools

import jax
import jax.numpy as jnp
from jax import lax
from jax.experimental import pallas as pl
from jax.experimental.pallas import tpu as pltpu
from jax.sharding import PartitionSpec as P

WIN_P = 2
WIN_H = 6
WIN_W = 12
TOK = WIN_P * WIN_H * WIN_W
LEVELS = 4
MICRO = 2
WIDTH = 384
HEADS = 12
FF = 1536
PIECES = 8
PROWS = 112
PACKED = 384
GRID_ROWS = LEVELS * WIN_H * WIN_W
GROUP = 640
GUSED = 576
KDIM = 288
LOG2E = 1.4426950408889634
MESH = pl.DeviceIdType.MESH


def divide(value, by):
    return (value * (-(-65536 // by))) >> 16


def token_parts(token):
    col = divide(token, 12)
    rest = token - col * 12
    level = (rest >= 6).astype(jnp.int32)
    return col, level, rest - level * 6


def packed_row(window, row_half, col_half, level, row, col):
    piece = window * 4 + row_half + 2 * col_half
    inner = level * 18 + row * 6 + col
    return jnp.where(inner < 32, piece * 32 + inner, 256 + piece * 16 + inner - 32)


def halves(position, extent):
    half = (position >= extent).astype(jnp.int32)
    return half, position - half * extent


def one_hot(rows, target):
    at = lax.broadcasted_iota(jnp.int32, (rows, target.shape[1]), 0)
    return (at == target).astype(jnp.float32).astype(jnp.bfloat16)


def grid_place(row, col, level):
    return (row * 12 + col) * 4 + level


def pack_matrix(target):
    row = lax.broadcasted_iota(jnp.int32, (PACKED, 1), 0)
    last = jnp.where((row & 12) == 12, -1, row - (row & 12))
    row = jnp.where(row < 256, row, last)
    return (row == target).astype(jnp.float32).astype(jnp.bfloat16)


def gather_matrix():
    place = lax.broadcasted_iota(jnp.int32, (1, GRID_ROWS), 1)
    pair = place >> 2
    row = divide(pair, 12)
    row_half, row_in = halves(row, 3)
    col_half, col_in = halves(pair - row * 12, 6)
    level = ((place & 3) + 3) & 3
    return pack_matrix(packed_row(level >> 1, 1 - row_half, 1 - col_half, level & 1, row_in, col_in))


def scatter_matrix():
    token = lax.broadcasted_iota(jnp.int32, (1, 2 * TOK), 1)
    window, rest = halves(token, TOK)
    col, level, row = token_parts(rest)
    row_half, row_in = halves(row, 3)
    col_half, col_in = halves(col, 6)
    return pack_matrix(packed_row(window, row_half, col_half, level, row_in, col_in))


def packed_parts():
    place = lax.broadcasted_iota(jnp.int32, (1, PACKED), 1)
    early = place < 256
    piece = jnp.where(early, place >> 5, (place - 256) >> 4)
    inner = jnp.where(early, place & 31, 32 + (place & 3))
    used = early | ((place & 12) != 12)
    level, rest = halves(inner, 18)
    row = divide(rest, 6)
    return used, piece & 1, (piece >> 1) & 1, 2 * (piece >> 2) + level, row, rest - row * 6


def into_matrix(one):
    used, row_half, col_half, level, row, col = packed_parts()
    row = row + 3 * (row_half * one + (1 - row_half) * (1 - one))
    col = col + 6 * (col_half * one + (1 - col_half) * (1 - one))
    level = (level + 1 - one) & 3
    token = (level >> 1) * TOK + col * 12 + (level & 1) * 6 + row
    return one_hot(2 * TOK, jnp.where(used, token, -1))


def back_matrix():
    used, row_half, col_half, level, row, col = packed_parts()
    place = grid_place(row + 3 * (1 - row_half), col + 6 * (1 - col_half), (level + 1) & 3)
    return one_hot(GRID_ROWS, jnp.where(used, place, -1))


def plain_matrix():
    token = lax.broadcasted_iota(jnp.int32, (1, 2 * TOK), 1)
    window, rest = halves(token, TOK)
    col, level, row = token_parts(rest)
    return one_hot(GRID_ROWS, grid_place(row, col, 2 * window + level))


def pack(rows, refs, m):
    rows = rows.astype(jnp.bfloat16)
    chunk = (lax.broadcasted_iota(jnp.int32, (16 * PIECES, 1), 0) >> 2) & 3
    last = rows[256:].astype(jnp.float32)
    last = jnp.where(chunk == 0, last[:, 0:128], jnp.where(chunk == 1, last[:, 128:256], last[:, 256:384]))
    last = last.astype(jnp.bfloat16)
    for piece in range(PIECES):
        for ref in refs[piece]:
            for c in range(3):
                ref[m, piece, c * 32 : c * 32 + 32, :] = rows[piece * 32 : piece * 32 + 32, c * 128 : c * 128 + 128]
            ref[m, piece, 96:112, :] = last[piece * 16 : piece * 16 + 16]


def unpack(ref, m):
    chunk = (lax.broadcasted_iota(jnp.int32, (16 * PIECES, 1), 0) >> 2) & 3
    rows = [
        jnp.concatenate([ref[m, piece, c * 32 : c * 32 + 32, :] for c in range(3)], axis=1)
        for piece in range(PIECES)
    ]
    last = jnp.concatenate([ref[m, piece, 96:112, :] for piece in range(PIECES)], axis=0).astype(jnp.float32)
    last = jnp.concatenate([jnp.where(chunk == c, last, 0.0) for c in range(3)], axis=1)
    return jnp.concatenate(rows + [last.astype(jnp.bfloat16)], axis=0)


def dot(a, b):
    return jnp.dot(a, b, preferred_element_type=jnp.float32)


def dot_nt(a, b):
    return lax.dot_general(a, b, (((1,), (1,)), ((), ())), preferred_element_type=jnp.float32)


def layer_norm(values, gain):
    average = jnp.mean(values, axis=-1, keepdims=True)
    centred = values - average
    spread = jnp.mean(centred * centred, axis=-1, keepdims=True)
    return centred * lax.rsqrt(spread + 1e-05) * gain


def gelu(x):
    return x * (0.5 + 0.5 * lax.erf(x * 0.7071067811865476))


def lane_tokens():
    lane = lax.broadcasted_iota(jnp.int32, (1, 256), 1)
    return jnp.where(lane < 128, lane, 128 + (lane & 15))


def prepare_bias(first, lat, lon, lat_count, lon_count, class_ref, table_ref, rows_ref, turned_ref, bias_ref):
    kinds = 2 * lat_count
    one = jnp.where(first, 1, 0)
    lats = (lat, lax.rem(lat + lat_count - one, lat_count))
    lons = (lon, lax.rem(lon + lon_count - one, lon_count))
    to_row = lax.broadcasted_iota(jnp.int32, (32, HEADS * kinds), 0)
    to_col = lax.broadcasted_iota(jnp.int32, (32, HEADS * kinds), 1)
    kind = jnp.where(to_row < 16, lat, lat_count + lats[1])
    wanted = (to_row & 15) * kinds + kind
    own = (to_col == wanted).astype(jnp.float32).astype(jnp.bfloat16)
    table = dot(own, table_ref[...].reshape(HEADS * kinds, -1)).astype(jnp.bfloat16)
    rows_ref[...] = jnp.zeros_like(rows_ref)
    for i in range(2):
        for j in range(12):
            pb, rb = j // 6, j % 6
            for pa in range(2):
                begin = pb * 1656 + pa * 828 + rb * 138
                rows_ref[i, j, :, pa * 144 : pa * 144 + 138] = table[
                    i * 16 : i * 16 + 16, begin : begin + 138
                ]
    to_row = lax.broadcasted_iota(jnp.int32, (192, 192), 0)
    to_col = lax.broadcasted_iota(jnp.int32, (192, 192), 1)
    swap = (((to_row & 15) << 4) + (to_row >> 4) == to_col).astype(jnp.float32).astype(jnp.bfloat16)
    by_head = [
        dot(swap, rows_ref[i].reshape(192, KDIM)).astype(jnp.bfloat16) for i in range(2)
    ]
    by_head = jnp.concatenate(by_head, axis=0)
    col_a, level_a, row_a = token_parts(lane_tokens())
    base = level_a * 144 + row_a * 23 + col_a + 11
    depth = lax.broadcasted_iota(jnp.int32, (KDIM, 256), 0)
    for cb in range(12):
        pick = (depth == base - cb).astype(jnp.float32).astype(jnp.bfloat16)
        spread = dot(by_head, pick)
        for i in range(2):
            for h in range(HEADS):
                start = i * 192 + h * 16
                turned_ref[i * HEADS + h, cb * 12 : cb * 12 + 12, :] = spread[start : start + 12]
    rows_all = 6 * lat_count
    cols_all = 12 * lon_count
    classes = class_ref[...].reshape(LEVELS * rows_all, cols_all).astype(jnp.float32).astype(jnp.bfloat16)
    col_b, level_b, row_b = token_parts(lax.broadcasted_iota(jnp.int32, (TOK, 1), 0))

    def wrap(v, extent):
        return jnp.where(v >= extent, v - extent, v)

    def onehot(a, b):
        return (a == b).astype(jnp.float32).astype(jnp.bfloat16)

    identity = (
        lax.broadcasted_iota(jnp.int32, (TOK, 256), 0) == lax.broadcasted_iota(jnp.int32, (TOK, 256), 1)
    )
    identity = identity.astype(jnp.float32).astype(jnp.bfloat16)
    place_a = lax.broadcasted_iota(jnp.int32, (LEVELS * rows_all, 256), 0)
    place_b = lax.broadcasted_iota(jnp.int32, (TOK, LEVELS * rows_all), 1)
    for i in range(2):
        row_start = lats[i] * 6 + 3 * one
        col_start = lons[i] * 12 + 6 * one
        across = dot(
            classes,
            onehot(lax.broadcasted_iota(jnp.int32, (cols_all, 256), 0), wrap(col_start + col_a, cols_all)),
        )
        down = dot_nt(
            onehot(lax.broadcasted_iota(jnp.int32, (TOK, cols_all), 1), wrap(col_start + col_b, cols_all)),
            classes,
        )

        def region(place, level, row, values, axis):
            at = ((2 * i + level + one) & 3) * rows_all + wrap(row_start + row, rows_all)
            value = jnp.sum(jnp.where(place == at, values, 0.0), axis=axis, keepdims=True)
            flags = 2 * (2 * i + level >= 3).astype(jnp.int32)
            flags = flags + (lats[i] * 6 + row >= rows_all - 3).astype(jnp.int32)
            return 4.0 * value + (one * flags).astype(jnp.float32)

        region_a = region(place_a, level_a, row_a, across, 0)
        region_b = region(place_b, level_b, row_b, down, 1)
        same = region_b == region_a
        for g in range(3):
            heads = [turned_ref[i * HEADS + g * 4 + t] for t in range(4)]
            stack = jnp.concatenate([h[0:128] for h in heads] + [h[128:144] for h in heads], axis=0)
            spread = dot_nt(identity, stack.astype(jnp.bfloat16)) * LOG2E
            for t in range(5):
                lanes = slice(t * 128, min(t * 128 + 128, GUSED))
                part = same[:, 0:128] if t < 4 else same[:, 128:192]
                to = slice(g * GROUP + lanes.start, g * GROUP + lanes.stop)
                bias_ref[i, :, to] = jnp.where(part, spread[:, lanes], -1e30)
            bias_ref[i, :, g * GROUP + GUSED : (g + 1) * GROUP] = jnp.full((TOK, GROUP - GUSED), -1e30, jnp.float32)


def attention(query, key, value, bias_ref, i):
    head = lax.broadcasted_iota(jnp.int32, (1, 128), 1) >> 5
    keep = [(head == t).astype(jnp.float32).astype(jnp.bfloat16) for t in range(4)]
    segment = lax.broadcasted_iota(jnp.int32, (1, 128), 1) >> 4
    blank = jnp.zeros((64, 128), jnp.bfloat16)
    blank_wide = jnp.zeros((64, 256), jnp.bfloat16)
    mixed = []
    for g in range(3):
        lanes = slice(g * 128, g * 128 + 128)
        q, k, v = query[:, lanes], key[:, lanes], value[:, lanes]
        wide = jnp.concatenate([k[0:128] * m for m in keep] + [k[128:144] * m for m in keep] + [blank], axis=0)
        scores = dot_nt(q, wide) + bias_ref[i, :, g * GROUP : (g + 1) * GROUP]
        tail = scores[:, 512:640]
        top, weights = [], []
        for t in range(4):
            main = scores[:, t * 128 : t * 128 + 128]
            joined = jnp.maximum(main, jnp.where(segment == t, tail, -1e30))
            top.append(jnp.max(joined, axis=1, keepdims=True))
            weights.append(jnp.exp2(main - top[t]).astype(jnp.bfloat16))
        tops = jnp.where(segment < 2, jnp.where(segment == 0, top[0], top[1]), jnp.where(segment == 2, top[2], top[3]))
        weights.append(jnp.exp2(tail - tops).astype(jnp.bfloat16))
        weights = jnp.concatenate(weights, axis=1)
        pairs = [jnp.concatenate([v[0:128] * m, jnp.broadcast_to(m, (128, 128))], axis=1) for m in keep]
        pairs += [jnp.concatenate([v[128:144] * m, jnp.broadcast_to(m, (16, 128))], axis=1) for m in keep]
        out = dot(weights, jnp.concatenate(pairs + [blank_wide], axis=0))
        mixed.append((out[:, 0:128] / out[:, 128:256]).astype(jnp.bfloat16))
    return jnp.concatenate(mixed, axis=1)


def block(x, gains_ref, joint_ref, out_ref, expand_ref, reduce_ref, bias_ref):
    gains = gains_ref[...].astype(jnp.float32)
    normed = layer_norm(x, gains[0:1]).astype(jnp.bfloat16)
    projected = dot(normed, joint_ref[...])
    query = (projected[:, 0:WIDTH] * (LOG2E * 32**-0.5)).astype(jnp.bfloat16)
    key = projected[:, WIDTH : 2 * WIDTH].astype(jnp.bfloat16)
    value = projected[:, 2 * WIDTH :].astype(jnp.bfloat16)
    mixed = []
    for i in range(2):
        rows = slice(i * TOK, i * TOK + TOK)
        mixed.append(attention(query[rows], key[rows], value[rows], bias_ref, i))
    hidden = x + dot(jnp.concatenate(mixed, axis=0), out_ref[...])
    again = layer_norm(hidden, gains[1:2]).astype(jnp.bfloat16)
    total = hidden
    step = 512
    for start in range(0, FF, step):
        act = gelu(dot(again, expand_ref[:, start : start + step])).astype(jnp.bfloat16)
        total = total + dot(act, reduce_ref[start : start + step, :])
    return total.astype(jnp.bfloat16)


def kernel(
    lat_count,
    lon_count,
    fields_hbm,
    class_hbm,
    gains_hbm,
    joint_hbm,
    oproj_hbm,
    expand_hbm,
    reduce_hbm,
    table_hbm,
    result_ref,
    fields_ref,
    class_ref,
    gains_ref,
    joint_ref,
    oproj_ref,
    expand_ref,
    reduce_ref,
    table_ref,
    into_ref,
    scatter_ref,
    last_ref,
    rows_ref,
    turned_ref,
    bias_ref,
    halo_ref,
    take_ref,
    done_ref,
    home_ref,
    load_sem,
    halo_send,
    take_recv,
    home_send,
    home_recv,
    next_send,
):
    sec = lax.axis_index("section")
    lat = lax.axis_index("lat")
    lon = lax.axis_index("lon")
    first = sec == 0
    lat_up = lax.rem(lat + 1, lat_count)
    lat_down = lax.rem(lat + lat_count - 1, lat_count)
    lon_up = lax.rem(lon + 1, lon_count)
    lon_down = lax.rem(lon + lon_count - 1, lon_count)
    own = (0, 7)
    others = (3, 4, 2, 5, 1, 6)

    def owner(piece, sign):
        row_half, col_half, window = piece & 1, (piece >> 1) & 1, piece >> 2
        up, right = sign * (row_half - window), sign * (col_half - window)
        where_lat = {0: lat, 1: lat_up, -1: lat_down}[up]
        where_lon = {0: lon, 1: lon_up, -1: lon_down}[right]
        return (where_lat, where_lon)

    barrier = pltpu.get_barrier_semaphore()

    @pl.when(first)
    def _():
        for piece in others:
            pl.semaphore_signal(barrier, inc=1, device_id=(0,) + owner(piece, 1), device_id_type=MESH)

    @pl.when(jnp.logical_not(first))
    def _():
        for piece in others + own[:1]:
            pl.semaphore_signal(barrier, inc=1, device_id=(0,) + owner(piece, 1), device_id_type=MESH)

    loads = []

    def load(src, dst):
        copy = pltpu.make_async_copy(src, dst, load_sem.at[len(loads)])
        copy.start()
        loads.append(copy)
        return copy

    load_fields = load(fields_hbm, fields_ref)
    prep = [load(table_hbm.at[0], table_ref), load(class_hbm, class_ref)]
    rest = [
        load(gains_hbm.at[0], gains_ref),
        load(joint_hbm.at[0], joint_ref),
        load(oproj_hbm.at[0], oproj_ref),
        load(expand_hbm.at[0], expand_ref),
        load(reduce_hbm.at[0], reduce_ref),
    ]

    def halo_copy(m, q):
        return pltpu.make_async_remote_copy(
            src_ref=halo_ref.at[m, q],
            dst_ref=take_ref.at[m, q],
            send_sem=halo_send.at[m, q],
            recv_sem=take_recv.at[m, q],
            device_id=(0,) + owner(q, -1),
            device_id_type=MESH,
        )

    def home_copy(m, q):
        return pltpu.make_async_remote_copy(
            src_ref=done_ref.at[m, q],
            dst_ref=home_ref.at[m, q],
            send_sem=home_send.at[m, q],
            recv_sem=home_recv.at[m, q],
            device_id=(0,) + owner(q, 1),
            device_id_type=MESH,
        )

    def next_copy(m, q):
        return pltpu.make_async_remote_copy(
            src_ref=done_ref.at[m, q],
            dst_ref=take_ref.at[m, q],
            send_sem=next_send.at[m, q],
            recv_sem=take_recv.at[m, q],
            device_id=(1,) + owner(q, 1),
            device_id_type=MESH,
        )

    load_fields.wait()

    @pl.when(first)
    def _():
        gather = gather_matrix()
        for m in range(MICRO):
            rows = dot(gather, fields_ref[m].reshape(GRID_ROWS, WIDTH))
            pack(rows, [[take_ref] if q in own else [halo_ref] for q in range(PIECES)], m)
            if m == 0:
                pl.semaphore_wait(barrier, 13)
            for q in others:
                halo_copy(m, q).start()

    into_ref[...] = into_matrix(jnp.where(first, 1, 0))

    @pl.when(first)
    def _():
        scatter_ref[...] = scatter_matrix()
        last_ref[...] = back_matrix()

    @pl.when(jnp.logical_not(first))
    def _():
        last_ref[:, 0 : 2 * TOK] = plain_matrix()

    for copy in prep:
        copy.wait()
    prepare_bias(first, lat, lon, lat_count, lon_count, class_ref, table_ref, rows_ref, turned_ref, bias_ref)
    for copy in rest:
        copy.wait()

    def step(m, carry):
        @pl.when(first)
        def _():
            for q in others:
                halo_copy(m, q).wait_recv()

        @pl.when(jnp.logical_not(first))
        def _():
            for q in range(PIECES):
                next_copy(m, q).wait_recv()

        x = dot(into_ref[...], unpack(take_ref, m))
        y = block(x, gains_ref, joint_ref, oproj_ref, expand_ref, reduce_ref, bias_ref)

        @pl.when(first)
        def _():
            pack(
                dot(scatter_ref[...], y),
                [[done_ref, home_ref] if q in own else [done_ref] for q in range(PIECES)],
                m,
            )
            for q in others + own:
                next_copy(m, q).start()
            for q in others:
                home_copy(m, q).start()

        @pl.when(jnp.logical_not(first))
        def _():
            write(m, dot(last_ref[:, 0 : 2 * TOK], y).astype(jnp.bfloat16))

        return carry

    def write(m, rows):
        result_ref[m] = rows.reshape(WIN_H, WIN_W, LEVELS, WIDTH)

    lax.fori_loop(0, MICRO, step, 0)

    @pl.when(first)
    def _():
        for m in range(MICRO):
            for q in others:
                home_copy(m, q).wait_recv()
            write(m, dot(last_ref[...], unpack(home_ref, m)).astype(jnp.bfloat16))
        for m in range(MICRO):
            for q in others:
                halo_copy(m, q).wait_send()
                home_copy(m, q).wait_send()
            for q in range(PIECES):
                next_copy(m, q).wait_send()


def body(
    fields, surface_class, norm_gains, joint_proj, out_proj, expand_proj, reduce_proj, earth_bias
):
    lat_count = lax.axis_size("lat")
    lon_count = lax.axis_size("lon")
    fields = jnp.transpose(fields, (0, 2, 3, 1, 4))
    operands = (
        fields, surface_class, norm_gains, joint_proj, out_proj, expand_proj, reduce_proj,
        jnp.transpose(earth_bias, (0, 2, 1, 3)),
    )
    bf16 = jnp.bfloat16
    scratch = [
        pltpu.VMEM(fields.shape, bf16),
        pltpu.VMEM(surface_class.shape, jnp.int32),
        pltpu.VMEM((2, WIDTH), bf16),
        pltpu.VMEM((WIDTH, 3 * WIDTH), bf16),
        pltpu.VMEM((WIDTH, WIDTH), bf16),
        pltpu.VMEM((WIDTH, FF), bf16),
        pltpu.VMEM((FF, WIDTH), bf16),
        pltpu.VMEM((HEADS,) + earth_bias.shape[1:2] + earth_bias.shape[3:], bf16),
        pltpu.VMEM((2 * TOK, PACKED), bf16),
        pltpu.VMEM((PACKED, 2 * TOK), bf16),
        pltpu.VMEM((GRID_ROWS, PACKED), bf16),
        pltpu.VMEM((2, 12, 16, KDIM), bf16),
        pltpu.VMEM((2 * HEADS, TOK, 256), jnp.float32),
        pltpu.VMEM((2, TOK, 3 * GROUP), jnp.float32),
        pltpu.VMEM((MICRO, PIECES, PROWS, 128), bf16),
        pltpu.VMEM((MICRO, PIECES, PROWS, 128), bf16),
        pltpu.VMEM((MICRO, PIECES, PROWS, 128), bf16),
        pltpu.VMEM((MICRO, PIECES, PROWS, 128), bf16),
        pltpu.SemaphoreType.DMA((14,)),
        pltpu.SemaphoreType.DMA((MICRO, PIECES)),
        pltpu.SemaphoreType.DMA((MICRO, PIECES)),
        pltpu.SemaphoreType.DMA((MICRO, PIECES)),
        pltpu.SemaphoreType.DMA((MICRO, PIECES)),
        pltpu.SemaphoreType.DMA((MICRO, PIECES)),
    ]
    result = pl.pallas_call(
        functools.partial(kernel, lat_count, lon_count),
        out_shape=pltpu.VMEM(fields.shape, bf16),
        in_specs=[pl.BlockSpec(memory_space=pltpu.HBM)] * len(operands),
        out_specs=pl.BlockSpec(memory_space=pltpu.VMEM),
        scratch_shapes=scratch,
        compiler_params=pltpu.CompilerParams(
            collective_id=0, has_side_effects=True, vmem_limit_bytes=56 * 1024 * 1024
        ),
        name="two_blocks",
    )(*operands)
    return jnp.transpose(result, (0, 3, 1, 2, 4))[None]


def solution(mesh):
    return jax.shard_map(
        body,
        mesh=mesh,
        in_specs=(
            P(None, None, "lat", "lon", None),
            P(),
            P("section", None, None),
            P("section", None, None),
            P("section", None, None),
            P("section", None, None),
            P("section", None, None),
            P("section", None, None, None),
        ),
        out_specs=P("section", None, None, "lat", "lon", None),
        check_vma=False,
    )
```

```python
import functools

import jax
import jax.numpy as jnp
from jax import lax
from jax.experimental import pallas as pl
from jax.experimental.pallas import tpu as pltpu
from jax.sharding import PartitionSpec as P

WIN_P = 2
WIN_H = 6
WIN_W = 12
TOK = WIN_P * WIN_H * WIN_W
LEVELS = 4
MICRO = 2
WIDTH = 384
HEADS = 12
FF = 1536
PIECES = 8
PROWS = 112
PACKED = 192
GRID_ROWS = LEVELS * WIN_H * WIN_W
GROUP = 640
GUSED = 576
KDIM = 288
LOG2E = 1.4426950408889634
MESH = pl.DeviceIdType.MESH


def divide(value, by):
    return (value * (-(-65536 // by))) >> 16


def token_parts(token):
    col = divide(token, 12)
    rest = token - col * 12
    level = (rest >= 6).astype(jnp.int32)
    return col, level, rest - level * 6


def packed_row(window, row_half, col_half, level, row, col):
    quarter = row_half + 2 * col_half
    inner = level * 18 + row * 6 + col
    return window * PACKED + jnp.where(inner < 32, quarter * 32 + inner, 96 + quarter * 16 + inner)


def halves(position, extent):
    half = (position >= extent).astype(jnp.int32)
    return half, position - half * extent


def one_hot(rows, target):
    at = lax.broadcasted_iota(jnp.int32, (rows, target.shape[1]), 0)
    return (at == target).astype(jnp.float32).astype(jnp.bfloat16)


def grid_place(row, col, level):
    return (row * 12 + col) * 4 + level


def pack_matrix(rows, target):
    row = lax.broadcasted_iota(jnp.int32, (rows, 1), 0)
    last = jnp.where((row & 12) == 12, -1, row - (row & 12))
    row = jnp.where(halves(row, PACKED)[1] < 128, row, last)
    return (row == target).astype(jnp.float32).astype(jnp.bfloat16)


def gather_matrix():
    place = lax.broadcasted_iota(jnp.int32, (1, GRID_ROWS), 1)
    pair = place >> 2
    row = divide(pair, 12)
    row_half, row_in = halves(row, 3)
    col_half, col_in = halves(pair - row * 12, 6)
    level = ((place & 3) + 3) & 3
    target = packed_row(level >> 1, 1 - row_half, 1 - col_half, level & 1, row_in, col_in)
    return pack_matrix(2 * PACKED, target)


def scatter_matrix():
    col, level, row = token_parts(lax.broadcasted_iota(jnp.int32, (1, TOK), 1))
    row_half, row_in = halves(row, 3)
    col_half, col_in = halves(col, 6)
    return pack_matrix(PACKED, packed_row(0, row_half, col_half, level, row_in, col_in))


def packed_parts(rows):
    place = lax.broadcasted_iota(jnp.int32, (1, rows), 1)
    window, place = halves(place, PACKED)
    early = place < 128
    quarter = jnp.where(early, place >> 5, (place - 128) >> 4)
    inner = jnp.where(early, place & 31, 32 + (place & 3))
    used = early | ((place & 12) != 12)
    level, rest = halves(inner, 18)
    row = divide(rest, 6)
    return used, quarter & 1, quarter >> 1, 2 * window + level, row, rest - row * 6


def shifted_matrix():
    used, row_half, col_half, level, row, col = packed_parts(PACKED)
    token = (col + 6 * col_half) * 12 + level * 6 + row + 3 * row_half
    return one_hot(TOK, jnp.where(used, token, -1))


def owned_parts():
    used, row_half, col_half, level, row, col = packed_parts(2 * PACKED)
    return used, (level + 1) & 3, row + 3 * (1 - row_half), col + 6 * (1 - col_half)


def owned_matrix():
    used, level, row, col = owned_parts()
    token = (level >> 1) * TOK + col * 12 + (level & 1) * 6 + row
    return one_hot(2 * TOK, jnp.where(used, token, -1))


def back_matrix():
    used, level, row, col = owned_parts()
    return one_hot(GRID_ROWS, jnp.where(used, grid_place(row, col, level), -1))


def plain_matrix():
    token = lax.broadcasted_iota(jnp.int32, (1, 2 * TOK), 1)
    window, rest = halves(token, TOK)
    col, level, row = token_parts(rest)
    return one_hot(GRID_ROWS, grid_place(row, col, 2 * window + level))


def pack(rows, refs, m, window):
    rows = rows.astype(jnp.bfloat16)
    chunk = (lax.broadcasted_iota(jnp.int32, (64, 1), 0) >> 2) & 3
    last = rows[128:].astype(jnp.float32)
    last = jnp.where(chunk == 0, last[:, 0:128], jnp.where(chunk == 1, last[:, 128:256], last[:, 256:384]))
    last = last.astype(jnp.bfloat16)
    for quarter in range(4):
        piece = window * 4 + quarter
        for ref in refs[piece]:
            for c in range(3):
                ref[m, piece, c * 32 : c * 32 + 32, :] = rows[quarter * 32 : quarter * 32 + 32, c * 128 : c * 128 + 128]
            ref[m, piece, 96:112, :] = last[quarter * 16 : quarter * 16 + 16]


def unpack(ref, m, window):
    chunk = (lax.broadcasted_iota(jnp.int32, (64, 1), 0) >> 2) & 3
    pieces = range(window * 4, window * 4 + 4)
    rows = [
        jnp.concatenate([ref[m, piece, c * 32 : c * 32 + 32, :] for c in range(3)], axis=1)
        for piece in pieces
    ]
    last = jnp.concatenate([ref[m, piece, 96:112, :] for piece in pieces], axis=0).astype(jnp.float32)
    last = jnp.concatenate([jnp.where(chunk == c, last, 0.0) for c in range(3)], axis=1)
    return jnp.concatenate(rows + [last.astype(jnp.bfloat16)], axis=0)


def unpack_both(ref, m):
    return jnp.concatenate([unpack(ref, m, window) for window in range(2)], axis=0)


def dot(a, b):
    return jnp.dot(a, b, preferred_element_type=jnp.float32)


def dot_nt(a, b):
    return lax.dot_general(a, b, (((1,), (1,)), ((), ())), preferred_element_type=jnp.float32)


def layer_norm(values, gain):
    average = jnp.mean(values, axis=-1, keepdims=True)
    centred = values - average
    spread = jnp.mean(centred * centred, axis=-1, keepdims=True)
    return centred * lax.rsqrt(spread + 1e-05) * gain


def gelu(x):
    return x * (0.5 + 0.5 * lax.erf(x * 0.7071067811865476))


def lane_tokens():
    lane = lax.broadcasted_iota(jnp.int32, (1, 256), 1)
    return jnp.where(lane < 128, lane, 128 + (lane & 15))


def prepare_bias(first, lat, lon, lat_count, lon_count, class_ref, table_ref, rows_ref, turned_ref, bias_ref):
    kinds = 2 * lat_count
    one = jnp.where(first, 1, 0)
    lats = (lat, lax.rem(lat + lat_count - one, lat_count))
    lons = (lon, lax.rem(lon + lon_count - one, lon_count))
    to_row = lax.broadcasted_iota(jnp.int32, (32, HEADS * kinds), 0)
    to_col = lax.broadcasted_iota(jnp.int32, (32, HEADS * kinds), 1)
    kind = jnp.where(to_row < 16, lat, lat_count + lats[1])
    wanted = (to_row & 15) * kinds + kind
    own = (to_col == wanted).astype(jnp.float32).astype(jnp.bfloat16)
    table = dot(own, table_ref[...].reshape(HEADS * kinds, -1)).astype(jnp.bfloat16)
    rows_ref[...] = jnp.zeros_like(rows_ref)
    for i in range(2):
        for j in range(12):
            pb, rb = j // 6, j % 6
            for pa in range(2):
                begin = pb * 1656 + pa * 828 + rb * 138
                rows_ref[i, j, :, pa * 144 : pa * 144 + 138] = table[
                    i * 16 : i * 16 + 16, begin : begin + 138
                ]
    to_row = lax.broadcasted_iota(jnp.int32, (192, 192), 0)
    to_col = lax.broadcasted_iota(jnp.int32, (192, 192), 1)
    swap = (((to_row & 15) << 4) + (to_row >> 4) == to_col).astype(jnp.float32).astype(jnp.bfloat16)
    by_head = [
        dot(swap, rows_ref[i].reshape(192, KDIM)).astype(jnp.bfloat16) for i in range(2)
    ]
    by_head = jnp.concatenate(by_head, axis=0)
    col_a, level_a, row_a = token_parts(lane_tokens())
    base = level_a * 144 + row_a * 23 + col_a + 11
    depth = lax.broadcasted_iota(jnp.int32, (KDIM, 256), 0)
    for cb in range(12):
        pick = (depth == base - cb).astype(jnp.float32).astype(jnp.bfloat16)
        spread = dot(by_head, pick)
        for i in range(2):
            for h in range(HEADS):
                start = i * 192 + h * 16
                turned_ref[i * HEADS + h, cb * 12 : cb * 12 + 12, :] = spread[start : start + 12]
    rows_all = 6 * lat_count
    cols_all = 12 * lon_count
    classes = class_ref[...].reshape(LEVELS * rows_all, cols_all).astype(jnp.float32).astype(jnp.bfloat16)
    col_b, level_b, row_b = token_parts(lax.broadcasted_iota(jnp.int32, (TOK, 1), 0))

    def wrap(v, extent):
        return jnp.where(v >= extent, v - extent, v)

    def onehot(a, b):
        return (a == b).astype(jnp.float32).astype(jnp.bfloat16)

    identity = (
        lax.broadcasted_iota(jnp.int32, (TOK, 256), 0) == lax.broadcasted_iota(jnp.int32, (TOK, 256), 1)
    )
    identity = identity.astype(jnp.float32).astype(jnp.bfloat16)
    place_a = lax.broadcasted_iota(jnp.int32, (LEVELS * rows_all, 256), 0)
    place_b = lax.broadcasted_iota(jnp.int32, (TOK, LEVELS * rows_all), 1)
    for i in range(2):
        row_start = lats[i] * 6 + 3 * one
        col_start = lons[i] * 12 + 6 * one
        across = dot(
            classes,
            onehot(lax.broadcasted_iota(jnp.int32, (cols_all, 256), 0), wrap(col_start + col_a, cols_all)),
        )
        down = dot_nt(
            onehot(lax.broadcasted_iota(jnp.int32, (TOK, cols_all), 1), wrap(col_start + col_b, cols_all)),
            classes,
        )

        def region(place, level, row, values, axis):
            at = ((2 * i + level + one) & 3) * rows_all + wrap(row_start + row, rows_all)
            value = jnp.sum(jnp.where(place == at, values, 0.0), axis=axis, keepdims=True)
            flags = 2 * (2 * i + level >= 3).astype(jnp.int32)
            flags = flags + (lats[i] * 6 + row >= rows_all - 3).astype(jnp.int32)
            return 4.0 * value + (one * flags).astype(jnp.float32)

        region_a = region(place_a, level_a, row_a, across, 0)
        region_b = region(place_b, level_b, row_b, down, 1)
        same = region_b == region_a
        for g in range(3):
            heads = [turned_ref[i * HEADS + g * 4 + t] for t in range(4)]
            stack = jnp.concatenate([h[0:128] for h in heads] + [h[128:144] for h in heads], axis=0)
            spread = dot_nt(identity, stack.astype(jnp.bfloat16)) * LOG2E
            for t in range(5):
                lanes = slice(t * 128, min(t * 128 + 128, GUSED))
                part = same[:, 0:128] if t < 4 else same[:, 128:192]
                to = slice(g * GROUP + lanes.start, g * GROUP + lanes.stop)
                bias_ref[i, :, to] = jnp.where(part, spread[:, lanes], -1e30)
            bias_ref[i, :, g * GROUP + GUSED : (g + 1) * GROUP] = jnp.full((TOK, GROUP - GUSED), -1e30, jnp.float32)


def attention(query, key, value, bias_ref, i):
    head = lax.broadcasted_iota(jnp.int32, (1, 128), 1) >> 5
    keep = [(head == t).astype(jnp.float32).astype(jnp.bfloat16) for t in range(4)]
    segment = lax.broadcasted_iota(jnp.int32, (1, 128), 1) >> 4
    blank = jnp.zeros((64, 128), jnp.bfloat16)
    blank_wide = jnp.zeros((64, 256), jnp.bfloat16)
    mixed = []
    for g in range(3):
        lanes = slice(g * 128, g * 128 + 128)
        q, k, v = query[:, lanes], key[:, lanes], value[:, lanes]
        wide = jnp.concatenate([k[0:128] * m for m in keep] + [k[128:144] * m for m in keep] + [blank], axis=0)
        scores = dot_nt(q, wide) + bias_ref[i, :, g * GROUP : (g + 1) * GROUP]
        tail = scores[:, 512:640]
        top, weights = [], []
        for t in range(4):
            main = scores[:, t * 128 : t * 128 + 128]
            joined = jnp.maximum(main, jnp.where(segment == t, tail, -1e30))
            top.append(jnp.max(joined, axis=1, keepdims=True))
            weights.append(jnp.exp2(main - top[t]).astype(jnp.bfloat16))
        tops = jnp.where(segment < 2, jnp.where(segment == 0, top[0], top[1]), jnp.where(segment == 2, top[2], top[3]))
        weights.append(jnp.exp2(tail - tops).astype(jnp.bfloat16))
        weights = jnp.concatenate(weights, axis=1)
        pairs = [jnp.concatenate([v[0:128] * m, jnp.broadcast_to(m, (128, 128))], axis=1) for m in keep]
        pairs += [jnp.concatenate([v[128:144] * m, jnp.broadcast_to(m, (16, 128))], axis=1) for m in keep]
        out = dot(weights, jnp.concatenate(pairs + [blank_wide], axis=0))
        mixed.append((out[:, 0:128] / out[:, 128:256]).astype(jnp.bfloat16))
    return jnp.concatenate(mixed, axis=1)


def block(x, gains_ref, joint_ref, out_ref, expand_ref, reduce_ref, bias_ref):
    gains = gains_ref[...].astype(jnp.float32)
    normed = layer_norm(x, gains[0:1]).astype(jnp.bfloat16)
    projected = dot(normed, joint_ref[...])
    query = (projected[:, 0:WIDTH] * (LOG2E * 32**-0.5)).astype(jnp.bfloat16)
    key = projected[:, WIDTH : 2 * WIDTH].astype(jnp.bfloat16)
    value = projected[:, 2 * WIDTH :].astype(jnp.bfloat16)
    mixed = []
    for i in range(2):
        rows = slice(i * TOK, i * TOK + TOK)
        mixed.append(attention(query[rows], key[rows], value[rows], bias_ref, i))
    hidden = x + dot(jnp.concatenate(mixed, axis=0), out_ref[...])
    again = layer_norm(hidden, gains[1:2]).astype(jnp.bfloat16)
    total = hidden
    step = 512
    for start in range(0, FF, step):
        act = gelu(dot(again, expand_ref[:, start : start + step])).astype(jnp.bfloat16)
        total = total + dot(act, reduce_ref[start : start + step, :])
    return total.astype(jnp.bfloat16)


def kernel(
    lat_count,
    lon_count,
    fields_hbm,
    class_hbm,
    gains_hbm,
    joint_hbm,
    oproj_hbm,
    expand_hbm,
    reduce_hbm,
    table_hbm,
    result_ref,
    fields_ref,
    class_ref,
    gains_ref,
    joint_ref,
    oproj_ref,
    expand_ref,
    reduce_ref,
    table_ref,
    into_ref,
    scatter_ref,
    last_ref,
    x_ref,
    y_ref,
    rows_ref,
    turned_ref,
    bias_ref,
    halo_ref,
    take_ref,
    done_ref,
    home_ref,
    load_sem,
    halo_send,
    take_recv,
    home_send,
    home_recv,
    next_send,
    hand_send,
):
    sec = lax.axis_index("section")
    lat = lax.axis_index("lat")
    lon = lax.axis_index("lon")
    first = sec == 0
    lat_up = lax.rem(lat + 1, lat_count)
    lat_down = lax.rem(lat + lat_count - 1, lat_count)
    lon_up = lax.rem(lon + 1, lon_count)
    lon_down = lax.rem(lon + lon_count - 1, lon_count)
    own = (0, 7)
    others = (3, 4, 2, 5, 1, 6)

    def owner(piece, sign):
        row_half, col_half, window = piece & 1, (piece >> 1) & 1, piece >> 2
        up, right = sign * (row_half - window), sign * (col_half - window)
        where_lat = {0: lat, 1: lat_up, -1: lat_down}[up]
        where_lon = {0: lon, 1: lon_up, -1: lon_down}[right]
        return (where_lat, where_lon)

    barrier = pltpu.get_barrier_semaphore()

    @pl.when(first)
    def _():
        for piece in others:
            pl.semaphore_signal(barrier, inc=1, device_id=(0,) + owner(piece, 1), device_id_type=MESH)
        pl.semaphore_signal(barrier, inc=1, device_id=(1, lat, lon), device_id_type=MESH)

    @pl.when(jnp.logical_not(first))
    def _():
        for piece in others + own[:1]:
            pl.semaphore_signal(barrier, inc=1, device_id=(0,) + owner(piece, 1), device_id_type=MESH)

    loads = []

    def load(src, dst):
        copy = pltpu.make_async_copy(src, dst, load_sem.at[len(loads)])
        copy.start()
        loads.append(copy)
        return copy

    load_fields = load(fields_hbm, fields_ref)
    prep = [load(table_hbm.at[0], table_ref), load(class_hbm, class_ref)]
    rest = [
        load(gains_hbm.at[0], gains_ref),
        load(joint_hbm.at[0], joint_ref),
        load(oproj_hbm.at[0], oproj_ref),
        load(expand_hbm.at[0], expand_ref),
        load(reduce_hbm.at[0], reduce_ref),
    ]

    def halo_copy(m, q):
        return pltpu.make_async_remote_copy(
            src_ref=halo_ref.at[m, q],
            dst_ref=take_ref.at[m, q],
            send_sem=halo_send.at[m, q],
            recv_sem=take_recv.at[m, q],
            device_id=(0,) + owner(q, -1),
            device_id_type=MESH,
        )

    def home_copy(m, q):
        return pltpu.make_async_remote_copy(
            src_ref=done_ref.at[m, q],
            dst_ref=home_ref.at[m, q],
            send_sem=home_send.at[m, q],
            recv_sem=home_recv.at[m, q],
            device_id=(0,) + owner(q, 1),
            device_id_type=MESH,
        )

    odd = lax.rem(lat, 2)
    lat_chip = lat + 1 - 2 * odd
    lon_chip = (lax.rem(lon + lon_count - odd, lon_count), lax.rem(lon + 1 - odd, lon_count))

    def chip_copy(m, col_half):
        piece = 1 + 3 * odd + 2 * col_half
        return pltpu.make_async_remote_copy(
            src_ref=done_ref.at[m, piece],
            dst_ref=home_ref.at[m, piece],
            send_sem=home_send.at[m, piece],
            recv_sem=home_recv.at[m, piece],
            device_id=(0, lat_chip, lon_chip[col_half]),
            device_id_type=MESH,
        )

    def hand_copy(m, col_half):
        piece = 1 + 3 * odd + 2 * col_half
        return pltpu.make_async_remote_copy(
            src_ref=take_ref.at[m, piece],
            dst_ref=home_ref.at[m, piece],
            send_sem=hand_send.at[m, col_half],
            recv_sem=home_recv.at[m, piece],
            device_id=(0, lat, lon),
            device_id_type=MESH,
        )

    def next_copy(m, q):
        return pltpu.make_async_remote_copy(
            src_ref=done_ref.at[m, q],
            dst_ref=take_ref.at[m, q],
            send_sem=next_send.at[m, q],
            recv_sem=take_recv.at[m, q],
            device_id=(1,) + owner(q, 1),
            device_id_type=MESH,
        )

    load_fields.wait()

    @pl.when(first)
    def _():
        gather = gather_matrix()
        for m in range(MICRO):
            rows = dot(gather, fields_ref[m].reshape(GRID_ROWS, WIDTH))
            refs = [[take_ref] if q in own else [halo_ref] for q in range(PIECES)]
            for window in range(2):
                pack(rows[window * PACKED : (window + 1) * PACKED], refs, m, window)
            if m == 0:
                pl.semaphore_wait(barrier, 13)
            for q in others:
                halo_copy(m, q).start()

    @pl.when(first)
    def _():
        into_ref[0:TOK, 0:PACKED] = shifted_matrix()
        scatter_ref[...] = scatter_matrix()
        last_ref[...] = back_matrix()

    @pl.when(jnp.logical_not(first))
    def _():
        into_ref[...] = owned_matrix()
        last_ref[:, 0 : 2 * TOK] = plain_matrix()
        pl.semaphore_wait(barrier, 1)

    for copy in prep:
        copy.wait()
    prepare_bias(first, lat, lon, lat_count, lon_count, class_ref, table_ref, rows_ref, turned_ref, bias_ref)
    for copy in rest:
        copy.wait()

    def step(m, carry):
        @pl.when(first)
        def _():
            for q in others:
                halo_copy(m, q).wait_recv()
            for window in range(2):
                rows = dot(into_ref[0:TOK, 0:PACKED], unpack(take_ref, m, window))
                x_ref[window * TOK : (window + 1) * TOK, :] = rows.astype(jnp.bfloat16)

        @pl.when(jnp.logical_not(first))
        def _():
            for q in range(PIECES):
                next_copy(m, q).wait_recv()
            for col_half in range(2):
                hand_copy(m, col_half).start()
            x_ref[...] = dot(into_ref[...], unpack_both(take_ref, m)).astype(jnp.bfloat16)

        x = x_ref[...].astype(jnp.float32)
        y_ref[...] = block(x, gains_ref, joint_ref, oproj_ref, expand_ref, reduce_ref, bias_ref)

        @pl.when(first)
        def _():
            refs = [[done_ref, home_ref] if q in own else [done_ref] for q in range(PIECES)]
            for window in range(2):
                y = y_ref[window * TOK : (window + 1) * TOK, :]
                pack(dot(scatter_ref[...], y), refs, m, window)
            for q in others + own:
                next_copy(m, q).start()
            for q in (2, 5):
                home_copy(m, q).start()
            for col_half in range(2):
                chip_copy(m, col_half).start()

        @pl.when(jnp.logical_not(first))
        def _():
            write(m, dot(last_ref[:, 0 : 2 * TOK], y_ref[...]).astype(jnp.bfloat16))

        return carry

    def write(m, rows):
        result_ref[m] = rows.reshape(WIN_H, WIN_W, LEVELS, WIDTH)

    lax.fori_loop(0, MICRO, step, 0)

    @pl.when(first)
    def _():
        for m in range(MICRO):
            for q in others:
                home_copy(m, q).wait_recv()
            write(m, dot(last_ref[...], unpack_both(home_ref, m)).astype(jnp.bfloat16))
        for m in range(MICRO):
            for q in others:
                halo_copy(m, q).wait_send()
            for q in (2, 5):
                home_copy(m, q).wait_send()
            for col_half in range(2):
                chip_copy(m, col_half).wait_send()
            for q in range(PIECES):
                next_copy(m, q).wait_send()

    @pl.when(jnp.logical_not(first))
    def _():
        for m in range(MICRO):
            for col_half in range(2):
                hand_copy(m, col_half).wait_send()


def body(
    fields, surface_class, norm_gains, joint_proj, out_proj, expand_proj, reduce_proj, earth_bias
):
    lat_count = lax.axis_size("lat")
    lon_count = lax.axis_size("lon")
    fields = jnp.transpose(fields, (0, 2, 3, 1, 4))
    operands = (
        fields, surface_class, norm_gains, joint_proj, out_proj, expand_proj, reduce_proj,
        jnp.transpose(earth_bias, (0, 2, 1, 3)),
    )
    bf16 = jnp.bfloat16
    scratch = [
        pltpu.VMEM(fields.shape, bf16),
        pltpu.VMEM(surface_class.shape, jnp.int32),
        pltpu.VMEM((2, WIDTH), bf16),
        pltpu.VMEM((WIDTH, 3 * WIDTH), bf16),
        pltpu.VMEM((WIDTH, WIDTH), bf16),
        pltpu.VMEM((WIDTH, FF), bf16),
        pltpu.VMEM((FF, WIDTH), bf16),
        pltpu.VMEM((HEADS,) + earth_bias.shape[1:2] + earth_bias.shape[3:], bf16),
        pltpu.VMEM((2 * TOK, 2 * PACKED), bf16),
        pltpu.VMEM((PACKED, TOK), bf16),
        pltpu.VMEM((GRID_ROWS, 2 * PACKED), bf16),
        pltpu.VMEM((2 * TOK, WIDTH), bf16),
        pltpu.VMEM((2 * TOK, WIDTH), bf16),
        pltpu.VMEM((2, 12, 16, KDIM), bf16),
        pltpu.VMEM((2 * HEADS, TOK, 256), jnp.float32),
        pltpu.VMEM((2, TOK, 3 * GROUP), jnp.float32),
        pltpu.VMEM((MICRO, PIECES, PROWS, 128), bf16),
        pltpu.VMEM((MICRO, PIECES, PROWS, 128), bf16),
        pltpu.VMEM((MICRO, PIECES, PROWS, 128), bf16),
        pltpu.VMEM((MICRO, PIECES, PROWS, 128), bf16),
        pltpu.SemaphoreType.DMA((14,)),
        pltpu.SemaphoreType.DMA((MICRO, PIECES)),
        pltpu.SemaphoreType.DMA((MICRO, PIECES)),
        pltpu.SemaphoreType.DMA((MICRO, PIECES)),
        pltpu.SemaphoreType.DMA((MICRO, PIECES)),
        pltpu.SemaphoreType.DMA((MICRO, PIECES)),
        pltpu.SemaphoreType.DMA((MICRO, 2)),
    ]
    result = pl.pallas_call(
        functools.partial(kernel, lat_count, lon_count),
        out_shape=pltpu.VMEM(fields.shape, bf16),
        in_specs=[pl.BlockSpec(memory_space=pltpu.HBM)] * len(operands),
        out_specs=pl.BlockSpec(memory_space=pltpu.VMEM),
        scratch_shapes=scratch,
        compiler_params=pltpu.CompilerParams(
            collective_id=0, has_side_effects=True, vmem_limit_bytes=56 * 1024 * 1024
        ),
        name="two_blocks",
    )(*operands)
    return jnp.transpose(result, (0, 3, 1, 2, 4))[None]


def solution(mesh):
    return jax.shard_map(
        body,
        mesh=mesh,
        in_specs=(
            P(None, None, "lat", "lon", None),
            P(),
            P("section", None, None),
            P("section", None, None),
            P("section", None, None),
            P("section", None, None),
            P("section", None, None),
            P("section", None, None, None),
        ),
        out_specs=P("section", None, None, "lat", "lon", None),
        check_vma=False,
    )
```

```python
import functools

import jax
import jax.numpy as jnp
from jax import lax
from jax.experimental import pallas as pl
from jax.experimental.pallas import tpu as pltpu
from jax.sharding import PartitionSpec as P

WIN_P = 2
WIN_H = 6
WIN_W = 12
TOK = WIN_P * WIN_H * WIN_W
LEVELS = 4
MICRO = 2
WIDTH = 384
HEADS = 12
FF = 1536
PIECES = 8
PROWS = 112
PACKED = 192
GRID_ROWS = LEVELS * WIN_H * WIN_W
GROUP = 640
GUSED = 576
KDIM = 288
LOG2E = 1.4426950408889634
MESH = pl.DeviceIdType.MESH


def divide(value, by):
    return (value * (-(-65536 // by))) >> 16


def token_parts(token):
    col = divide(token, 12)
    rest = token - col * 12
    level = (rest >= 6).astype(jnp.int32)
    return col, level, rest - level * 6


def packed_row(window, row_half, col_half, level, row, col):
    quarter = row_half + 2 * col_half
    inner = level * 18 + row * 6 + col
    return window * PACKED + jnp.where(inner < 32, quarter * 32 + inner, 96 + quarter * 16 + inner)


def halves(position, extent):
    half = (position >= extent).astype(jnp.int32)
    return half, position - half * extent


def one_hot(rows, target):
    at = lax.broadcasted_iota(jnp.int32, (rows, target.shape[1]), 0)
    return (at == target).astype(jnp.float32).astype(jnp.bfloat16)


def grid_place(row, col, level):
    return (row * 12 + col) * 4 + level


def pack_matrix(rows, target):
    row = lax.broadcasted_iota(jnp.int32, (rows, 1), 0)
    last = jnp.where((row & 12) == 12, -1, row - (row & 12))
    row = jnp.where(halves(row, PACKED)[1] < 128, row, last)
    return (row == target).astype(jnp.float32).astype(jnp.bfloat16)


def gather_matrix():
    place = lax.broadcasted_iota(jnp.int32, (1, GRID_ROWS), 1)
    pair = place >> 2
    row = divide(pair, 12)
    row_half, row_in = halves(row, 3)
    col_half, col_in = halves(pair - row * 12, 6)
    level = ((place & 3) + 3) & 3
    target = packed_row(level >> 1, 1 - row_half, 1 - col_half, level & 1, row_in, col_in)
    return pack_matrix(2 * PACKED, target)


def scatter_matrix():
    col, level, row = token_parts(lax.broadcasted_iota(jnp.int32, (1, TOK), 1))
    row_half, row_in = halves(row, 3)
    col_half, col_in = halves(col, 6)
    return pack_matrix(PACKED, packed_row(0, row_half, col_half, level, row_in, col_in))


def packed_parts(rows):
    place = lax.broadcasted_iota(jnp.int32, (1, rows), 1)
    window, place = halves(place, PACKED)
    early = place < 128
    quarter = jnp.where(early, place >> 5, (place - 128) >> 4)
    inner = jnp.where(early, place & 31, 32 + (place & 3))
    used = early | ((place & 12) != 12)
    level, rest = halves(inner, 18)
    row = divide(rest, 6)
    return used, quarter & 1, quarter >> 1, 2 * window + level, row, rest - row * 6


def shifted_matrix():
    used, row_half, col_half, level, row, col = packed_parts(PACKED)
    token = (col + 6 * col_half) * 12 + level * 6 + row + 3 * row_half
    return one_hot(TOK, jnp.where(used, token, -1))


def owned_parts():
    used, row_half, col_half, level, row, col = packed_parts(2 * PACKED)
    return used, (level + 1) & 3, row + 3 * (1 - row_half), col + 6 * (1 - col_half)


def owned_matrix():
    used, level, row, col = owned_parts()
    token = (level >> 1) * TOK + col * 12 + (level & 1) * 6 + row
    return one_hot(2 * TOK, jnp.where(used, token, -1))


def back_matrix():
    used, level, row, col = owned_parts()
    return one_hot(GRID_ROWS, jnp.where(used, grid_place(row, col, level), -1))


def plain_matrix():
    token = lax.broadcasted_iota(jnp.int32, (1, 2 * TOK), 1)
    window, rest = halves(token, TOK)
    col, level, row = token_parts(rest)
    return one_hot(GRID_ROWS, grid_place(row, col, 2 * window + level))


def pack(rows, refs, m, window):
    rows = rows.astype(jnp.bfloat16)
    chunk = (lax.broadcasted_iota(jnp.int32, (64, 1), 0) >> 2) & 3
    last = rows[128:].astype(jnp.float32)
    last = jnp.where(chunk == 0, last[:, 0:128], jnp.where(chunk == 1, last[:, 128:256], last[:, 256:384]))
    last = last.astype(jnp.bfloat16)
    for quarter in range(4):
        piece = window * 4 + quarter
        for ref in refs[piece]:
            for c in range(3):
                ref[m, piece, c * 32 : c * 32 + 32, :] = rows[quarter * 32 : quarter * 32 + 32, c * 128 : c * 128 + 128]
            ref[m, piece, 96:112, :] = last[quarter * 16 : quarter * 16 + 16]


def unpack(ref, m, window):
    chunk = (lax.broadcasted_iota(jnp.int32, (64, 1), 0) >> 2) & 3
    pieces = range(window * 4, window * 4 + 4)
    rows = [
        jnp.concatenate([ref[m, piece, c * 32 : c * 32 + 32, :] for c in range(3)], axis=1)
        for piece in pieces
    ]
    last = jnp.concatenate([ref[m, piece, 96:112, :] for piece in pieces], axis=0).astype(jnp.float32)
    last = jnp.concatenate([jnp.where(chunk == c, last, 0.0) for c in range(3)], axis=1)
    return jnp.concatenate(rows + [last.astype(jnp.bfloat16)], axis=0)


def unpack_both(ref, m):
    return jnp.concatenate([unpack(ref, m, window) for window in range(2)], axis=0)


def dot(a, b):
    return jnp.dot(a, b, preferred_element_type=jnp.float32)


def dot_nt(a, b):
    return lax.dot_general(a, b, (((1,), (1,)), ((), ())), preferred_element_type=jnp.float32)


def layer_norm(values, gain):
    average = jnp.mean(values, axis=-1, keepdims=True)
    centred = values - average
    spread = jnp.mean(centred * centred, axis=-1, keepdims=True)
    return centred * lax.rsqrt(spread + 1e-05) * gain


def gelu(x):
    return x * (0.5 + 0.5 * lax.erf(x * 0.7071067811865476))


def lane_tokens():
    lane = lax.broadcasted_iota(jnp.int32, (1, 256), 1)
    return jnp.where(lane < 128, lane, 128 + (lane & 15))


def prepare_bias(first, lat, lon, lat_count, lon_count, class_ref, table_ref, rows_ref, turned_ref, bias_ref):
    kinds = 2 * lat_count
    one = jnp.where(first, 1, 0)
    lats = (lat, lax.rem(lat + lat_count - one, lat_count))
    lons = (lon, lax.rem(lon + lon_count - one, lon_count))
    to_row = lax.broadcasted_iota(jnp.int32, (32, HEADS * kinds), 0)
    to_col = lax.broadcasted_iota(jnp.int32, (32, HEADS * kinds), 1)
    kind = jnp.where(to_row < 16, lat, lat_count + lats[1])
    wanted = (to_row & 15) * kinds + kind
    own = (to_col == wanted).astype(jnp.float32).astype(jnp.bfloat16)
    table = dot(own, table_ref[...].reshape(HEADS * kinds, -1)).astype(jnp.bfloat16)
    rows_ref[...] = jnp.zeros_like(rows_ref)
    for i in range(2):
        for j in range(12):
            pb, rb = j // 6, j % 6
            for pa in range(2):
                begin = pb * 1656 + pa * 828 + rb * 138
                rows_ref[i, j, :, pa * 144 : pa * 144 + 138] = table[
                    i * 16 : i * 16 + 16, begin : begin + 138
                ]
    to_row = lax.broadcasted_iota(jnp.int32, (192, 192), 0)
    to_col = lax.broadcasted_iota(jnp.int32, (192, 192), 1)
    swap = (((to_row & 15) << 4) + (to_row >> 4) == to_col).astype(jnp.float32).astype(jnp.bfloat16)
    by_head = [
        dot(swap, rows_ref[i].reshape(192, KDIM)).astype(jnp.bfloat16) for i in range(2)
    ]
    by_head = jnp.concatenate(by_head, axis=0)
    col_a, level_a, row_a = token_parts(lane_tokens())
    base = level_a * 144 + row_a * 23 + col_a + 11
    depth = lax.broadcasted_iota(jnp.int32, (KDIM, 256), 0)
    for cb in range(12):
        pick = (depth == base - cb).astype(jnp.float32).astype(jnp.bfloat16)
        spread = dot(by_head, pick)
        for i in range(2):
            for h in range(HEADS):
                start = i * 192 + h * 16
                turned_ref[i * HEADS + h, cb * 12 : cb * 12 + 12, :] = spread[start : start + 12]
    rows_all = 6 * lat_count
    cols_all = 12 * lon_count
    classes = class_ref[...].reshape(LEVELS * rows_all, cols_all).astype(jnp.float32).astype(jnp.bfloat16)
    col_b, level_b, row_b = token_parts(lax.broadcasted_iota(jnp.int32, (TOK, 1), 0))

    def wrap(v, extent):
        return jnp.where(v >= extent, v - extent, v)

    def onehot(a, b):
        return (a == b).astype(jnp.float32).astype(jnp.bfloat16)

    identity = (
        lax.broadcasted_iota(jnp.int32, (TOK, 256), 0) == lax.broadcasted_iota(jnp.int32, (TOK, 256), 1)
    )
    identity = identity.astype(jnp.float32).astype(jnp.bfloat16)
    place_a = lax.broadcasted_iota(jnp.int32, (LEVELS * rows_all, 256), 0)
    place_b = lax.broadcasted_iota(jnp.int32, (TOK, LEVELS * rows_all), 1)
    for i in range(2):
        row_start = lats[i] * 6 + 3 * one
        col_start = lons[i] * 12 + 6 * one
        across = dot(
            classes,
            onehot(lax.broadcasted_iota(jnp.int32, (cols_all, 256), 0), wrap(col_start + col_a, cols_all)),
        )
        down = dot_nt(
            onehot(lax.broadcasted_iota(jnp.int32, (TOK, cols_all), 1), wrap(col_start + col_b, cols_all)),
            classes,
        )

        def region(place, level, row, values, axis):
            at = ((2 * i + level + one) & 3) * rows_all + wrap(row_start + row, rows_all)
            value = jnp.sum(jnp.where(place == at, values, 0.0), axis=axis, keepdims=True)
            flags = 2 * (2 * i + level >= 3).astype(jnp.int32)
            flags = flags + (lats[i] * 6 + row >= rows_all - 3).astype(jnp.int32)
            return 4.0 * value + (one * flags).astype(jnp.float32)

        region_a = region(place_a, level_a, row_a, across, 0)
        region_b = region(place_b, level_b, row_b, down, 1)
        same = region_b == region_a
        for g in range(3):
            heads = [turned_ref[i * HEADS + g * 4 + t] for t in range(4)]
            stack = jnp.concatenate([h[0:128] for h in heads] + [h[128:144] for h in heads], axis=0)
            spread = dot_nt(identity, stack.astype(jnp.bfloat16)) * LOG2E
            for t in range(5):
                lanes = slice(t * 128, min(t * 128 + 128, GUSED))
                part = same[:, 0:128] if t < 4 else same[:, 128:192]
                to = slice(g * GROUP + lanes.start, g * GROUP + lanes.stop)
                bias_ref[i, :, to] = jnp.where(part, spread[:, lanes], -1e30)
            bias_ref[i, :, g * GROUP + GUSED : (g + 1) * GROUP] = jnp.full((TOK, GROUP - GUSED), -1e30, jnp.float32)


def attention(query, key, value, bias_ref, i):
    head = lax.broadcasted_iota(jnp.int32, (1, 128), 1) >> 5
    keep = [(head == t).astype(jnp.float32).astype(jnp.bfloat16) for t in range(4)]
    segment = lax.broadcasted_iota(jnp.int32, (1, 128), 1) >> 4
    blank = jnp.zeros((64, 128), jnp.bfloat16)
    blank_wide = jnp.zeros((64, 256), jnp.bfloat16)
    mixed = []
    for g in range(3):
        lanes = slice(g * 128, g * 128 + 128)
        q, k, v = query[:, lanes], key[:, lanes], value[:, lanes]
        wide = jnp.concatenate([k[0:128] * m for m in keep] + [k[128:144] * m for m in keep] + [blank], axis=0)
        scores = dot_nt(q, wide) + bias_ref[i, :, g * GROUP : (g + 1) * GROUP]
        tail = scores[:, 512:640]
        top, weights = [], []
        for t in range(4):
            main = scores[:, t * 128 : t * 128 + 128]
            joined = jnp.maximum(main, jnp.where(segment == t, tail, -1e30))
            top.append(jnp.max(joined, axis=1, keepdims=True))
            weights.append(jnp.exp2(main - top[t]).astype(jnp.bfloat16))
        tops = jnp.where(segment < 2, jnp.where(segment == 0, top[0], top[1]), jnp.where(segment == 2, top[2], top[3]))
        weights.append(jnp.exp2(tail - tops).astype(jnp.bfloat16))
        weights = jnp.concatenate(weights, axis=1)
        pairs = [jnp.concatenate([v[0:128] * m, jnp.broadcast_to(m, (128, 128))], axis=1) for m in keep]
        pairs += [jnp.concatenate([v[128:144] * m, jnp.broadcast_to(m, (16, 128))], axis=1) for m in keep]
        out = dot(weights, jnp.concatenate(pairs + [blank_wide], axis=0))
        mixed.append((out[:, 0:128] / out[:, 128:256]).astype(jnp.bfloat16))
    return jnp.concatenate(mixed, axis=1)


def project(x, gains_ref, joint_ref):
    normed = layer_norm(x, gains_ref[0:1].astype(jnp.float32)).astype(jnp.bfloat16)
    projected = dot(normed, joint_ref[...])
    query = projected[:, 0:WIDTH] * (LOG2E * 32**-0.5)
    return jnp.concatenate([query, projected[:, WIDTH:]], axis=1).astype(jnp.bfloat16)


def finish(x, projected, gains_ref, out_ref, expand_ref, reduce_ref, bias_ref):
    query, key, value = (projected[:, n * WIDTH : (n + 1) * WIDTH] for n in range(3))
    mixed = []
    for i in range(2):
        rows = slice(i * TOK, (i + 1) * TOK)
        mixed.append(attention(query[rows], key[rows], value[rows], bias_ref, i))
    hidden = x + dot(jnp.concatenate(mixed, axis=0), out_ref[...])
    again = layer_norm(hidden, gains_ref[1:2].astype(jnp.float32)).astype(jnp.bfloat16)
    act = gelu(dot(again, expand_ref[...])).astype(jnp.bfloat16)
    return (hidden + dot(act, reduce_ref[...])).astype(jnp.bfloat16)


def kernel(
    lat_count,
    lon_count,
    fields_hbm,
    class_hbm,
    gains_hbm,
    joint_hbm,
    oproj_hbm,
    expand_hbm,
    reduce_hbm,
    table_hbm,
    result_ref,
    fields_ref,
    class_ref,
    gains_ref,
    joint_ref,
    oproj_ref,
    expand_ref,
    reduce_ref,
    table_ref,
    gather_ref,
    into_ref,
    scatter_ref,
    last_ref,
    x_ref,
    y_ref,
    rows_ref,
    turned_ref,
    bias_ref,
    halo_ref,
    take_ref,
    done_ref,
    home_ref,
    load_sem,
    halo_send,
    take_recv,
    home_send,
    home_recv,
    next_send,
    hand_send,
):
    sec = lax.axis_index("section")
    lat = lax.axis_index("lat")
    lon = lax.axis_index("lon")
    first = sec == 0
    lat_up = lax.rem(lat + 1, lat_count)
    lat_down = lax.rem(lat + lat_count - 1, lat_count)
    lon_up = lax.rem(lon + 1, lon_count)
    lon_down = lax.rem(lon + lon_count - 1, lon_count)
    own = (0, 7)
    others = (3, 4, 2, 5, 1, 6)

    def owner(piece, sign):
        row_half, col_half, window = piece & 1, (piece >> 1) & 1, piece >> 2
        up, right = sign * (row_half - window), sign * (col_half - window)
        where_lat = {0: lat, 1: lat_up, -1: lat_down}[up]
        where_lon = {0: lon, 1: lon_up, -1: lon_down}[right]
        return (where_lat, where_lon)

    barrier = pltpu.get_barrier_semaphore()

    @pl.when(first)
    def _():
        for piece in others:
            pl.semaphore_signal(barrier, inc=1, device_id=(0,) + owner(piece, 1), device_id_type=MESH)
        pl.semaphore_signal(barrier, inc=1, device_id=(1, lat, lon), device_id_type=MESH)

    @pl.when(jnp.logical_not(first))
    def _():
        for piece in others + own[:1]:
            pl.semaphore_signal(barrier, inc=1, device_id=(0,) + owner(piece, 1), device_id_type=MESH)

    loads = []

    def load(src, dst):
        copy = pltpu.make_async_copy(src, dst, load_sem.at[len(loads)])
        copy.start()
        loads.append(copy)
        return copy

    load_fields = [load(fields_hbm.at[m], fields_ref.at[m]) for m in range(MICRO)]
    prep = [load(table_hbm.at[0], table_ref), load(class_hbm, class_ref)]
    rest = [
        load(gains_hbm.at[0], gains_ref),
        load(joint_hbm.at[0], joint_ref),
        load(oproj_hbm.at[0], oproj_ref),
        load(expand_hbm.at[0], expand_ref),
        load(reduce_hbm.at[0], reduce_ref),
    ]

    def halo_copy(m, q):
        return pltpu.make_async_remote_copy(
            src_ref=halo_ref.at[m, q],
            dst_ref=take_ref.at[m, q],
            send_sem=halo_send.at[m, q],
            recv_sem=take_recv.at[m, q],
            device_id=(0,) + owner(q, -1),
            device_id_type=MESH,
        )

    def home_copy(m, q):
        return pltpu.make_async_remote_copy(
            src_ref=done_ref.at[m, q],
            dst_ref=home_ref.at[m, q],
            send_sem=home_send.at[m, q],
            recv_sem=home_recv.at[m, q],
            device_id=(0,) + owner(q, 1),
            device_id_type=MESH,
        )

    odd = lax.rem(lat, 2)
    lat_chip = lat + 1 - 2 * odd
    lat_cross = lax.rem(lat + lat_count - 1 + 2 * odd, lat_count)
    lon_cross = (lax.rem(lon + lon_count - 1 + odd, lon_count), lax.rem(lon + odd, lon_count))
    lon_chip = (lax.rem(lon + lon_count - odd, lon_count), lax.rem(lon + 1 - odd, lon_count))

    def chip_copy(m, col_half):
        piece = 1 + 3 * odd + 2 * col_half
        return pltpu.make_async_remote_copy(
            src_ref=done_ref.at[m, piece],
            dst_ref=home_ref.at[m, piece],
            send_sem=home_send.at[m, piece],
            recv_sem=home_recv.at[m, piece],
            device_id=(0, lat_chip, lon_chip[col_half]),
            device_id_type=MESH,
        )

    def cross_copy(m, col_half):
        piece = 4 - 3 * odd + 2 * col_half
        return pltpu.make_async_remote_copy(
            src_ref=done_ref.at[m, piece],
            dst_ref=home_ref.at[m, piece],
            send_sem=home_send.at[m, piece],
            recv_sem=home_recv.at[m, piece],
            device_id=(0, lat_cross, lon_cross[col_half]),
            device_id_type=MESH,
        )

    def hand_copy(m, col_half):
        piece = 1 + 3 * odd + 2 * col_half
        return pltpu.make_async_remote_copy(
            src_ref=take_ref.at[m, piece],
            dst_ref=home_ref.at[m, piece],
            send_sem=hand_send.at[m, col_half],
            recv_sem=home_recv.at[m, piece],
            device_id=(0, lat, lon),
            device_id_type=MESH,
        )

    def next_copy(m, q):
        return pltpu.make_async_remote_copy(
            src_ref=done_ref.at[m, q],
            dst_ref=take_ref.at[m, q],
            send_sem=next_send.at[m, q],
            recv_sem=take_recv.at[m, q],
            device_id=(1,) + owner(q, 1),
            device_id_type=MESH,
        )

    @pl.when(first)
    def _():
        gather_ref[...] = gather_matrix()
        for m in range(MICRO):
            load_fields[m].wait()
            rows = dot(gather_ref[...], fields_ref[m].reshape(GRID_ROWS, WIDTH))
            refs = [[take_ref] if q in own else [halo_ref] for q in range(PIECES)]
            for window in range(2):
                pack(rows[window * PACKED : (window + 1) * PACKED], refs, m, window)
            if m == 0:
                pl.semaphore_wait(barrier, 13)
            for q in others:
                halo_copy(m, q).start()

    @pl.when(first)
    def _():
        into_ref[0:TOK, 0:PACKED] = shifted_matrix()
        scatter_ref[...] = scatter_matrix()
        last_ref[...] = back_matrix()

    @pl.when(jnp.logical_not(first))
    def _():
        for copy in load_fields:
            copy.wait()
        into_ref[...] = owned_matrix()
        last_ref[:, 0 : 2 * TOK] = plain_matrix()
        pl.semaphore_wait(barrier, 1)

    for copy in prep:
        copy.wait()
    prepare_bias(first, lat, lon, lat_count, lon_count, class_ref, table_ref, rows_ref, turned_ref, bias_ref)
    for copy in rest:
        copy.wait()

    def step(m, carry):
        @pl.when(first)
        def _():
            for q in others:
                halo_copy(m, q).wait_recv()
            for window in range(2):
                rows = dot(into_ref[0:TOK, 0:PACKED], unpack(take_ref, m, window))
                x_ref[window * TOK : (window + 1) * TOK, :] = rows.astype(jnp.bfloat16)

        @pl.when(jnp.logical_not(first))
        def _():
            for q in range(PIECES):
                next_copy(m, q).wait_recv()

            @pl.when(m < MICRO - 1)
            def _():
                for col_half in range(2):
                    hand_copy(m, col_half).start()

            x_ref[...] = dot(into_ref[...], unpack_both(take_ref, m)).astype(jnp.bfloat16)

        x = x_ref[...].astype(jnp.float32)
        projected = project(x, gains_ref, joint_ref)
        y_ref[...] = finish(x, projected, gains_ref, oproj_ref, expand_ref, reduce_ref, bias_ref)
        refs = [[done_ref, home_ref] if q in own else [done_ref] for q in range(PIECES)]

        @pl.when(first)
        def _():
            for window in range(2):
                rows = slice(window * TOK, (window + 1) * TOK)
                pack(dot(scatter_ref[...], y_ref[rows, :]), refs, m, window)
                for q in (3, 1, 2, 0) if window == 0 else (4, 6, 5, 7):
                    next_copy(m, q).start()
            @pl.when(m == MICRO - 1)
            def _():
                for col_half in range(2):
                    cross_copy(m, col_half).start()

            for q in (2, 5):
                home_copy(m, q).start()
            for col_half in range(2):
                chip_copy(m, col_half).start()

        @pl.when(jnp.logical_not(first))
        def _():
            write(m, dot(last_ref[:, 0 : 2 * TOK], y_ref[...]).astype(jnp.bfloat16))

        return carry

    def write(m, rows):
        result_ref[m] = rows.reshape(WIN_H, WIN_W, LEVELS, WIDTH)

    lax.fori_loop(0, MICRO, step, 0)

    @pl.when(first)
    def _():
        for m in range(MICRO):
            for q in others:
                home_copy(m, q).wait_recv()
            write(m, dot(last_ref[...], unpack_both(home_ref, m)).astype(jnp.bfloat16))
        for m in range(MICRO):
            for q in others:
                halo_copy(m, q).wait_send()
            for q in (2, 5):
                home_copy(m, q).wait_send()
            for col_half in range(2):
                chip_copy(m, col_half).wait_send()
                if m == MICRO - 1:
                    cross_copy(m, col_half).wait_send()
            for q in range(PIECES):
                next_copy(m, q).wait_send()

    @pl.when(jnp.logical_not(first))
    def _():
        for m in range(MICRO - 1):
            for col_half in range(2):
                hand_copy(m, col_half).wait_send()


def body(
    fields, surface_class, norm_gains, joint_proj, out_proj, expand_proj, reduce_proj, earth_bias
):
    lat_count = lax.axis_size("lat")
    lon_count = lax.axis_size("lon")
    fields = jnp.transpose(fields, (0, 2, 3, 1, 4))
    operands = (
        fields, surface_class, norm_gains, joint_proj, out_proj, expand_proj, reduce_proj,
        jnp.transpose(earth_bias, (0, 2, 1, 3)),
    )
    bf16 = jnp.bfloat16
    scratch = [
        pltpu.VMEM(fields.shape, bf16),
        pltpu.VMEM(surface_class.shape, jnp.int32),
        pltpu.VMEM((2, WIDTH), bf16),
        pltpu.VMEM((WIDTH, 3 * WIDTH), bf16),
        pltpu.VMEM((WIDTH, WIDTH), bf16),
        pltpu.VMEM((WIDTH, FF), bf16),
        pltpu.VMEM((FF, WIDTH), bf16),
        pltpu.VMEM((HEADS,) + earth_bias.shape[1:2] + earth_bias.shape[3:], bf16),
        pltpu.VMEM((2 * PACKED, GRID_ROWS), bf16),
        pltpu.VMEM((2 * TOK, 2 * PACKED), bf16),
        pltpu.VMEM((PACKED, TOK), bf16),
        pltpu.VMEM((GRID_ROWS, 2 * PACKED), bf16),
        pltpu.VMEM((2 * TOK, WIDTH), bf16),
        pltpu.VMEM((2 * TOK, WIDTH), bf16),
        pltpu.VMEM((2, 12, 16, KDIM), bf16),
        pltpu.VMEM((2 * HEADS, TOK, 256), jnp.float32),
        pltpu.VMEM((2, TOK, 3 * GROUP), jnp.float32),
        pltpu.VMEM((MICRO, PIECES, PROWS, 128), bf16),
        pltpu.VMEM((MICRO, PIECES, PROWS, 128), bf16),
        pltpu.VMEM((MICRO, PIECES, PROWS, 128), bf16),
        pltpu.VMEM((MICRO, PIECES, PROWS, 128), bf16),
        pltpu.SemaphoreType.DMA((14,)),
        pltpu.SemaphoreType.DMA((MICRO, PIECES)),
        pltpu.SemaphoreType.DMA((MICRO, PIECES)),
        pltpu.SemaphoreType.DMA((MICRO, PIECES)),
        pltpu.SemaphoreType.DMA((MICRO, PIECES)),
        pltpu.SemaphoreType.DMA((MICRO, PIECES)),
        pltpu.SemaphoreType.DMA((MICRO, 2)),
    ]
    result = pl.pallas_call(
        functools.partial(kernel, lat_count, lon_count),
        out_shape=pltpu.VMEM(fields.shape, bf16),
        in_specs=[pl.BlockSpec(memory_space=pltpu.HBM)] * len(operands),
        out_specs=pl.BlockSpec(memory_space=pltpu.VMEM),
        scratch_shapes=scratch,
        compiler_params=pltpu.CompilerParams(
            collective_id=0, has_side_effects=True, vmem_limit_bytes=56 * 1024 * 1024
        ),
        name="two_blocks",
    )(*operands)
    return jnp.transpose(result, (0, 3, 1, 2, 4))[None]


def solution(mesh):
    return jax.shard_map(
        body,
        mesh=mesh,
        in_specs=(
            P(None, None, "lat", "lon", None),
            P(),
            P("section", None, None),
            P("section", None, None),
            P("section", None, None),
            P("section", None, None),
            P("section", None, None),
            P("section", None, None, None),
        ),
        out_specs=P("section", None, None, "lat", "lon", None),
        check_vma=False,
    )
```

```python
import functools

import jax
import jax.numpy as jnp
from jax import lax
from jax.experimental import pallas as pl
from jax.experimental.pallas import tpu as pltpu
from jax.sharding import PartitionSpec as P

WIN_P = 2
WIN_H = 6
WIN_W = 12
TOK = WIN_P * WIN_H * WIN_W
LEVELS = 4
MICRO = 2
WIDTH = 384
HEADS = 12
FF = 1536
PIECES = 8
PROWS = 112
PACKED = 192
GRID_ROWS = LEVELS * WIN_H * WIN_W
GROUP = 640
GUSED = 576
KDIM = 288
LOG2E = 1.4426950408889634
MESH = pl.DeviceIdType.MESH


def divide(value, by):
    return (value * (-(-65536 // by))) >> 16


def token_parts(token):
    col = divide(token, 12)
    rest = token - col * 12
    level = (rest >= 6).astype(jnp.int32)
    return col, level, rest - level * 6


def packed_row(window, row_half, col_half, level, row, col):
    quarter = row_half + 2 * col_half
    inner = level * 18 + row * 6 + col
    return window * PACKED + jnp.where(inner < 32, quarter * 32 + inner, 96 + quarter * 16 + inner)


def halves(position, extent):
    half = (position >= extent).astype(jnp.int32)
    return half, position - half * extent


def one_hot(rows, target):
    at = lax.broadcasted_iota(jnp.int32, (rows, target.shape[1]), 0)
    return (at == target).astype(jnp.float32).astype(jnp.bfloat16)


def grid_place(row, col, level):
    return (row * 12 + col) * 4 + level


def pack_matrix(rows, target):
    row = lax.broadcasted_iota(jnp.int32, (rows, 1), 0)
    last = jnp.where((row & 12) == 12, -1, row - (row & 12))
    row = jnp.where(halves(row, PACKED)[1] < 128, row, last)
    return (row == target).astype(jnp.float32).astype(jnp.bfloat16)


def gather_matrix():
    place = lax.broadcasted_iota(jnp.int32, (1, GRID_ROWS), 1)
    pair = place >> 2
    row = divide(pair, 12)
    row_half, row_in = halves(row, 3)
    col_half, col_in = halves(pair - row * 12, 6)
    level = ((place & 3) + 3) & 3
    target = packed_row(level >> 1, 1 - row_half, 1 - col_half, level & 1, row_in, col_in)
    return pack_matrix(2 * PACKED, target)


def scatter_matrix():
    col, level, row = token_parts(lax.broadcasted_iota(jnp.int32, (1, TOK), 1))
    row_half, row_in = halves(row, 3)
    col_half, col_in = halves(col, 6)
    return pack_matrix(PACKED, packed_row(0, row_half, col_half, level, row_in, col_in))


def packed_parts(rows):
    place = lax.broadcasted_iota(jnp.int32, (1, rows), 1)
    window, place = halves(place, PACKED)
    early = place < 128
    quarter = jnp.where(early, place >> 5, (place - 128) >> 4)
    inner = jnp.where(early, place & 31, 32 + (place & 3))
    used = early | ((place & 12) != 12)
    level, rest = halves(inner, 18)
    row = divide(rest, 6)
    return used, quarter & 1, quarter >> 1, 2 * window + level, row, rest - row * 6


def shifted_matrix():
    used, row_half, col_half, level, row, col = packed_parts(PACKED)
    token = (col + 6 * col_half) * 12 + level * 6 + row + 3 * row_half
    return one_hot(TOK, jnp.where(used, token, -1))


def owned_parts():
    used, row_half, col_half, level, row, col = packed_parts(2 * PACKED)
    return used, (level + 1) & 3, row + 3 * (1 - row_half), col + 6 * (1 - col_half)


def owned_matrix():
    used, level, row, col = owned_parts()
    token = (level >> 1) * TOK + col * 12 + (level & 1) * 6 + row
    return one_hot(2 * TOK, jnp.where(used, token, -1))


def back_matrix():
    used, level, row, col = owned_parts()
    return one_hot(GRID_ROWS, jnp.where(used, grid_place(row, col, level), -1))


def plain_matrix():
    token = lax.broadcasted_iota(jnp.int32, (1, 2 * TOK), 1)
    window, rest = halves(token, TOK)
    col, level, row = token_parts(rest)
    return one_hot(GRID_ROWS, grid_place(row, col, 2 * window + level))


def pack(rows, refs, m, window):
    rows = rows.astype(jnp.bfloat16)
    chunk = (lax.broadcasted_iota(jnp.int32, (64, 1), 0) >> 2) & 3
    last = rows[128:].astype(jnp.float32)
    last = jnp.where(chunk == 0, last[:, 0:128], jnp.where(chunk == 1, last[:, 128:256], last[:, 256:384]))
    last = last.astype(jnp.bfloat16)
    for quarter in range(4):
        piece = window * 4 + quarter
        for ref in refs[piece]:
            for c in range(3):
                ref[m, piece, c * 32 : c * 32 + 32, :] = rows[quarter * 32 : quarter * 32 + 32, c * 128 : c * 128 + 128]
            ref[m, piece, 96:112, :] = last[quarter * 16 : quarter * 16 + 16]


def unpack(ref, m, window):
    chunk = (lax.broadcasted_iota(jnp.int32, (64, 1), 0) >> 2) & 3
    pieces = range(window * 4, window * 4 + 4)
    rows = [
        jnp.concatenate([ref[m, piece, c * 32 : c * 32 + 32, :] for c in range(3)], axis=1)
        for piece in pieces
    ]
    last = jnp.concatenate([ref[m, piece, 96:112, :] for piece in pieces], axis=0).astype(jnp.float32)
    last = jnp.concatenate([jnp.where(chunk == c, last, 0.0) for c in range(3)], axis=1)
    return jnp.concatenate(rows + [last.astype(jnp.bfloat16)], axis=0)


def unpack_both(ref, m):
    return jnp.concatenate([unpack(ref, m, window) for window in range(2)], axis=0)


def dot(a, b):
    return jnp.dot(a, b, preferred_element_type=jnp.float32)


def dot_nt(a, b):
    return lax.dot_general(a, b, (((1,), (1,)), ((), ())), preferred_element_type=jnp.float32)


def layer_norm(values, gain):
    average = jnp.mean(values, axis=-1, keepdims=True)
    centred = values - average
    spread = jnp.mean(centred * centred, axis=-1, keepdims=True)
    return centred * lax.rsqrt(spread + 1e-05) * gain


def gelu(x):
    return x * (0.5 + 0.5 * lax.erf(x * 0.7071067811865476))


def lane_tokens():
    lane = lax.broadcasted_iota(jnp.int32, (1, 256), 1)
    return jnp.where(lane < 128, lane, 128 + (lane & 15))


def prepare_bias(first, lat, lon, lat_count, lon_count, class_ref, table_ref, rows_ref, turned_ref, bias_ref):
    kinds = 2 * lat_count
    one = jnp.where(first, 1, 0)
    lats = (lat, lax.rem(lat + lat_count - one, lat_count))
    lons = (lon, lax.rem(lon + lon_count - one, lon_count))
    to_row = lax.broadcasted_iota(jnp.int32, (32, HEADS * kinds), 0)
    to_col = lax.broadcasted_iota(jnp.int32, (32, HEADS * kinds), 1)
    kind = jnp.where(to_row < 16, lat, lat_count + lats[1])
    wanted = (to_row & 15) * kinds + kind
    own = (to_col == wanted).astype(jnp.float32).astype(jnp.bfloat16)
    table = dot(own, table_ref[...].reshape(HEADS * kinds, -1)).astype(jnp.bfloat16)
    rows_ref[...] = jnp.zeros_like(rows_ref)
    for i in range(2):
        for j in range(12):
            pb, rb = j // 6, j % 6
            for pa in range(2):
                begin = pb * 1656 + pa * 828 + rb * 138
                rows_ref[i, j, :, pa * 144 : pa * 144 + 138] = table[
                    i * 16 : i * 16 + 16, begin : begin + 138
                ]
    to_row = lax.broadcasted_iota(jnp.int32, (192, 192), 0)
    to_col = lax.broadcasted_iota(jnp.int32, (192, 192), 1)
    swap = (((to_row & 15) << 4) + (to_row >> 4) == to_col).astype(jnp.float32).astype(jnp.bfloat16)
    by_head = [
        dot(swap, rows_ref[i].reshape(192, KDIM)).astype(jnp.bfloat16) for i in range(2)
    ]
    by_head = jnp.concatenate(by_head, axis=0)
    col_a, level_a, row_a = token_parts(lane_tokens())
    base = level_a * 144 + row_a * 23 + col_a + 11
    depth = lax.broadcasted_iota(jnp.int32, (KDIM, 256), 0)
    for cb in range(12):
        pick = (depth == base - cb).astype(jnp.float32).astype(jnp.bfloat16)
        spread = dot(by_head, pick)
        for i in range(2):
            for h in range(HEADS):
                start = i * 192 + h * 16
                turned_ref[i * HEADS + h, cb * 12 : cb * 12 + 12, :] = spread[start : start + 12]
    rows_all = 6 * lat_count
    cols_all = 12 * lon_count
    classes = class_ref[...].reshape(LEVELS * rows_all, cols_all).astype(jnp.float32).astype(jnp.bfloat16)
    col_b, level_b, row_b = token_parts(lax.broadcasted_iota(jnp.int32, (TOK, 1), 0))

    def wrap(v, extent):
        return jnp.where(v >= extent, v - extent, v)

    def onehot(a, b):
        return (a == b).astype(jnp.float32).astype(jnp.bfloat16)

    identity = (
        lax.broadcasted_iota(jnp.int32, (TOK, 256), 0) == lax.broadcasted_iota(jnp.int32, (TOK, 256), 1)
    )
    identity = identity.astype(jnp.float32).astype(jnp.bfloat16)
    place_a = lax.broadcasted_iota(jnp.int32, (LEVELS * rows_all, 256), 0)
    place_b = lax.broadcasted_iota(jnp.int32, (TOK, LEVELS * rows_all), 1)
    for i in range(2):
        row_start = lats[i] * 6 + 3 * one
        col_start = lons[i] * 12 + 6 * one
        across = dot(
            classes,
            onehot(lax.broadcasted_iota(jnp.int32, (cols_all, 256), 0), wrap(col_start + col_a, cols_all)),
        )
        down = dot_nt(
            onehot(lax.broadcasted_iota(jnp.int32, (TOK, cols_all), 1), wrap(col_start + col_b, cols_all)),
            classes,
        )

        def region(place, level, row, values, axis):
            at = ((2 * i + level + one) & 3) * rows_all + wrap(row_start + row, rows_all)
            value = jnp.sum(jnp.where(place == at, values, 0.0), axis=axis, keepdims=True)
            flags = 2 * (2 * i + level >= 3).astype(jnp.int32)
            flags = flags + (lats[i] * 6 + row >= rows_all - 3).astype(jnp.int32)
            return 4.0 * value + (one * flags).astype(jnp.float32)

        region_a = region(place_a, level_a, row_a, across, 0)
        region_b = region(place_b, level_b, row_b, down, 1)
        same = region_b == region_a
        for g in range(3):
            heads = [turned_ref[i * HEADS + g * 4 + t] for t in range(4)]
            stack = jnp.concatenate([h[0:128] for h in heads] + [h[128:144] for h in heads], axis=0)
            spread = dot_nt(identity, stack.astype(jnp.bfloat16)) * LOG2E
            for t in range(5):
                lanes = slice(t * 128, min(t * 128 + 128, GUSED))
                part = same[:, 0:128] if t < 4 else same[:, 128:192]
                to = slice(g * GROUP + lanes.start, g * GROUP + lanes.stop)
                bias_ref[i, :, to] = jnp.where(part, spread[:, lanes], -1e30)
            bias_ref[i, :, g * GROUP + GUSED : (g + 1) * GROUP] = jnp.full((TOK, GROUP - GUSED), -1e30, jnp.float32)


def attention(query, key, value, bias_ref, i):
    head = lax.broadcasted_iota(jnp.int32, (1, 128), 1) >> 5
    keep = [(head == t).astype(jnp.float32).astype(jnp.bfloat16) for t in range(4)]
    segment = lax.broadcasted_iota(jnp.int32, (1, 128), 1) >> 4
    blank = jnp.zeros((64, 128), jnp.bfloat16)
    blank_wide = jnp.zeros((64, 256), jnp.bfloat16)
    mixed = []
    for g in range(3):
        lanes = slice(g * 128, g * 128 + 128)
        q, k, v = query[:, lanes], key[:, lanes], value[:, lanes]
        wide = jnp.concatenate([k[0:128] * m for m in keep] + [k[128:144] * m for m in keep] + [blank], axis=0)
        scores = dot_nt(q, wide) + bias_ref[i, :, g * GROUP : (g + 1) * GROUP]
        tail = scores[:, 512:640]
        top, weights = [], []
        for t in range(4):
            main = scores[:, t * 128 : t * 128 + 128]
            joined = jnp.maximum(main, jnp.where(segment == t, tail, -1e30))
            top.append(jnp.max(joined, axis=1, keepdims=True))
            weights.append(jnp.exp2(main - top[t]).astype(jnp.bfloat16))
        tops = jnp.where(segment < 2, jnp.where(segment == 0, top[0], top[1]), jnp.where(segment == 2, top[2], top[3]))
        weights.append(jnp.exp2(tail - tops).astype(jnp.bfloat16))
        weights = jnp.concatenate(weights, axis=1)
        pairs = [jnp.concatenate([v[0:128] * m, jnp.broadcast_to(m, (128, 128))], axis=1) for m in keep]
        pairs += [jnp.concatenate([v[128:144] * m, jnp.broadcast_to(m, (16, 128))], axis=1) for m in keep]
        out = dot(weights, jnp.concatenate(pairs + [blank_wide], axis=0))
        mixed.append((out[:, 0:128] / out[:, 128:256]).astype(jnp.bfloat16))
    return jnp.concatenate(mixed, axis=1)


def project(x, gains_ref, joint_ref):
    normed = layer_norm(x, gains_ref[0:1].astype(jnp.float32)).astype(jnp.bfloat16)
    projected = dot(normed, joint_ref[...])
    query = projected[:, 0:WIDTH] * (LOG2E * 32**-0.5)
    return jnp.concatenate([query, projected[:, WIDTH:]], axis=1).astype(jnp.bfloat16)


def finish(x, projected, gains_ref, out_ref, expand_ref, reduce_ref, bias_ref):
    query, key, value = (projected[:, n * WIDTH : (n + 1) * WIDTH] for n in range(3))
    mixed = []
    for i in range(2):
        rows = slice(i * TOK, (i + 1) * TOK)
        mixed.append(attention(query[rows], key[rows], value[rows], bias_ref, i))
    hidden = x + dot(jnp.concatenate(mixed, axis=0), out_ref[...])
    again = layer_norm(hidden, gains_ref[1:2].astype(jnp.float32)).astype(jnp.bfloat16)
    act = gelu(dot(again, expand_ref[...])).astype(jnp.bfloat16)
    return (hidden + dot(act, reduce_ref[...])).astype(jnp.bfloat16)


def kernel(
    lat_count,
    lon_count,
    fields_hbm,
    class_hbm,
    gains_hbm,
    joint_hbm,
    oproj_hbm,
    expand_hbm,
    reduce_hbm,
    table_hbm,
    result_ref,
    fields_ref,
    class_ref,
    gains_ref,
    joint_ref,
    oproj_ref,
    expand_ref,
    reduce_ref,
    table_ref,
    gather_ref,
    into_ref,
    scatter_ref,
    last_ref,
    x_ref,
    y_ref,
    rows_ref,
    turned_ref,
    bias_ref,
    halo_ref,
    take_ref,
    done_ref,
    home_ref,
    load_sem,
    halo_send,
    take_recv,
    home_send,
    home_recv,
    next_send,
    hand_send,
    ready_sem,
):
    sec = lax.axis_index("section")
    lat = lax.axis_index("lat")
    lon = lax.axis_index("lon")
    first = sec == 0
    lat_up = lax.rem(lat + 1, lat_count)
    lat_down = lax.rem(lat + lat_count - 1, lat_count)
    lon_up = lax.rem(lon + 1, lon_count)
    lon_down = lax.rem(lon + lon_count - 1, lon_count)
    own = (0, 7)
    others = (3, 4, 2, 5, 1, 6)

    def owner(piece, sign):
        row_half, col_half, window = piece & 1, (piece >> 1) & 1, piece >> 2
        up, right = sign * (row_half - window), sign * (col_half - window)
        where_lat = {0: lat, 1: lat_up, -1: lat_down}[up]
        where_lon = {0: lon, 1: lon_up, -1: lon_down}[right]
        return (where_lat, where_lon)

    barrier = pltpu.get_barrier_semaphore()

    @pl.when(first)
    def _():
        for piece in others:
            pl.semaphore_signal(barrier, inc=1, device_id=(0,) + owner(piece, 1), device_id_type=MESH)
        for piece in others + own[:1]:
            pl.semaphore_signal(barrier, inc=1, device_id=(1,) + owner(piece, 1), device_id_type=MESH)

    loads = []

    def load(src, dst):
        copy = pltpu.make_async_copy(src, dst, load_sem.at[len(loads)])
        copy.start()
        loads.append(copy)
        return copy

    load_fields = [load(fields_hbm.at[m], fields_ref.at[m]) for m in range(MICRO)]
    prep = [load(table_hbm.at[0], table_ref), load(class_hbm, class_ref)]
    rest = [
        load(gains_hbm.at[0], gains_ref),
        load(joint_hbm.at[0], joint_ref),
        load(oproj_hbm.at[0], oproj_ref),
        load(expand_hbm.at[0], expand_ref),
        load(reduce_hbm.at[0], reduce_ref),
    ]

    def halo_copy(m, q):
        return pltpu.make_async_remote_copy(
            src_ref=halo_ref.at[m, q],
            dst_ref=take_ref.at[m, q],
            send_sem=halo_send.at[m, q],
            recv_sem=take_recv.at[m, q],
            device_id=(0,) + owner(q, -1),
            device_id_type=MESH,
        )

    def home_copy(m, q):
        return pltpu.make_async_remote_copy(
            src_ref=done_ref.at[m, q],
            dst_ref=home_ref.at[m, q],
            send_sem=home_send.at[m, q],
            recv_sem=home_recv.at[m, q],
            device_id=(0,) + owner(q, 1),
            device_id_type=MESH,
        )

    odd = lax.rem(lat, 2)
    lat_chip = lat + 1 - 2 * odd
    lat_cross = lax.rem(lat + lat_count - 1 + 2 * odd, lat_count)
    lon_cross = (lax.rem(lon + lon_count - 1 + odd, lon_count), lax.rem(lon + odd, lon_count))
    lon_chip = (lax.rem(lon + lon_count - odd, lon_count), lax.rem(lon + 1 - odd, lon_count))

    def chip_copy(m, col_half):
        piece = 1 + 3 * odd + 2 * col_half
        return pltpu.make_async_remote_copy(
            src_ref=done_ref.at[m, piece],
            dst_ref=home_ref.at[m, piece],
            send_sem=home_send.at[m, piece],
            recv_sem=home_recv.at[m, piece],
            device_id=(0, lat_chip, lon_chip[col_half]),
            device_id_type=MESH,
        )

    def cross_copy(m, col_half):
        piece = 4 - 3 * odd + 2 * col_half
        return pltpu.make_async_remote_copy(
            src_ref=done_ref.at[m, piece],
            dst_ref=home_ref.at[m, piece],
            send_sem=home_send.at[m, piece],
            recv_sem=home_recv.at[m, piece],
            device_id=(0, lat_cross, lon_cross[col_half]),
            device_id_type=MESH,
        )

    def hand_copy(m, col_half):
        piece = 1 + 3 * odd + 2 * col_half
        return pltpu.make_async_remote_copy(
            src_ref=take_ref.at[m, piece],
            dst_ref=home_ref.at[m, piece],
            send_sem=hand_send.at[m, col_half],
            recv_sem=home_recv.at[m, piece],
            device_id=(0, lat, lon),
            device_id_type=MESH,
        )

    def next_copy(m, q):
        return pltpu.make_async_remote_copy(
            src_ref=done_ref.at[m, q],
            dst_ref=take_ref.at[m, q],
            send_sem=next_send.at[m, q],
            recv_sem=take_recv.at[m, q],
            device_id=(1,) + owner(q, 1),
            device_id_type=MESH,
        )

    def send_halo(m):
        load_fields[m].wait()
        rows = dot(gather_ref[...], fields_ref[m].reshape(GRID_ROWS, WIDTH))
        refs = [[take_ref] if q in own else [halo_ref] for q in range(PIECES)]
        for window in range(2):
            pack(rows[window * PACKED : (window + 1) * PACKED], refs, m, window)
        if m == 0:
            pl.semaphore_wait(barrier, 6)
        for q in others:
            halo_copy(m, q).start()

    @pl.when(first)
    def _():
        gather_ref[...] = gather_matrix()
        send_halo(0)

    @pl.when(first)
    def _():
        into_ref[0:TOK, 0:PACKED] = shifted_matrix()
        scatter_ref[...] = scatter_matrix()
        last_ref[...] = back_matrix()

    @pl.when(jnp.logical_not(first))
    def _():
        for copy in load_fields:
            copy.wait()
        into_ref[...] = owned_matrix()
        last_ref[:, 0 : 2 * TOK] = plain_matrix()
        pl.semaphore_wait(barrier, 7)
        for piece in others + own[:1]:
            pl.semaphore_signal(ready_sem, inc=1, device_id=(0,) + owner(piece, 1), device_id_type=MESH)

    for copy in prep:
        copy.wait()
    prepare_bias(first, lat, lon, lat_count, lon_count, class_ref, table_ref, rows_ref, turned_ref, bias_ref)

    @pl.when(first)
    def _():
        send_halo(1)

    for copy in rest:
        copy.wait()

    def send_rest(m):
        for q in (1, 6, 0, 7):
            next_copy(m, q).start()
        for q in (2, 5):
            home_copy(m, q).start()
        for col_half in range(2):
            chip_copy(m, col_half).start()

    def step(m, carry):
        @pl.when(first)
        def _():
            for q in others:
                halo_copy(m, q).wait_recv()
            for window in range(2):
                rows = dot(into_ref[0:TOK, 0:PACKED], unpack(take_ref, m, window))
                x_ref[window * TOK : (window + 1) * TOK, :] = rows.astype(jnp.bfloat16)

            @pl.when(m > 0)
            def _():
                send_rest(m - 1)

        @pl.when(jnp.logical_not(first))
        def _():
            for q in range(PIECES):
                next_copy(m, q).wait_recv()

            @pl.when(m < MICRO - 1)
            def _():
                for col_half in range(2):
                    hand_copy(m, col_half).start()

            x_ref[...] = dot(into_ref[...], unpack_both(take_ref, m)).astype(jnp.bfloat16)

        x = x_ref[...].astype(jnp.float32)
        projected = project(x, gains_ref, joint_ref)
        y_ref[...] = finish(x, projected, gains_ref, oproj_ref, expand_ref, reduce_ref, bias_ref)
        refs = [[done_ref, home_ref] if q in own else [done_ref] for q in range(PIECES)]

        @pl.when(first)
        def _():
            for window in range(2):
                rows = slice(window * TOK, (window + 1) * TOK)
                pack(dot(scatter_ref[...], y_ref[rows, :]), refs, m, window)

            @pl.when(m == 0)
            def _():
                pl.semaphore_wait(ready_sem, 7)

            for q in (3, 4, 2, 5):
                next_copy(m, q).start()

            @pl.when(m == MICRO - 1)
            def _():
                send_rest(m)
                for col_half in range(2):
                    cross_copy(m, col_half).start()

        @pl.when(jnp.logical_not(first))
        def _():
            write(m, dot(last_ref[:, 0 : 2 * TOK], y_ref[...]).astype(jnp.bfloat16))

        return carry

    def write(m, rows):
        result_ref[m] = rows.reshape(WIN_H, WIN_W, LEVELS, WIDTH)

    lax.fori_loop(0, MICRO, step, 0)

    @pl.when(first)
    def _():
        for m in range(MICRO):
            for q in others:
                home_copy(m, q).wait_recv()
            write(m, dot(last_ref[...], unpack_both(home_ref, m)).astype(jnp.bfloat16))
        for m in range(MICRO):
            for q in others:
                halo_copy(m, q).wait_send()
            for q in (2, 5):
                home_copy(m, q).wait_send()
            for col_half in range(2):
                chip_copy(m, col_half).wait_send()
                if m == MICRO - 1:
                    cross_copy(m, col_half).wait_send()
            for q in range(PIECES):
                next_copy(m, q).wait_send()

    @pl.when(jnp.logical_not(first))
    def _():
        for m in range(MICRO - 1):
            for col_half in range(2):
                hand_copy(m, col_half).wait_send()


def body(
    fields, surface_class, norm_gains, joint_proj, out_proj, expand_proj, reduce_proj, earth_bias
):
    lat_count = lax.axis_size("lat")
    lon_count = lax.axis_size("lon")
    fields = jnp.transpose(fields, (0, 2, 3, 1, 4))
    operands = (
        fields, surface_class, norm_gains, joint_proj, out_proj, expand_proj, reduce_proj,
        jnp.transpose(earth_bias, (0, 2, 1, 3)),
    )
    bf16 = jnp.bfloat16
    scratch = [
        pltpu.VMEM(fields.shape, bf16),
        pltpu.VMEM(surface_class.shape, jnp.int32),
        pltpu.VMEM((2, WIDTH), bf16),
        pltpu.VMEM((WIDTH, 3 * WIDTH), bf16),
        pltpu.VMEM((WIDTH, WIDTH), bf16),
        pltpu.VMEM((WIDTH, FF), bf16),
        pltpu.VMEM((FF, WIDTH), bf16),
        pltpu.VMEM((HEADS,) + earth_bias.shape[1:2] + earth_bias.shape[3:], bf16),
        pltpu.VMEM((2 * PACKED, GRID_ROWS), bf16),
        pltpu.VMEM((2 * TOK, 2 * PACKED), bf16),
        pltpu.VMEM((PACKED, TOK), bf16),
        pltpu.VMEM((GRID_ROWS, 2 * PACKED), bf16),
        pltpu.VMEM((2 * TOK, WIDTH), bf16),
        pltpu.VMEM((2 * TOK, WIDTH), bf16),
        pltpu.VMEM((2, 12, 16, KDIM), bf16),
        pltpu.VMEM((2 * HEADS, TOK, 256), jnp.float32),
        pltpu.VMEM((2, TOK, 3 * GROUP), jnp.float32),
        pltpu.VMEM((MICRO, PIECES, PROWS, 128), bf16),
        pltpu.VMEM((MICRO, PIECES, PROWS, 128), bf16),
        pltpu.VMEM((MICRO, PIECES, PROWS, 128), bf16),
        pltpu.VMEM((MICRO, PIECES, PROWS, 128), bf16),
        pltpu.SemaphoreType.DMA((14,)),
        pltpu.SemaphoreType.DMA((MICRO, PIECES)),
        pltpu.SemaphoreType.DMA((MICRO, PIECES)),
        pltpu.SemaphoreType.DMA((MICRO, PIECES)),
        pltpu.SemaphoreType.DMA((MICRO, PIECES)),
        pltpu.SemaphoreType.DMA((MICRO, PIECES)),
        pltpu.SemaphoreType.DMA((MICRO, 2)),
        pltpu.SemaphoreType.REGULAR,
    ]
    result = pl.pallas_call(
        functools.partial(kernel, lat_count, lon_count),
        out_shape=pltpu.VMEM(fields.shape, bf16),
        in_specs=[pl.BlockSpec(memory_space=pltpu.HBM)] * len(operands),
        out_specs=pl.BlockSpec(memory_space=pltpu.VMEM),
        scratch_shapes=scratch,
        compiler_params=pltpu.CompilerParams(
            collective_id=0, has_side_effects=True, vmem_limit_bytes=56 * 1024 * 1024
        ),
        name="two_blocks",
    )(*operands)
    return jnp.transpose(result, (0, 3, 1, 2, 4))[None]


def solution(mesh):
    return jax.shard_map(
        body,
        mesh=mesh,
        in_specs=(
            P(None, None, "lat", "lon", None),
            P(),
            P("section", None, None),
            P("section", None, None),
            P("section", None, None),
            P("section", None, None),
            P("section", None, None),
            P("section", None, None, None),
        ),
        out_specs=P("section", None, None, "lat", "lon", None),
        check_vma=False,
    )
```

```python
import functools

import jax
import jax.numpy as jnp
from jax import lax
from jax.experimental import pallas as pl
from jax.experimental.pallas import tpu as pltpu
from jax.sharding import PartitionSpec as P

WIN_P = 2
WIN_H = 6
WIN_W = 12
TOK = WIN_P * WIN_H * WIN_W
LEVELS = 4
MICRO = 2
WIDTH = 384
HEADS = 12
FF = 1536
PIECES = 8
PROWS = 112
PACKED = 192
GRID_ROWS = LEVELS * WIN_H * WIN_W
GROUP = 640
GUSED = 576
KDIM = 288
LOG2E = 1.4426950408889634
MESH = pl.DeviceIdType.MESH


def divide(value, by):
    return (value * (-(-65536 // by))) >> 16


def token_parts(token):
    col = divide(token, 12)
    rest = token - col * 12
    level = (rest >= 6).astype(jnp.int32)
    return col, level, rest - level * 6


def packed_row(window, row_half, col_half, level, row, col):
    quarter = row_half + 2 * col_half
    inner = level * 18 + row * 6 + col
    return window * PACKED + jnp.where(inner < 32, quarter * 32 + inner, 96 + quarter * 16 + inner)


def halves(position, extent):
    half = (position >= extent).astype(jnp.int32)
    return half, position - half * extent


def one_hot(rows, target):
    at = lax.broadcasted_iota(jnp.int32, (rows, target.shape[1]), 0)
    return (at == target).astype(jnp.float32).astype(jnp.bfloat16)


def grid_place(row, col, level):
    return (row * 12 + col) * 4 + level


def pack_matrix(rows, target):
    row = lax.broadcasted_iota(jnp.int32, (rows, 1), 0)
    last = jnp.where((row & 12) == 12, -1, row - (row & 12))
    row = jnp.where(halves(row, PACKED)[1] < 128, row, last)
    return (row == target).astype(jnp.float32).astype(jnp.bfloat16)


def gather_matrix():
    place = lax.broadcasted_iota(jnp.int32, (1, GRID_ROWS), 1)
    pair = place >> 2
    row = divide(pair, 12)
    row_half, row_in = halves(row, 3)
    col_half, col_in = halves(pair - row * 12, 6)
    level = ((place & 3) + 3) & 3
    target = packed_row(level >> 1, 1 - row_half, 1 - col_half, level & 1, row_in, col_in)
    return pack_matrix(2 * PACKED, target)


def scatter_matrix():
    col, level, row = token_parts(lax.broadcasted_iota(jnp.int32, (1, TOK), 1))
    row_half, row_in = halves(row, 3)
    col_half, col_in = halves(col, 6)
    return pack_matrix(PACKED, packed_row(0, row_half, col_half, level, row_in, col_in))


def packed_parts(rows):
    place = lax.broadcasted_iota(jnp.int32, (1, rows), 1)
    window, place = halves(place, PACKED)
    early = place < 128
    quarter = jnp.where(early, place >> 5, (place - 128) >> 4)
    inner = jnp.where(early, place & 31, 32 + (place & 3))
    used = early | ((place & 12) != 12)
    level, rest = halves(inner, 18)
    row = divide(rest, 6)
    return used, quarter & 1, quarter >> 1, 2 * window + level, row, rest - row * 6


def shifted_matrix():
    used, row_half, col_half, level, row, col = packed_parts(PACKED)
    token = (col + 6 * col_half) * 12 + level * 6 + row + 3 * row_half
    return one_hot(TOK, jnp.where(used, token, -1))


def owned_parts():
    used, row_half, col_half, level, row, col = packed_parts(2 * PACKED)
    return used, (level + 1) & 3, row + 3 * (1 - row_half), col + 6 * (1 - col_half)


def owned_matrix():
    used, level, row, col = owned_parts()
    token = (level >> 1) * TOK + col * 12 + (level & 1) * 6 + row
    return one_hot(2 * TOK, jnp.where(used, token, -1))


def back_matrix():
    used, level, row, col = owned_parts()
    return one_hot(GRID_ROWS, jnp.where(used, grid_place(row, col, level), -1))


def plain_matrix():
    token = lax.broadcasted_iota(jnp.int32, (1, 2 * TOK), 1)
    window, rest = halves(token, TOK)
    col, level, row = token_parts(rest)
    return one_hot(GRID_ROWS, grid_place(row, col, 2 * window + level))


def pack(rows, refs, m, window):
    rows = rows.astype(jnp.bfloat16)
    chunk = (lax.broadcasted_iota(jnp.int32, (64, 1), 0) >> 2) & 3
    last = rows[128:].astype(jnp.float32)
    last = jnp.where(chunk == 0, last[:, 0:128], jnp.where(chunk == 1, last[:, 128:256], last[:, 256:384]))
    last = last.astype(jnp.bfloat16)
    for quarter in range(4):
        piece = window * 4 + quarter
        for ref in refs[piece]:
            for c in range(3):
                ref[m, piece, c * 32 : c * 32 + 32, :] = rows[quarter * 32 : quarter * 32 + 32, c * 128 : c * 128 + 128]
            ref[m, piece, 96:112, :] = last[quarter * 16 : quarter * 16 + 16]


def unpack(ref, m, window):
    chunk = (lax.broadcasted_iota(jnp.int32, (64, 1), 0) >> 2) & 3
    pieces = range(window * 4, window * 4 + 4)
    rows = [
        jnp.concatenate([ref[m, piece, c * 32 : c * 32 + 32, :] for c in range(3)], axis=1)
        for piece in pieces
    ]
    last = jnp.concatenate([ref[m, piece, 96:112, :] for piece in pieces], axis=0).astype(jnp.float32)
    last = jnp.concatenate([jnp.where(chunk == c, last, 0.0) for c in range(3)], axis=1)
    return jnp.concatenate(rows + [last.astype(jnp.bfloat16)], axis=0)


def unpack_both(ref, m):
    return jnp.concatenate([unpack(ref, m, window) for window in range(2)], axis=0)


def dot(a, b):
    return jnp.dot(a, b, preferred_element_type=jnp.float32)


def dot_nt(a, b):
    return lax.dot_general(a, b, (((1,), (1,)), ((), ())), preferred_element_type=jnp.float32)


def layer_norm(values, gain):
    average = jnp.mean(values, axis=-1, keepdims=True)
    centred = values - average
    spread = jnp.mean(centred * centred, axis=-1, keepdims=True)
    return centred * lax.rsqrt(spread + 1e-05) * gain


def gelu(x):
    return x * (0.5 + 0.5 * lax.erf(x * 0.7071067811865476))


def lane_tokens():
    lane = lax.broadcasted_iota(jnp.int32, (1, 256), 1)
    return jnp.where(lane < 128, lane, 128 + (lane & 15))


def prepare_bias(first, lat, lon, lat_count, lon_count, class_ref, table_ref, rows_ref, turned_ref, bias_ref):
    kinds = 2 * lat_count
    one = jnp.where(first, 1, 0)
    lats = (lat, lax.rem(lat + lat_count - one, lat_count))
    lons = (lon, lax.rem(lon + lon_count - one, lon_count))
    to_row = lax.broadcasted_iota(jnp.int32, (32, HEADS * kinds), 0)
    to_col = lax.broadcasted_iota(jnp.int32, (32, HEADS * kinds), 1)
    kind = jnp.where(to_row < 16, lat, lat_count + lats[1])
    wanted = (to_row & 15) * kinds + kind
    own = (to_col == wanted).astype(jnp.float32).astype(jnp.bfloat16)
    table = dot(own, table_ref[...].reshape(HEADS * kinds, -1)).astype(jnp.bfloat16)
    rows_ref[...] = jnp.zeros_like(rows_ref)
    for i in range(2):
        for j in range(12):
            pb, rb = j // 6, j % 6
            for pa in range(2):
                begin = pb * 1656 + pa * 828 + rb * 138
                rows_ref[i, j, :, pa * 144 : pa * 144 + 138] = table[
                    i * 16 : i * 16 + 16, begin : begin + 138
                ]
    to_row = lax.broadcasted_iota(jnp.int32, (192, 192), 0)
    to_col = lax.broadcasted_iota(jnp.int32, (192, 192), 1)
    swap = (((to_row & 15) << 4) + (to_row >> 4) == to_col).astype(jnp.float32).astype(jnp.bfloat16)
    by_head = [
        dot(swap, rows_ref[i].reshape(192, KDIM)).astype(jnp.bfloat16) for i in range(2)
    ]
    by_head = jnp.concatenate(by_head, axis=0)
    col_a, level_a, row_a = token_parts(lane_tokens())
    base = level_a * 144 + row_a * 23 + col_a + 11
    depth = lax.broadcasted_iota(jnp.int32, (KDIM, 256), 0)
    for cb in range(12):
        pick = (depth == base - cb).astype(jnp.float32).astype(jnp.bfloat16)
        spread = dot(by_head, pick)
        for i in range(2):
            for h in range(HEADS):
                start = i * 192 + h * 16
                turned_ref[i * HEADS + h, cb * 12 : cb * 12 + 12, :] = spread[start : start + 12]
    rows_all = 6 * lat_count
    cols_all = 12 * lon_count
    classes = class_ref[...].reshape(LEVELS * rows_all, cols_all).astype(jnp.float32).astype(jnp.bfloat16)
    col_b, level_b, row_b = token_parts(lax.broadcasted_iota(jnp.int32, (TOK, 1), 0))

    def wrap(v, extent):
        return jnp.where(v >= extent, v - extent, v)

    def onehot(a, b):
        return (a == b).astype(jnp.float32).astype(jnp.bfloat16)

    identity = (
        lax.broadcasted_iota(jnp.int32, (TOK, 256), 0) == lax.broadcasted_iota(jnp.int32, (TOK, 256), 1)
    )
    identity = identity.astype(jnp.float32).astype(jnp.bfloat16)
    place_a = lax.broadcasted_iota(jnp.int32, (LEVELS * rows_all, 256), 0)
    place_b = lax.broadcasted_iota(jnp.int32, (TOK, LEVELS * rows_all), 1)
    for i in range(2):
        row_start = lats[i] * 6 + 3 * one
        col_start = lons[i] * 12 + 6 * one
        across = dot(
            classes,
            onehot(lax.broadcasted_iota(jnp.int32, (cols_all, 256), 0), wrap(col_start + col_a, cols_all)),
        )
        down = dot_nt(
            onehot(lax.broadcasted_iota(jnp.int32, (TOK, cols_all), 1), wrap(col_start + col_b, cols_all)),
            classes,
        )

        def region(place, level, row, values, axis):
            at = ((2 * i + level + one) & 3) * rows_all + wrap(row_start + row, rows_all)
            value = jnp.sum(jnp.where(place == at, values, 0.0), axis=axis, keepdims=True)
            flags = 2 * (2 * i + level >= 3).astype(jnp.int32)
            flags = flags + (lats[i] * 6 + row >= rows_all - 3).astype(jnp.int32)
            return 4.0 * value + (one * flags).astype(jnp.float32)

        region_a = region(place_a, level_a, row_a, across, 0)
        region_b = region(place_b, level_b, row_b, down, 1)
        same = region_b == region_a
        for g in range(3):
            heads = [turned_ref[i * HEADS + g * 4 + t] for t in range(4)]
            stack = jnp.concatenate([h[0:128] for h in heads] + [h[128:144] for h in heads], axis=0)
            spread = dot_nt(identity, stack.astype(jnp.bfloat16)) * LOG2E
            for t in range(5):
                lanes = slice(t * 128, min(t * 128 + 128, GUSED))
                part = same[:, 0:128] if t < 4 else same[:, 128:192]
                to = slice(g * GROUP + lanes.start, g * GROUP + lanes.stop)
                bias_ref[i, :, to] = jnp.where(part, spread[:, lanes], -1e30)
            bias_ref[i, :, g * GROUP + GUSED : (g + 1) * GROUP] = jnp.full((TOK, GROUP - GUSED), -1e30, jnp.float32)


def attention(query, key, value, bias_ref, i):
    head = lax.broadcasted_iota(jnp.int32, (1, 128), 1) >> 5
    keep = [(head == t).astype(jnp.float32).astype(jnp.bfloat16) for t in range(4)]
    segment = lax.broadcasted_iota(jnp.int32, (1, 128), 1) >> 4
    blank = jnp.zeros((64, 128), jnp.bfloat16)
    blank_wide = jnp.zeros((64, 256), jnp.bfloat16)
    mixed = []
    for g in range(3):
        lanes = slice(g * 128, g * 128 + 128)
        q, k, v = query[:, lanes], key[:, lanes], value[:, lanes]
        wide = jnp.concatenate([k[0:128] * m for m in keep] + [k[128:144] * m for m in keep] + [blank], axis=0)
        scores = dot_nt(q, wide) + bias_ref[i, :, g * GROUP : (g + 1) * GROUP]
        tail = scores[:, 512:640]
        top, weights = [], []
        for t in range(4):
            main = scores[:, t * 128 : t * 128 + 128]
            joined = jnp.maximum(main, jnp.where(segment == t, tail, -1e30))
            top.append(jnp.max(joined, axis=1, keepdims=True))
            weights.append(jnp.exp2(main - top[t]).astype(jnp.bfloat16))
        tops = jnp.where(segment < 2, jnp.where(segment == 0, top[0], top[1]), jnp.where(segment == 2, top[2], top[3]))
        weights.append(jnp.exp2(tail - tops).astype(jnp.bfloat16))
        weights = jnp.concatenate(weights, axis=1)
        pairs = [jnp.concatenate([v[0:128] * m, jnp.broadcast_to(m, (128, 128))], axis=1) for m in keep]
        pairs += [jnp.concatenate([v[128:144] * m, jnp.broadcast_to(m, (16, 128))], axis=1) for m in keep]
        out = dot(weights, jnp.concatenate(pairs + [blank_wide], axis=0))
        mixed.append((out[:, 0:128] / out[:, 128:256]).astype(jnp.bfloat16))
    return jnp.concatenate(mixed, axis=1)


def project(x, gains_ref, joint_ref):
    normed = layer_norm(x, gains_ref[0:1].astype(jnp.float32)).astype(jnp.bfloat16)
    projected = dot(normed, joint_ref[...])
    query = projected[:, 0:WIDTH] * (LOG2E * 32**-0.5)
    return jnp.concatenate([query, projected[:, WIDTH:]], axis=1).astype(jnp.bfloat16)


def finish(x, projected, gains_ref, out_ref, expand_ref, reduce_ref, bias_ref):
    query, key, value = (projected[:, n * WIDTH : (n + 1) * WIDTH] for n in range(3))
    mixed = []
    for i in range(2):
        rows = slice(i * TOK, (i + 1) * TOK)
        mixed.append(attention(query[rows], key[rows], value[rows], bias_ref, i))
    hidden = x + dot(jnp.concatenate(mixed, axis=0), out_ref[...])
    again = layer_norm(hidden, gains_ref[1:2].astype(jnp.float32)).astype(jnp.bfloat16)
    act = gelu(dot(again, expand_ref[...])).astype(jnp.bfloat16)
    return (hidden + dot(act, reduce_ref[...])).astype(jnp.bfloat16)


def kernel(
    lat_count,
    lon_count,
    fields_hbm,
    class_hbm,
    gains_hbm,
    joint_hbm,
    oproj_hbm,
    expand_hbm,
    reduce_hbm,
    table_hbm,
    result_ref,
    fields_ref,
    class_ref,
    gains_ref,
    joint_ref,
    oproj_ref,
    expand_ref,
    reduce_ref,
    table_ref,
    gather_ref,
    into_ref,
    scatter_ref,
    last_ref,
    x_ref,
    y_ref,
    rows_ref,
    turned_ref,
    bias_ref,
    halo_ref,
    take_ref,
    done_ref,
    home_ref,
    load_sem,
    halo_send,
    take_recv,
    home_send,
    home_recv,
    next_send,
    hand_send,
):
    sec = lax.axis_index("section")
    lat = lax.axis_index("lat")
    lon = lax.axis_index("lon")
    first = sec == 0
    lat_up = lax.rem(lat + 1, lat_count)
    lat_down = lax.rem(lat + lat_count - 1, lat_count)
    lon_up = lax.rem(lon + 1, lon_count)
    lon_down = lax.rem(lon + lon_count - 1, lon_count)
    own = (0, 7)
    others = (3, 4, 2, 5, 1, 6)

    def owner(piece, sign):
        row_half, col_half, window = piece & 1, (piece >> 1) & 1, piece >> 2
        up, right = sign * (row_half - window), sign * (col_half - window)
        where_lat = {0: lat, 1: lat_up, -1: lat_down}[up]
        where_lon = {0: lon, 1: lon_up, -1: lon_down}[right]
        return (where_lat, where_lon)

    barrier = pltpu.get_barrier_semaphore()

    @pl.when(first)
    def _():
        for piece in others:
            pl.semaphore_signal(barrier, inc=1, device_id=(0,) + owner(piece, 1), device_id_type=MESH)
        pl.semaphore_signal(barrier, inc=1, device_id=(1, lat, lon), device_id_type=MESH)

    @pl.when(jnp.logical_not(first))
    def _():
        for piece in others + own[:1]:
            pl.semaphore_signal(barrier, inc=1, device_id=(0,) + owner(piece, 1), device_id_type=MESH)

    loads = []

    def load(src, dst):
        copy = pltpu.make_async_copy(src, dst, load_sem.at[len(loads)])
        copy.start()
        loads.append(copy)
        return copy

    load_fields = [load(fields_hbm.at[m], fields_ref.at[m]) for m in range(MICRO)]
    prep = [load(table_hbm.at[0], table_ref), load(class_hbm, class_ref)]
    rest = [
        load(gains_hbm.at[0], gains_ref),
        load(joint_hbm.at[0], joint_ref),
        load(oproj_hbm.at[0], oproj_ref),
        load(expand_hbm.at[0], expand_ref),
        load(reduce_hbm.at[0], reduce_ref),
    ]

    def halo_copy(m, q):
        return pltpu.make_async_remote_copy(
            src_ref=halo_ref.at[m, q],
            dst_ref=take_ref.at[m, q],
            send_sem=halo_send.at[m, q],
            recv_sem=take_recv.at[m, q],
            device_id=(0,) + owner(q, -1),
            device_id_type=MESH,
        )

    def home_copy(m, q):
        return pltpu.make_async_remote_copy(
            src_ref=done_ref.at[m, q],
            dst_ref=home_ref.at[m, q],
            send_sem=home_send.at[m, q],
            recv_sem=home_recv.at[m, q],
            device_id=(0,) + owner(q, 1),
            device_id_type=MESH,
        )

    odd = lax.rem(lat, 2)
    lat_chip = lat + 1 - 2 * odd
    lat_cross = lax.rem(lat + lat_count - 1 + 2 * odd, lat_count)
    lon_cross = (lax.rem(lon + lon_count - 1 + odd, lon_count), lax.rem(lon + odd, lon_count))
    lon_chip = (lax.rem(lon + lon_count - odd, lon_count), lax.rem(lon + 1 - odd, lon_count))

    def chip_copy(m, col_half):
        piece = 1 + 3 * odd + 2 * col_half
        return pltpu.make_async_remote_copy(
            src_ref=done_ref.at[m, piece],
            dst_ref=home_ref.at[m, piece],
            send_sem=home_send.at[m, piece],
            recv_sem=home_recv.at[m, piece],
            device_id=(0, lat_chip, lon_chip[col_half]),
            device_id_type=MESH,
        )

    def cross_copy(m, col_half):
        piece = 4 - 3 * odd + 2 * col_half
        return pltpu.make_async_remote_copy(
            src_ref=done_ref.at[m, piece],
            dst_ref=home_ref.at[m, piece],
            send_sem=home_send.at[m, piece],
            recv_sem=home_recv.at[m, piece],
            device_id=(0, lat_cross, lon_cross[col_half]),
            device_id_type=MESH,
        )

    def hand_copy(m, col_half):
        piece = 1 + 3 * odd + 2 * col_half
        return pltpu.make_async_remote_copy(
            src_ref=take_ref.at[m, piece],
            dst_ref=home_ref.at[m, piece],
            send_sem=hand_send.at[m, col_half],
            recv_sem=home_recv.at[m, piece],
            device_id=(0, lat, lon),
            device_id_type=MESH,
        )

    def next_copy(m, q):
        return pltpu.make_async_remote_copy(
            src_ref=done_ref.at[m, q],
            dst_ref=take_ref.at[m, q],
            send_sem=next_send.at[m, q],
            recv_sem=take_recv.at[m, q],
            device_id=(1,) + owner(q, 1),
            device_id_type=MESH,
        )

    def send_halo(m):
        load_fields[m].wait()
        rows = dot(gather_ref[...], fields_ref[m].reshape(GRID_ROWS, WIDTH))
        refs = [[take_ref] if q in own else [halo_ref] for q in range(PIECES)]
        for window in range(2):
            pack(rows[window * PACKED : (window + 1) * PACKED], refs, m, window)
        if m == 0:
            pl.semaphore_wait(barrier, 13)
        for q in others:
            halo_copy(m, q).start()

    @pl.when(first)
    def _():
        gather_ref[...] = gather_matrix()
        send_halo(0)

    @pl.when(first)
    def _():
        into_ref[0:TOK, 0:PACKED] = shifted_matrix()
        scatter_ref[...] = scatter_matrix()
        last_ref[...] = back_matrix()

    @pl.when(jnp.logical_not(first))
    def _():
        for copy in load_fields:
            copy.wait()
        into_ref[...] = owned_matrix()
        last_ref[:, 0 : 2 * TOK] = plain_matrix()
        pl.semaphore_wait(barrier, 1)

    for copy in prep:
        copy.wait()
    prepare_bias(first, lat, lon, lat_count, lon_count, class_ref, table_ref, rows_ref, turned_ref, bias_ref)

    @pl.when(first)
    def _():
        send_halo(1)

    for copy in rest:
        copy.wait()

    def step(m, carry):
        @pl.when(first)
        def _():
            for q in others:
                halo_copy(m, q).wait_recv()
            for window in range(2):
                rows = dot(into_ref[0:TOK, 0:PACKED], unpack(take_ref, m, window))
                x_ref[window * TOK : (window + 1) * TOK, :] = rows.astype(jnp.bfloat16)

        @pl.when(jnp.logical_not(first))
        def _():
            for q in range(PIECES):
                next_copy(m, q).wait_recv()

            @pl.when(m < MICRO - 1)
            def _():
                for col_half in range(2):
                    hand_copy(m, col_half).start()

            x_ref[...] = dot(into_ref[...], unpack_both(take_ref, m)).astype(jnp.bfloat16)

        x = x_ref[...].astype(jnp.float32)
        projected = project(x, gains_ref, joint_ref)
        y_ref[...] = finish(x, projected, gains_ref, oproj_ref, expand_ref, reduce_ref, bias_ref)
        refs = [[done_ref, home_ref] if q in own else [done_ref] for q in range(PIECES)]

        @pl.when(first)
        def _():
            for window in range(2):
                rows = slice(window * TOK, (window + 1) * TOK)
                pack(dot(scatter_ref[...], y_ref[rows, :]), refs, m, window)
                for q in (3, 1, 2, 0) if window == 0 else (4, 6, 5, 7):
                    next_copy(m, q).start()
            @pl.when(m == MICRO - 1)
            def _():
                for col_half in range(2):
                    cross_copy(m, col_half).start()

            for q in (2, 5):
                home_copy(m, q).start()
            for col_half in range(2):
                chip_copy(m, col_half).start()

        @pl.when(jnp.logical_not(first))
        def _():
            write(m, dot(last_ref[:, 0 : 2 * TOK], y_ref[...]).astype(jnp.bfloat16))

        return carry

    def write(m, rows):
        result_ref[m] = rows.reshape(WIN_H, WIN_W, LEVELS, WIDTH)

    lax.fori_loop(0, MICRO, step, 0)

    @pl.when(first)
    def _():
        for m in range(MICRO):
            for q in others:
                home_copy(m, q).wait_recv()
            write(m, dot(last_ref[...], unpack_both(home_ref, m)).astype(jnp.bfloat16))
        for m in range(MICRO):
            for q in others:
                halo_copy(m, q).wait_send()
            for q in (2, 5):
                home_copy(m, q).wait_send()
            for col_half in range(2):
                chip_copy(m, col_half).wait_send()
                if m == MICRO - 1:
                    cross_copy(m, col_half).wait_send()
            for q in range(PIECES):
                next_copy(m, q).wait_send()

    @pl.when(jnp.logical_not(first))
    def _():
        for m in range(MICRO - 1):
            for col_half in range(2):
                hand_copy(m, col_half).wait_send()


def write_out(result_ref, out_ref, sem):
    copies = [
        pltpu.make_async_copy(
            result_ref.at[m, pl.ds(3 * half, 3)], out_ref.at[m, pl.ds(3 * half, 3)], sem.at[m, half]
        )
        for m in range(MICRO)
        for half in range(2)
    ]
    for copy in copies:
        copy.start()
    for copy in copies:
        copy.wait()


def body(
    fields, surface_class, norm_gains, joint_proj, out_proj, expand_proj, reduce_proj, earth_bias
):
    lat_count = lax.axis_size("lat")
    lon_count = lax.axis_size("lon")
    fields = jnp.transpose(fields, (0, 2, 3, 1, 4))
    operands = (
        fields, surface_class, norm_gains, joint_proj, out_proj, expand_proj, reduce_proj,
        jnp.transpose(earth_bias, (0, 2, 1, 3)),
    )
    bf16 = jnp.bfloat16
    scratch = [
        pltpu.VMEM(fields.shape, bf16),
        pltpu.VMEM(surface_class.shape, jnp.int32),
        pltpu.VMEM((2, WIDTH), bf16),
        pltpu.VMEM((WIDTH, 3 * WIDTH), bf16),
        pltpu.VMEM((WIDTH, WIDTH), bf16),
        pltpu.VMEM((WIDTH, FF), bf16),
        pltpu.VMEM((FF, WIDTH), bf16),
        pltpu.VMEM((HEADS,) + earth_bias.shape[1:2] + earth_bias.shape[3:], bf16),
        pltpu.VMEM((2 * PACKED, GRID_ROWS), bf16),
        pltpu.VMEM((2 * TOK, 2 * PACKED), bf16),
        pltpu.VMEM((PACKED, TOK), bf16),
        pltpu.VMEM((GRID_ROWS, 2 * PACKED), bf16),
        pltpu.VMEM((2 * TOK, WIDTH), bf16),
        pltpu.VMEM((2 * TOK, WIDTH), bf16),
        pltpu.VMEM((2, 12, 16, KDIM), bf16),
        pltpu.VMEM((2 * HEADS, TOK, 256), jnp.float32),
        pltpu.VMEM((2, TOK, 3 * GROUP), jnp.float32),
        pltpu.VMEM((MICRO, PIECES, PROWS, 128), bf16),
        pltpu.VMEM((MICRO, PIECES, PROWS, 128), bf16),
        pltpu.VMEM((MICRO, PIECES, PROWS, 128), bf16),
        pltpu.VMEM((MICRO, PIECES, PROWS, 128), bf16),
        pltpu.SemaphoreType.DMA((14,)),
        pltpu.SemaphoreType.DMA((MICRO, PIECES)),
        pltpu.SemaphoreType.DMA((MICRO, PIECES)),
        pltpu.SemaphoreType.DMA((MICRO, PIECES)),
        pltpu.SemaphoreType.DMA((MICRO, PIECES)),
        pltpu.SemaphoreType.DMA((MICRO, PIECES)),
        pltpu.SemaphoreType.DMA((MICRO, 2)),
    ]
    result = pl.pallas_call(
        functools.partial(kernel, lat_count, lon_count),
        out_shape=pltpu.VMEM(fields.shape, bf16),
        in_specs=[pl.BlockSpec(memory_space=pltpu.HBM)] * len(operands),
        out_specs=pl.BlockSpec(memory_space=pltpu.VMEM),
        scratch_shapes=scratch,
        compiler_params=pltpu.CompilerParams(
            collective_id=0, has_side_effects=True, vmem_limit_bytes=56 * 1024 * 1024
        ),
        name="two_blocks",
    )(*operands)
    result = pl.pallas_call(
        write_out,
        out_shape=jax.ShapeDtypeStruct(result.shape, bf16),
        in_specs=[pl.BlockSpec(memory_space=pl.ANY)],
        out_specs=pl.BlockSpec(memory_space=pl.ANY),
        scratch_shapes=[pltpu.SemaphoreType.DMA((MICRO, 2))],
        compiler_params=pltpu.CompilerParams(vmem_limit_bytes=1024 * 1024),
        name="write_out",
    )(result)
    return jnp.transpose(result, (0, 3, 1, 2, 4))[None]


def solution(mesh):
    return jax.shard_map(
        body,
        mesh=mesh,
        in_specs=(
            P(None, None, "lat", "lon", None),
            P(),
            P("section", None, None),
            P("section", None, None),
            P("section", None, None),
            P("section", None, None),
            P("section", None, None),
            P("section", None, None, None),
        ),
        out_specs=P("section", None, None, "lat", "lon", None),
        check_vma=False,
    )
```
